32 devices in a mesh: section: 8 (over z, y), dp: 4 (over x, core).
Axes of the slice: x: 2, y: 2, z: 4, core: 2. Of those that a mesh axis runs over, the one named last changes fastest.
Arguments:
- tokens: bfloat16 [1024, 960], P('dp'), may hold values from -16 to 16
- cotangent: bfloat16 [1024, 960], P('dp'), may hold values from -6 to 6
- seq_counts: int32 [16, 2], P('dp'), may hold values from 0 to 4, as said below
- attn_gain: float32 [8, 960], P('section'), may hold values from 0.25 to 1.75
- w_qkv: bfloat16 [8, 960, 1600], P('section'), may hold values from -0.1875 to 0.1875
- w_out: bfloat16 [8, 960, 960], P('section'), may hold values from -0.75 to 0.75
- ffn_gain: float32 [8, 960], P('section'), may hold values from 0.25 to 1.75
- w_gate_up: bfloat16 [8, 960, 5120], P('section'), may hold values from -0.1875 to 0.1875
- w_down: bfloat16 [8, 2560, 960], P('section'), may hold values from -0.125 to 0.125
Outputs:
- section_outputs: bfloat16 [8, 1024, 960], P('section', 'dp')
- section_input_grads: bfloat16 [8, 1024, 960], P('section', 'dp')
- attn_gain_grad: float32 [8, 960], P('section', 'dp')
- w_qkv_grad: float32 [8, 960, 1600], P('section', 'dp')
- w_out_grad: float32 [8, 960, 960], P('section', None, 'dp')
- ffn_gain_grad: float32 [8, 960], P('section', 'dp')
- w_gate_up_grad: float32 [8, 960, 5120], P('section', 'dp')
- w_down_grad: float32 [8, 2560, 960], P('section', None, 'dp')
The draws below stay inside these ranges and needn't reach their ends.
Inputs may be any that keep to these rules, and one draw needn't show every extreme that they name: `seq_counts`: column 0 is the number of 64-token sequences (0 or 1) and column 1 the number of 16-token sequences of a micro-batch, laid from its first slot: a micro-batch holds one long sequence or two to four short ones. Every data group has a micro-batch with a long sequence and one with four short ones.
All inputs are finite; a program needn't handle non-finite values.
Results may differ from the reference program's by a relative error of at most 0.035.
Values may be sent and summed in bfloat16 or wider, within the bound.
A program may use at most 320 MiB of HBM per device.

```python
from functools import partial
import jax
import jax.numpy as jnp
from jax import lax

D = 960
HEADS = 15
KV_HEADS = 5
HEAD_DIM = 64
FF = 2560
SHORT_LEN = 16
LONG_LEN = 64
MICRO = 4
SECTIONS = 8
BATCHES = 16
TOKENS = 1024
Q_WIDTH = 960
QKV_WIDTH = 1600


def draw_seq_counts(key, part):
    key = jax.random.fold_in(key, 7)
    key_long, key_short, key_first, key_other = jax.random.split(key, 4)
    groups = BATCHES // MICRO
    longs = jax.random.randint(key_long, (groups, MICRO), 0, 2)
    shorts = jax.random.randint(key_short, (groups, MICRO), 2, 5)
    first = jax.random.randint(key_first, (groups, 1), 0, MICRO)
    other = (first + jax.random.randint(key_other, (groups, 1), 1, MICRO)) % MICRO
    slot_ids = jnp.arange(MICRO, dtype=jnp.int32)[None, :]
    longs = jnp.where(slot_ids == first, 1, jnp.where(slot_ids == other, 0, longs))
    shorts = jnp.where(longs == 1, 0, jnp.where(slot_ids == other, 4, shorts))
    return jnp.stack([longs, shorts], -1).reshape(BATCHES, 2).astype(jnp.int32)


def shard_levels(rng, extent, cuts, least, top_value):
    gain = 1.0
    for axis_at, parts in cuts:
        draws = jax.random.uniform(jax.random.fold_in(jax.random.fold_in(rng, 6), axis_at), (parts,), jnp.float32, least / len(cuts), top_value / len(cuts))
        gain = gain * jnp.repeat(jnp.exp(draws), extent[axis_at] // parts).reshape((-1,) + (1,) * (len(extent) - 1 - axis_at))
    return gain


def normal_values(own_key, shape, deviation, reach, pieces=(), kind=jnp.bfloat16):
    array = deviation * jax.random.normal(own_key, shape, jnp.float32)
    if pieces:
        array = array * shard_levels(own_key, shape, pieces, -0.22, 0.18)
    return jnp.clip(array, -reach, reach).astype(kind)


def setup_inputs(seed: int = 0) -> dict:
    arg_keys = jax.random.split(jax.random.key(seed), 10)
    tokens = normal_values(arg_keys[0], (TOKENS, D), 4.0, 16.0, ((0, 4),))
    cotangent = normal_values(arg_keys[1], (TOKENS, D), 1.0, 6.0, ((0, 4),))
    seq_counts = draw_seq_counts(jax.random.fold_in(arg_keys[9], 71), 0)
    attn_gain = jnp.clip(1.0 + 0.15 * jax.random.normal(arg_keys[3], (SECTIONS, D), jnp.float32), 0.25, 1.75)
    w_qkv = normal_values(arg_keys[4], (SECTIONS, D, QKV_WIDTH), D ** -0.5, 0.1875, ((0, 8),))
    w_out = normal_values(arg_keys[5], (SECTIONS, Q_WIDTH, D), (Q_WIDTH // 16) ** -0.5, 0.75, ((0, 8),))
    ffn_gain = jnp.clip(1.0 + 0.15 * jax.random.normal(arg_keys[6], (SECTIONS, D), jnp.float32), 0.25, 1.75)
    w_gate_up = normal_values(arg_keys[7], (SECTIONS, D, 2 * FF), D ** -0.5, 0.1875, ((0, 8),))
    w_down = normal_values(arg_keys[8], (SECTIONS, FF, D), FF ** -0.5, 0.125, ((0, 8),))
    return dict(tokens=tokens, cotangent=cotangent, seq_counts=seq_counts, attn_gain=attn_gain, w_qkv=w_qkv, w_out=w_out, ffn_gain=ffn_gain, w_gate_up=w_gate_up, w_down=w_down)


EPS = 1e-05
BASE = 10000.0
NEG = -1e+30
HIGHEST = lax.Precision.HIGHEST

@jax.custom_vjp
def low(v):
    return lax.optimization_barrier(v.astype(jnp.bfloat16)).astype(jnp.float32)

@jax.custom_vjp
def low_back(v):
    return v

def low_keep(v):
    return (low(v), None)

def low_pass(kept, grad):
    return (grad,)

def back_keep(v):
    return (v, None)

def back_low(kept, grad):
    return (low(grad),)
low.defvjp(low_keep, low_pass)
low_back.defvjp(back_keep, back_low)

def layout(counts, length, short_len):
    slot_ids = jnp.arange(length, dtype=jnp.int32)
    piece_ids = slot_ids // short_len
    is_long = counts[0] > 0
    valid_mask = jnp.where(is_long, True, piece_ids < counts[1])
    document = jnp.where(is_long, 0, piece_ids)
    document = jnp.where(valid_mask, document, length + slot_ids)
    position = jnp.where(is_long, slot_ids, slot_ids % short_len)
    return (document, position, valid_mask)

def rotary(position, head_dim):
    half_dim = head_dim // 2
    frequency = BASE ** (-2.0 * jnp.arange(half_dim, dtype=jnp.float32) / head_dim)
    angles = position.astype(jnp.float32)[:, None] * frequency[None, :]
    return (jnp.cos(angles), jnp.sin(angles))

def rotate(heads_in, cosine, sine_part):
    half_dim = heads_in.shape[-1] // 2
    first = heads_in[..., :half_dim]
    second = heads_in[..., half_dim:]
    cos_wide = cosine[:, None, :]
    sin_wide = sine_part[:, None, :]
    return jnp.concatenate([first * cos_wide - second * sin_wide, second * cos_wide + first * sin_wide], -1)

def block_apply(stream, document, position, gain_attn, w_qkv, w_out, gain_ffn, w_gate_up, w_down):
    num_rows = stream.shape[0]
    q_width = HEADS * HEAD_DIM
    kv_width = KV_HEADS * HEAD_DIM
    repeat = HEADS // KV_HEADS
    score_scale = HEAD_DIM ** (-0.5)
    slot_ids = jnp.arange(num_rows, dtype=jnp.int32)
    allowed = (document[:, None] == document[None, :]) & (slot_ids[:, None] >= slot_ids[None, :])
    cosine, sine_part = rotary(position, HEAD_DIM)
    inv_attn = lax.rsqrt(lax.optimization_barrier(jnp.mean(stream * stream, -1, keepdims=True)) + EPS)
    normed = low(stream * inv_attn * gain_attn)
    qkv_proj = low_back(jnp.dot(normed, w_qkv, precision=HIGHEST))
    queries = low(rotate(qkv_proj[:, :q_width].reshape(num_rows, HEADS, HEAD_DIM), cosine, sine_part))
    queries = queries.reshape(num_rows, KV_HEADS, repeat, HEAD_DIM)
    key_heads = low(rotate(qkv_proj[:, q_width:q_width + kv_width].reshape(num_rows, KV_HEADS, HEAD_DIM), cosine, sine_part))
    value_heads = low(qkv_proj[:, q_width + kv_width:].reshape(num_rows, KV_HEADS, HEAD_DIM))
    scores = low_back(jnp.einsum('qgrd,kgd->grqk', queries, key_heads, precision=HIGHEST) * score_scale)
    scores = jnp.where(allowed, scores, NEG)
    row_max = lax.optimization_barrier(jnp.max(scores, -1, keepdims=True))
    expanded = jnp.exp(scores - row_max)
    probabilities = low(expanded / lax.optimization_barrier(jnp.sum(expanded, -1, keepdims=True)))
    mixed_heads = jnp.einsum('grqk,kgd->qgrd', probabilities, value_heads, precision=HIGHEST)
    mixed_heads = low_back(low(mixed_heads.reshape(num_rows, q_width)))
    middle = stream + low_back(jnp.dot(mixed_heads, w_out, precision=HIGHEST))
    inv_ffn = lax.rsqrt(lax.optimization_barrier(jnp.mean(middle * middle, -1, keepdims=True)) + EPS)
    normed_ffn = low(middle * inv_ffn * gain_ffn)
    gate_up = low_back(jnp.dot(normed_ffn, w_gate_up, precision=HIGHEST))
    gate_part = gate_up[:, :FF]
    up_part = gate_up[:, FF:]
    hidden = low(gate_part * jax.nn.sigmoid(gate_part) * up_part)
    return middle + low_back(jnp.dot(hidden, w_down, precision=HIGHEST))

def reference(tokens, cotangent, seq_counts, attn_gain, w_qkv, w_out, ffn_gain, w_gate_up, w_down):
    batches = seq_counts.shape[0]
    document, position, valid_mask = jax.vmap(partial(layout, length=LONG_LEN, short_len=SHORT_LEN))(seq_counts)
    keep_rows = valid_mask.astype(jnp.float32)[:, :, None]
    apply_all = jax.checkpoint(jax.vmap(block_apply, in_axes=(0, 0, 0, None, None, None, None, None, None)))

    def forward(inputs, nudges, gains_attn, weights_qkv, weights_out, gains_ffn, weights_gate_up, weights_down):
        stream = inputs.reshape(batches, LONG_LEN, D) + nudges[0]
        results = []
        for section_num in range(SECTIONS):
            if section_num > 0:
                stream = low_back(results[-1]) + nudges[section_num]
            section_weights = (gains_attn[section_num], weights_qkv[section_num], weights_out[section_num], gains_ffn[section_num], weights_gate_up[section_num], weights_down[section_num])
            middle_run = apply_all(stream, document, position, *section_weights)
            final_run = apply_all(middle_run, document, position, *section_weights)
            results.append(low(final_run * keep_rows))
        return jnp.stack(results)
    primals = (tokens.astype(jnp.float32), jnp.zeros((SECTIONS, batches, LONG_LEN, D), jnp.float32), attn_gain.astype(jnp.float32), w_qkv.astype(jnp.float32), w_out.astype(jnp.float32), ffn_gain.astype(jnp.float32), w_gate_up.astype(jnp.float32), w_down.astype(jnp.float32))
    outputs, backward = jax.vjp(forward, *primals)
    start_grads = jnp.zeros_like(outputs).at[SECTIONS - 1].set(cotangent.astype(jnp.float32).reshape(batches, LONG_LEN, D))
    grads = backward(start_grads)
    section_outputs = outputs.reshape(SECTIONS, batches * LONG_LEN, D).astype(jnp.bfloat16)
    section_input_grads = grads[1].reshape(SECTIONS, batches * LONG_LEN, D).astype(jnp.bfloat16)
    return (section_outputs, section_input_grads, grads[2], grads[3], grads[4], grads[5], grads[6], grads[7])
```

```python
import functools

import jax
import jax.numpy as jnp
import numpy as np
from jax import lax
from jax.experimental import pallas as pl
from jax.experimental.pallas import tpu as pltpu
from jax.sharding import PartitionSpec as P

HEADS = 15
KV_HEADS = 5
HEAD_DIM = 64
FF = 2560
D = 960
Q_WIDTH = 960
QKV_WIDTH = 1600
SHORT_LEN = 16
LONG_LEN = 64
EPS = 1e-05
BASE = 10000.0
NEG = -1e30

BF = jnp.bfloat16
F32 = jnp.float32
MICROS = 2
ROWS = MICROS * LONG_LEN
CHUNK = 256
TILE = 128
TILES = 8
K_HALF = 15
V_HALF = 20
MESH = pl.DeviceIdType.MESH

KEEP = {"x": (0, 1024), "mid": (1024, 1024), "p": (2048, 1024), "qkv": (3072, 1664)}
KEEP["A"] = (4736, FF)
KEEP["B"] = (7296, FF)
KEEP_WIDTH = 9856
LEFT = {"n1": D, "mix": D, "n2": D, "hid": FF}
RIGHT = {"gqkv": QKV_WIDTH, "gat": D, "ggu": 2 * FF, "gff": D}
WEIGHTS = {"qkv": (D, QKV_WIDTH), "out": (Q_WIDTH, D), "gu": (D, 2 * FF), "dn": (FF, D)}


def nn(a, b):
    return lax.dot_general(a, b, (((1,), (0,)), ((), ())), preferred_element_type=F32)


def nt(a, b):
    return lax.dot_general(a, b, (((1,), (1,)), ((), ())), preferred_element_type=F32)


def tn(a, b):
    return lax.dot_general(a, b, (((0,), (0,)), ((), ())), preferred_element_type=F32)


def chunks(total, width=CHUNK):
    return [(c, min(width, total - c)) for c in range(0, total, width)]


def lane(rows):
    return lax.broadcasted_iota(jnp.int32, (rows, TILE), 1)


def inverse_rms(x):
    return lax.rsqrt(jnp.mean(x * x, -1, keepdims=True) + EPS)


def turn(tile):
    first = (lane(tile.shape[0]) % HEAD_DIM) < HEAD_DIM // 2
    return jnp.where(first, pltpu.roll(tile, TILE - 32, 1), pltpu.roll(tile, 32, 1))


def query_scale(column, rows):
    scale = HEAD_DIM**-0.5
    if column + TILE <= Q_WIDTH:
        return scale
    return jnp.where(lane(rows) < HEAD_DIM, scale, 1.0)


def head_pairs(ref, rows, first):
    low = lane(LONG_LEN) < HEAD_DIM
    tiles = {}
    spread = []
    for head in range(KV_HEADS):
        place = first + head
        t = place // 2
        if t not in tiles:
            width = min(TILE, QKV_WIDTH - t * TILE)
            x = ref[rows, t * TILE : t * TILE + width].astype(F32)
            if width < TILE:
                x = jnp.concatenate([x, x], 1)
            tiles[t] = (x, pltpu.roll(x, HEAD_DIM, 1))
        x, swapped = tiles[t]
        spread.append(jnp.where(low, x, swapped) if place % 2 == 0 else jnp.where(low, swapped, x))
    pairs = []
    for t in range(TILES):
        a = 2 * t // 3
        b = min((2 * t + 1) // 3, KV_HEADS - 1)
        pairs.append((spread[a] if a == b else jnp.where(low, spread[a], spread[b])).astype(BF))
    return pairs


def diagonal(ref, rows, t):
    low = lane(LONG_LEN) < HEAD_DIM
    x = ref[rows, t * TILE : (t + 1) * TILE].astype(F32)
    above = jnp.where(low, x, 0.0).astype(BF)
    below = jnp.where(low, 0.0, x).astype(BF)
    if t == TILES - 1:
        below = jnp.zeros_like(below)
    return jnp.concatenate([above, below], 0)


def micro_rows():
    return [slice(b * LONG_LEN, (b + 1) * LONG_LEN) for b in range(MICROS)]


def attention_forward(S):
    low = lane(LONG_LEN) < HEAD_DIM
    for rows in micro_rows():
        keys = head_pairs(S["qkv"], rows, K_HALF)
        for t in range(TILES):
            S["e"][rows, t * TILE : (t + 1) * TILE] = nt(keys[t], diagonal(S["qkv"], rows, t))
    for rows in micro_rows():
        bias = S["bias"][rows, :]
        for t in range(TILES):
            s = S["e"][rows, t * TILE : (t + 1) * TILE] + bias
            e = jnp.exp(s - jnp.max(s, 0, keepdims=True))
            z = 1.0 / jnp.sum(e, 0, keepdims=True)
            S["p"][rows, t * TILE : (t + 1) * TILE] = (e * z).astype(BF)
    for rows in micro_rows():
        values = head_pairs(S["qkv"], rows, V_HALF)
        for t in range(TILES):
            o = tn(S["p"][rows, t * TILE : (t + 1) * TILE], values[t])
            m = jnp.where(low, o[:LONG_LEN], o[LONG_LEN:]).astype(BF)
            width = min(TILE, Q_WIDTH - t * TILE)
            S["mix"][rows, t * TILE : t * TILE + width] = m[:, :width]


def block_forward(W, S, arrived):
    h = S["h"]
    x = h[...]
    S["x"][:, :D] = x.astype(BF)
    S["n1"][...] = (x * inverse_rms(x) * W["ga"][...]).astype(BF)
    arrived("qkv")
    n1 = S["n1"][...]
    for c, w in chunks(QKV_WIDTH):
        o = nn(n1, W["qkv"][:, c : c + w])
        for t, tw in chunks(w, TILE):
            column = c + t
            tile = o[:, t : t + tw]
            if column < Q_WIDTH + KV_HEADS * HEAD_DIM:
                tile = tile * S["cos"][...] + turn(tile) * S["sin"][...]
                if column < Q_WIDTH:
                    tile = tile * query_scale(column, ROWS)
            S["qkv"][:, column : column + tw] = tile.astype(BF)
    attention_forward(S)
    arrived("out")
    mix = S["mix"][...]
    for c, w in chunks(D):
        h[:, c : c + w] = h[:, c : c + w] + nn(mix, W["out"][:, c : c + w])
    x = h[...]
    S["mid"][:, :D] = x.astype(BF)
    S["n2"][...] = (x * inverse_rms(x) * W["gf"][...]).astype(BF)
    arrived("gu")
    n2 = S["n2"][...]
    for c, w in chunks(FF):
        gate = nn(n2, W["gu"][:, c : c + w])
        up = nn(n2, W["gu"][:, FF + c : FF + c + w])
        sg = 1.0 / (1.0 + jnp.exp(-gate))
        act = gate * sg
        S["B"][:, c : c + w] = act.astype(BF)
        S["A"][:, c : c + w] = (up * sg * (1.0 + gate * (1.0 - sg))).astype(BF)
        S["hid"][:, c : c + w] = (act * up).astype(BF)
    arrived("dn")
    hid = S["hid"][...]
    for c, w in chunks(D):
        h[:, c : c + w] = h[:, c : c + w] + nn(hid, W["dn"][:, c : c + w])


def attention_backward(S):
    low = lane(LONG_LEN) < HEAD_DIM
    for rows in micro_rows():
        values = head_pairs(S["qkv"], rows, V_HALF)
        for t in range(TILES):
            S["e"][rows, t * TILE : (t + 1) * TILE] = nt(values[t], diagonal(S["gm"], rows, t))
    for rows in micro_rows():
        for t in range(TILES):
            gp = S["e"][rows, t * TILE : (t + 1) * TILE]
            p = S["p"][rows, t * TILE : (t + 1) * TILE].astype(F32)
            total = jnp.sum(gp * p, 0, keepdims=True)
            S["gs"][rows, t * TILE : (t + 1) * TILE] = (p * (gp - total)).astype(BF)

    def store(rows, column, value, turned):
        if turned:
            value = value * S["cos"][rows, :] - turn(value) * S["sin"][rows, :]
        width = min(TILE, QKV_WIDTH - column)
        S["gqkv"][rows, column : column + width] = value[:, :width].astype(BF)

    def fold(parts):
        sums = []
        for head in range(KV_HEADS):
            lower, upper = None, None
            for q in (3 * head, 3 * head + 1, 3 * head + 2):
                part = parts[q // 2]
                if q % 2 == 0:
                    lower = part if lower is None else lower + part
                else:
                    upper = part if upper is None else upper + part
            sums.append((jnp.where(low, lower, 0.0), jnp.where(low, 0.0, upper)))
        return sums

    def placed(sums, head, half):
        lower, upper = sums[head]
        if half == 0:
            return lower + pltpu.roll(upper, HEAD_DIM, 1)
        return upper + pltpu.roll(lower, HEAD_DIM, 1)

    for rows in micro_rows():
        keys = head_pairs(S["qkv"], rows, K_HALF)
        grad_k, grad_v = [], []
        last = None
        for t in range(TILES):
            gs = S["gs"][rows, t * TILE : (t + 1) * TILE]
            grad_k.append(nn(gs, diagonal(S["qkv"], rows, t)))
            grad_v.append(
                nn(S["p"][rows, t * TILE : (t + 1) * TILE], diagonal(S["gm"], rows, t))
            )
            o = tn(gs, keys[t])
            grad_q = jnp.where(low, o[:LONG_LEN], o[LONG_LEN:]) * HEAD_DIM**-0.5
            if t < TILES - 1:
                store(rows, t * TILE, grad_q, True)
            else:
                last = grad_q
        k, v = fold(grad_k), fold(grad_v)
        store(rows, 896, jnp.where(low, last, placed(k, 0, 1)), True)
        store(rows, 1024, placed(k, 1, 0) + placed(k, 2, 1), True)
        store(rows, 1152, placed(k, 3, 0) + placed(k, 4, 1), True)
        store(rows, 1280, placed(v, 0, 0) + placed(v, 1, 1), False)
        store(rows, 1408, placed(v, 2, 0) + placed(v, 3, 1), False)
        store(rows, 1536, placed(v, 4, 0), False)


def rms_backward(x, gain, e, base):
    r = inverse_rms(x)
    scaled = e * gain
    mean = jnp.mean(x * scaled, -1, keepdims=True)
    return base + r * scaled - x * (r * r * r * mean), jnp.sum(e * x * r, 0, keepdims=True)


def block_backward(W, S, gain_attn_grad, gain_ffn_grad):
    g = S["h"]
    S["gff"][...] = g[...].astype(BF)
    gff = S["gff"][...]
    for c, w in chunks(FF):
        gh = nn(gff, W["dnT"][:, c : c + w])
        S["ggu"][:, c : c + w] = (gh * S["A"][:, c : c + w].astype(F32)).astype(BF)
        S["ggu"][:, FF + c : FF + c + w] = (gh * S["B"][:, c : c + w].astype(F32)).astype(BF)
    ggu = S["ggu"][...]
    for c, w in chunks(D):
        S["e"][:, c : c + w] = nn(ggu, W["guT"][:, c : c + w])
    new, gain = rms_backward(S["mid"][:, :D].astype(F32), W["gf"][...], S["e"][:, :D], g[...])
    gain_ffn_grad[...] += gain
    g[...] = new
    S["gat"][...] = new.astype(BF)
    gat = S["gat"][...]
    for c, w in chunks(Q_WIDTH):
        S["gm"][:, c : c + w] = nn(gat, W["outT"][:, c : c + w]).astype(BF)
    attention_backward(S)
    gqkv = S["gqkv"][...]
    for c, w in chunks(D):
        S["e"][:, c : c + w] = nn(gqkv, W["qkvT"][:, c : c + w])
    new, gain = rms_backward(S["x"][:, :D].astype(F32), W["ga"][...], S["e"][:, :D], g[...])
    gain_attn_grad[...] += gain
    g[...] = new


def transpose_weights(W):
    row = lax.broadcasted_iota(jnp.int32, (CHUNK, CHUNK), 0)
    column = lax.broadcasted_iota(jnp.int32, (CHUNK, CHUNK), 1)
    unit = jnp.where(row == column, 1.0, 0.0).astype(BF)
    for name, (depth, width) in WEIGHTS.items():
        source, target = W[name], W[name + "T"]

        def strip(start, size, source=source, target=target, depth=depth):
            for k, kw in chunks(depth):
                tile = nt(unit[:size, :size], source[k : k + kw, pl.ds(start, size)])
                target[pl.ds(start, size), k : k + kw] = tile.astype(BF)

        whole = width // CHUNK

        def one(i, carry, strip=strip):
            strip(pl.multiple_of(i * CHUNK, CHUNK), CHUNK)
            return carry

        lax.fori_loop(0, whole, one, 0)
        if width % CHUNK:
            strip(whole * CHUNK, width % CHUNK)


def make_constants(S, meta, item, tables):
    cos_long, sin_long, cos_short, sin_short = tables
    shape = (LONG_LEN, TILE)
    slot = lax.broadcasted_iota(jnp.int32, shape, 0)
    other = lane(LONG_LEN) % LONG_LEN
    piece = (slot // SHORT_LEN).astype(F32)
    other_piece = (other // SHORT_LEN).astype(F32)
    for b, rows in enumerate(micro_rows()):
        is_long = jnp.broadcast_to(meta[item, b : b + 1, :], shape) > 0.5
        count = jnp.broadcast_to(meta[item, MICROS + b : MICROS + b + 1, :], shape)
        S["cos"][rows, :] = jnp.where(is_long, cos_long[...], cos_short[...])
        S["sin"][rows, :] = jnp.where(is_long, sin_long[...], sin_short[...])
        short = jnp.where(other_piece < count, 0.0, jnp.where(slot == other, 0.0, NEG))
        short = jnp.where(piece == other_piece, short, NEG)
        bias = jnp.where(is_long, 0.0, short)
        S["bias"][rows, :] = jnp.where(slot <= other, bias, NEG)
        S["valid"][rows, :] = jnp.where(is_long, 1.0, jnp.where(piece < count, 1.0, 0.0))


IN_NAMES = (
    ["tok", "cot", "meta", "ga", "gf"] + list(WEIGHTS) + ["cosl", "sinl", "coss", "sins"]
)
OUT_NAMES = ["out", "gin"] + list(LEFT) + list(RIGHT) + ["keep", "gga", "ggf"]


def pipeline_kernel(sections, chips, own, scratch_names, *refs):
    refs = list(refs)
    I = dict(zip(IN_NAMES, refs))
    O = dict(zip(OUT_NAMES, refs[len(IN_NAMES) :]))
    R = dict(zip(scratch_names, refs[len(IN_NAMES) + len(OUT_NAMES) :]))
    far = own * (chips - 1)
    section = lax.axis_index("section")
    data = lax.axis_index("dp")
    chip, core = data // 2, data % 2
    is_first, is_last = section == 0, section == sections - 1
    W = {name: R["w_" + name] for name in WEIGHTS}
    W.update({name + "T": R["t_" + name] for name in WEIGHTS})
    W["ga"], W["gf"] = I["ga"], I["gf"]

    def partner(d):
        return lax.rem(chip - d + chips, chips) * 2 + core

    barrier = pltpu.get_barrier_semaphore()

    @pl.when(section > 0)
    def _():
        pl.semaphore_signal(barrier, 1, device_id={"section": section - 1}, device_id_type=MESH)

    @pl.when(section < sections - 1)
    def _():
        pl.semaphore_signal(barrier, 1, device_id={"section": section + 1}, device_id_type=MESH)

    for d in range(1, chips):
        pl.semaphore_signal(barrier, 1, device_id={"dp": partner(d)}, device_id_type=MESH)

    weight_copies = {
        name: pltpu.make_async_copy(I[name], W[name], R["w_sem"].at[k])
        for k, name in enumerate(WEIGHTS)
    }
    for copy in weight_copies.values():
        copy.start()

    def rows_of(ref, j):
        return ref.at[pl.ds(pl.multiple_of(j * ROWS, ROWS), ROWS), :]

    def token_copy(j):
        return pltpu.make_async_copy(rows_of(I["tok"], j), R["fin"].at[j], R["f_sem"].at[j])

    def cotangent_copy(j):
        return pltpu.make_async_copy(rows_of(I["cot"], j), R["bin"].at[j], R["b_sem"].at[j])

    @pl.when(is_first)
    def _():
        for j in range(own):
            token_copy(j).start()

    @pl.when(is_last)
    def _():
        for j in range(own):
            cotangent_copy(j).start()

    R["meta"][0:own] = I["meta"][...]
    O["gga"][...] = jnp.zeros_like(O["gga"])
    O["ggf"][...] = jnp.zeros_like(O["ggf"])
    R["gm"][...] = jnp.zeros_like(R["gm"])

    others = chips - 1
    near = jnp.where(is_first, 0, 1) + jnp.where(is_last, 0, 1)
    pl.semaphore_wait(barrier, near + others)

    def meta_copy(d):
        return pltpu.make_async_remote_copy(
            src_ref=I["meta"],
            dst_ref=R["meta"].at[pl.ds(own * d, own)],
            send_sem=R["ms_sem"].at[d - 1],
            recv_sem=R["m_sem"].at[d - 1],
            device_id={"dp": partner(d)},
            device_id_type=MESH,
        )

    def next_copy(j):
        return pltpu.make_async_remote_copy(
            src_ref=R["outs"].at[j],
            dst_ref=R["fin"].at[j],
            send_sem=R["fs_sem"].at[j],
            recv_sem=R["f_sem"].at[j],
            device_id={"section": section + 1},
            device_id_type=MESH,
        )

    def previous_copy(j):
        return pltpu.make_async_remote_copy(
            src_ref=R["outs"].at[j],
            dst_ref=R["bin"].at[j],
            send_sem=R["bs_sem"].at[j],
            recv_sem=R["b_sem"].at[j],
            device_id={"section": section - 1},
            device_id_type=MESH,
        )

    def far_copy(buffer, recv, send, d, j):
        return pltpu.make_async_remote_copy(
            src_ref=R[buffer].at[j],
            dst_ref=R[buffer].at[own * d + j],
            send_sem=R[send].at[own * (d - 1) + j],
            recv_sem=R[recv].at[own * d + j],
            device_id={"dp": partner(d)},
            device_id_type=MESH,
        )

    def far_forward(d, j):
        return far_copy("fin", "f_sem", "fx_sem", d, j)

    def far_backward(d, j):
        return far_copy("bin", "b_sem", "bx_sem", d, j)

    def out_copy(j):
        return pltpu.make_async_copy(R["outs"].at[j], rows_of(O["out"], j), R["o_sem"].at[j])

    def grad_copy(j):
        return pltpu.make_async_copy(R["outs"].at[j], rows_of(O["gin"], j), R["g_sem"].at[j])

    for d in range(1, chips):
        meta_copy(d).start()

    early = section >= sections // 2

    def views(slot):
        S = {name: R[name] for name in ("h", "e", "gm", "gs", "cos", "sin", "bias", "valid")}
        for name, (start, width) in KEEP.items():
            S[name] = R["keep"].at[slot, :, start : start + width]
        for name in list(LEFT) + list(RIGHT):
            S[name] = R[name].at[slot]
        return S

    def left_copies(slot, index):
        pairs = [(R["keep"].at[slot], O["keep"].at[index])]
        pairs += [(R[name].at[slot], O[name].at[index]) for name in LEFT]
        return [
            pltpu.make_async_copy(a, b, R["l_sem"].at[slot, k]) for k, (a, b) in enumerate(pairs)
        ]

    def right_copies(slot, index):
        return [
            pltpu.make_async_copy(R[name].at[slot], O[name].at[index], R["r_sem"].at[slot, k])
            for k, name in enumerate(RIGHT)
        ]

    def keep_load(slot, index):
        return pltpu.make_async_copy(O["keep"].at[index], R["keep"].at[slot], R["k_sem"].at[slot])

    def forward_phase(start, count, is_far):
        def step(k, carry):
            item = start + k

            @pl.when(is_far)
            def _():
                d = item // own
                far_copy("fin", "f_sem", "fx_sem", d, item - own * d).wait_recv()

            @pl.when(jnp.logical_not(is_far))
            def _():
                @pl.when(is_first)
                def _():
                    token_copy(item).wait()

                @pl.when(jnp.logical_not(is_first))
                def _():
                    next_copy(item).wait_recv()

                for d in range(1, chips):
                    far_forward(d, item).start()

            make_constants(
                R, R["meta"], item, (I["cosl"], I["sinl"], I["coss"], I["sins"])
            )
            R["h"][...] = R["fin"][item].astype(F32)

            def one(f, carry):
                @pl.when(k > 0)
                def _():
                    for copy in left_copies(f, 2 * (item - 1) + f):
                        copy.wait()

                fresh = jnp.logical_not(early) & (item == 0) & (f == 0)

                def arrived(name):
                    @pl.when(fresh)
                    def _():
                        weight_copies[name].wait()

                block_forward(W, views(f), arrived)
                for copy in left_copies(f, 2 * item + f):
                    copy.start()
                return carry

            lax.fori_loop(0, 2, one, 0)

            @pl.when(jnp.logical_not(is_far))
            def _():
                R["outs"][item] = (R["h"][...] * R["valid"][:, 0:1]).astype(BF)

                @pl.when(jnp.logical_not(is_last))
                def _():
                    next_copy(item).start()

                out_copy(item).start()

            return carry

        lax.fori_loop(0, count, step, 0)
        for f in range(2):
            for copy in left_copies(f, 2 * (start + count - 1) + f):
                copy.wait()

    def backward_phase(start, count, is_far):
        keep_load(1, 2 * start + 1).start()

        def step(k, carry):
            item = start + k

            @pl.when(is_far)
            def _():
                d = item // own
                far_copy("bin", "b_sem", "bx_sem", d, item - own * d).wait_recv()

            @pl.when(jnp.logical_not(is_far))
            def _():
                @pl.when(is_last)
                def _():
                    cotangent_copy(item).wait()

                @pl.when(jnp.logical_not(is_last))
                def _():
                    previous_copy(item).wait_recv()

                for d in range(1, chips):
                    far_backward(d, item).start()

            make_constants(
                R, R["meta"], item, (I["cosl"], I["sinl"], I["coss"], I["sins"])
            )
            R["h"][...] = R["bin"][item].astype(F32) * R["valid"][:, 0:1]

            def one(i, carry):
                f = 1 - i
                keep_load(f, 2 * item + f).wait()

                @pl.when(f == 1)
                def _():
                    keep_load(0, 2 * item).start()

                @pl.when((f == 0) & (k < count - 1))
                def _():
                    keep_load(1, 2 * item + 3).start()

                @pl.when(k > 0)
                def _():
                    for copy in right_copies(f, 2 * (item - 1) + f):
                        copy.wait()

                block_backward(W, views(f), O["gga"], O["ggf"])
                for copy in right_copies(f, 2 * item + f):
                    copy.start()
                return carry

            lax.fori_loop(0, 2, one, 0)

            @pl.when(jnp.logical_not(is_far))
            def _():
                @pl.when(jnp.logical_not(is_last))
                def _():
                    next_copy(item).wait_send()

                out_copy(item).wait()
                R["outs"][item] = R["h"][...].astype(BF)

                @pl.when(jnp.logical_not(is_first))
                def _():
                    previous_copy(item).start()

                grad_copy(item).start()

            return carry

        lax.fori_loop(0, count, step, 0)
        for f in range(2):
            for copy in right_copies(f, 2 * (start + count - 1) + f):
                copy.wait()

    phases = 4 if far else 2

    def phase(p, carry):
        if far:
            is_far = jnp.where(is_last, p >= 2, lax.rem(p, 2) == 1)
            is_back = jnp.where(is_last, lax.rem(p, 2) == 1, p >= 2)
            start = jnp.where(is_far, own, 0)
            count = jnp.where(is_far, far, own)
        else:
            is_far, is_back, start, count = p < 0, p == 1, 0, own

        @pl.when((p == 0) & early)
        def _():
            for copy in weight_copies.values():
                copy.wait()

        @pl.when(jnp.where(early, p == 0, p == phases // 2))
        def _():
            transpose_weights(W)

        if far:

            @pl.when(is_far & jnp.logical_not(is_back))
            def _():
                for d in range(1, chips):
                    meta_copy(d).wait_recv()

        @pl.when(jnp.logical_not(is_back))
        def _():
            forward_phase(start, count, is_far)

        @pl.when(is_back)
        def _():
            backward_phase(start, count, is_far)

        return carry

    lax.fori_loop(0, phases, phase, 0)

    for j in range(own):

        @pl.when(jnp.logical_not(is_first))
        def _():
            previous_copy(j).wait_send()

        grad_copy(j).wait()
        for d in range(1, chips):
            far_forward(d, j).wait_send()
            far_backward(d, j).wait_send()
    for d in range(1, chips):
        meta_copy(d).wait_send()


def rotary_tables():
    half = HEAD_DIM // 2
    frequency = BASE ** (-2.0 * np.arange(half, dtype=np.float32) / HEAD_DIM)
    slots = np.arange(LONG_LEN)
    tables = []
    for position in (slots, slots % SHORT_LEN):
        angle = position.astype(np.float32)[:, None] * frequency[None, :].astype(np.float32)
        cos, sin = np.cos(angle), np.sin(angle)
        tables.append(np.tile(np.concatenate([cos, cos], 1), (1, 2)).astype(np.float32))
        tables.append(np.tile(np.concatenate([-sin, sin], 1), (1, 2)).astype(np.float32))
    return tables


def run_pipeline(sections, chips, own, *args):
    items = own * chips
    vmem = lambda *shape, dtype=BF: pltpu.VMEM(shape, dtype)
    scratch = {
        "fin": vmem(items, ROWS, D),
        "bin": vmem(items, ROWS, D),
        "outs": vmem(own, ROWS, D),
        "meta": vmem(items, 8, TILE, dtype=F32),
        "keep": vmem(2, ROWS, KEEP_WIDTH),
        "h": vmem(ROWS, D, dtype=F32),
        "e": vmem(ROWS, 1024, dtype=F32),
        "gm": vmem(ROWS, 1024),
        "gs": vmem(ROWS, 1024),
    }
    for name in ("cos", "sin", "bias", "valid"):
        scratch[name] = vmem(ROWS, TILE, dtype=F32)
    for name, width in {**LEFT, **RIGHT}.items():
        scratch[name] = vmem(2, ROWS, width)
    for name, (depth, width) in WEIGHTS.items():
        scratch["w_" + name] = vmem(depth, width)
        scratch["t_" + name] = vmem(width, depth)
    far = max(1, own * (chips - 1))
    counts = {
        "w_sem": (len(WEIGHTS),),
        "f_sem": (items,),
        "b_sem": (items,),
        "fs_sem": (own,),
        "bs_sem": (own,),
        "fx_sem": (far,),
        "bx_sem": (far,),
        "m_sem": (max(1, chips - 1),),
        "ms_sem": (max(1, chips - 1),),
        "o_sem": (own,),
        "g_sem": (own,),
        "l_sem": (2, 1 + len(LEFT)),
        "r_sem": (2, len(RIGHT)),
        "k_sem": (2,),
    }
    for name, shape in counts.items():
        scratch[name] = pltpu.SemaphoreType.DMA(shape)
    hbm, local = pl.BlockSpec(memory_space=pl.ANY), pl.BlockSpec(memory_space=pltpu.VMEM)
    shapes = {"out": (own * ROWS, D), "gin": (own * ROWS, D)}
    for name, width in {**LEFT, **RIGHT}.items():
        shapes[name] = (2 * items, ROWS, width)
    shapes["keep"] = (2 * items, ROWS, KEEP_WIDTH)
    out_shape = [jax.ShapeDtypeStruct(shapes[name], BF) for name in OUT_NAMES[:-2]]
    out_shape += [jax.ShapeDtypeStruct((1, D), F32)] * 2
    in_vmem = ("meta", "ga", "gf", "cosl", "sinl", "coss", "sins")
    return pl.pallas_call(
        functools.partial(pipeline_kernel, sections, chips, own, list(scratch)),
        out_shape=out_shape,
        in_specs=[local if name in in_vmem else hbm for name in IN_NAMES],
        out_specs=[hbm] * (len(OUT_NAMES) - 2) + [local] * 2,
        scratch_shapes=list(scratch.values()),
        compiler_params=pltpu.CompilerParams(
            collective_id=0, has_side_effects=True, vmem_limit_bytes=127 * 2**19
        ),
    )(*args)


def body(tokens, cotangent, seq_counts, attn_gain, w_qkv, w_out, ffn_gain, w_gate_up, w_down):
    sections = lax.axis_size("section")
    groups = lax.axis_size("dp")
    data = lax.axis_index("dp")
    chips = groups // 2
    own = tokens.shape[0] // ROWS
    meta = seq_counts.astype(F32).reshape(own, MICROS, 2).transpose(0, 2, 1)
    meta = jnp.pad(meta.reshape(own, 2 * MICROS), ((0, 0), (0, 8 - 2 * MICROS)))
    meta = jnp.broadcast_to(meta[:, :, None], (own, 8, TILE))
    results = run_pipeline(
        sections,
        chips,
        own,
        tokens,
        cotangent,
        meta,
        attn_gain,
        ffn_gain,
        w_qkv[0],
        w_out[0],
        w_gate_up[0],
        w_down[0],
        *[jnp.asarray(table) for table in rotary_tables()],
    )
    O = dict(zip(OUT_NAMES, results))
    share = D // groups
    begin = (data // 2) * 2 * share
    flip = [(i, i ^ 1) for i in range(groups)]

    def flat(name):
        return O[name].reshape(-1, O[name].shape[-1])

    def part(value, axis=1):
        return lax.dynamic_slice_in_dim(value, begin, 2 * share, axis)

    def exchange(both, axis):
        mine = lax.dynamic_slice_in_dim(both, (data % 2) * share, share, axis)
        other = lax.dynamic_slice_in_dim(both, (1 - data % 2) * share, share, axis)
        return mine + lax.ppermute(other.astype(BF), "dp", flip).astype(F32)

    gate_up_grad = exchange(tn(part(flat("n2")), flat("ggu")), 0)
    down_grad = exchange(tn(flat("hid"), part(flat("gff"))), 1)
    qkv_grad = exchange(tn(part(flat("n1")), flat("gqkv")), 0)
    out_grad = exchange(tn(flat("mix"), part(flat("gat"))), 1)
    attn_gain_grad = exchange(part(O["gga"]), 1)
    ffn_gain_grad = exchange(part(O["ggf"]), 1)
    return (
        O["out"][None],
        O["gin"][None],
        attn_gain_grad,
        qkv_grad[None],
        out_grad[None],
        ffn_gain_grad,
        gate_up_grad[None],
        down_grad[None],
    )


def solution(mesh):
    in_specs = (
        P("dp", None),
        P("dp", None),
        P("dp", None),
        P("section", None),
        P("section", None, None),
        P("section", None, None),
        P("section", None),
        P("section", None, None),
        P("section", None, None),
    )
    out_specs = (
        P("section", "dp", None),
        P("section", "dp", None),
        P("section", "dp"),
        P("section", "dp", None),
        P("section", None, "dp"),
        P("section", "dp"),
        P("section", "dp", None),
        P("section", None, "dp"),
    )
    return jax.shard_map(body, mesh=mesh, in_specs=in_specs, out_specs=out_specs, check_vma=False)
```

```python
import functools

import jax
import jax.numpy as jnp
import numpy as np
from jax import lax
from jax.experimental import pallas as pl
from jax.experimental.pallas import tpu as pltpu
from jax.sharding import PartitionSpec as P

HEADS = 15
KV_HEADS = 5
HEAD_DIM = 64
FF = 2560
D = 960
Q_WIDTH = 960
QKV_WIDTH = 1600
SHORT_LEN = 16
LONG_LEN = 64
EPS = 1e-05
BASE = 10000.0
NEG = -1e30


class Box(dict):
    __getattr__ = dict.__getitem__
    __setattr__ = dict.__setitem__


BF = jnp.bfloat16
F32 = jnp.float32
MICROS = 2
ROWS = MICROS * LONG_LEN
CHUNK = 256
TILE = 128
TILES = 8
K_HALF = 15
V_HALF = 20
MESH = pl.DeviceIdType.MESH
DOWN = "dnT"

KEEP = dict(x=(0, 1024), mid=(1024, 1024), p=(2048, 1024), qkv=(3072, 1664))
KEEP.update(A=(4736, FF), B=(7296, FF))
KEEP_WIDTH = 9856
LEFT = dict(n1=D, mix=D, n2=D, hid=FF)
RIGHT = dict(gqkv=QKV_WIDTH, gat=D, ggu=2 * FF, gff=D)
WEIGHTS = dict(qkv=(D, QKV_WIDTH), out=(Q_WIDTH, D), gu=(D, 2 * FF), dn=(FF, D))


def nn(a, b):
    return lax.dot_general(a, b, (((1,), (0,)), ((), ())), preferred_element_type=F32)


def nt(a, b):
    return lax.dot_general(a, b, (((1,), (1,)), ((), ())), preferred_element_type=F32)


def tn(a, b):
    return lax.dot_general(a, b, (((0,), (0,)), ((), ())), preferred_element_type=F32)


def chunks(total, width=CHUNK):
    return [(c, min(width, total - c)) for c in range(0, total, width)]


def lane(rows):
    return lax.broadcasted_iota(jnp.int32, (rows, TILE), 1)


def inverse_rms(x):
    return lax.rsqrt(jnp.mean(x * x, -1, keepdims=True) + EPS)


def turn(tile):
    first = (lane(tile.shape[0]) % HEAD_DIM) < HEAD_DIM // 2
    return jnp.where(first, pltpu.roll(tile, TILE - 32, 1), pltpu.roll(tile, 32, 1))


def query_scale(column, rows):
    scale = HEAD_DIM**-0.5
    if column + TILE <= Q_WIDTH:
        return scale
    return jnp.where(lane(rows) < HEAD_DIM, scale, 1.0)


def head_pairs(ref, rows, first):
    low = lane(LONG_LEN) < HEAD_DIM
    tiles = {}
    spread = []
    for head in range(KV_HEADS):
        place = first + head
        t = place // 2
        if t not in tiles:
            width = min(TILE, QKV_WIDTH - t * TILE)
            x = ref[rows, t * TILE : t * TILE + width].astype(F32)
            if width < TILE:
                x = jnp.concatenate([x, x], 1)
            tiles[t] = (x, pltpu.roll(x, HEAD_DIM, 1))
        x, swapped = tiles[t]
        spread.append(jnp.where(low, x, swapped) if place % 2 == 0 else jnp.where(low, swapped, x))
    pairs = []
    for t in range(TILES):
        a = 2 * t // 3
        b = min((2 * t + 1) // 3, KV_HEADS - 1)
        pairs.append((spread[a] if a == b else jnp.where(low, spread[a], spread[b])).astype(BF))
    return pairs


def diagonal(ref, rows, t):
    low = lane(LONG_LEN) < HEAD_DIM
    x = ref[rows, t * TILE : (t + 1) * TILE].astype(F32)
    above = jnp.where(low, x, 0.0).astype(BF)
    below = jnp.where(low, 0.0, x).astype(BF)
    if t == TILES - 1:
        below = jnp.zeros_like(below)
    return jnp.concatenate([above, below], 0)


def micro_rows():
    return [slice(b * LONG_LEN, (b + 1) * LONG_LEN) for b in range(MICROS)]


def attention_forward(S):
    low = lane(LONG_LEN) < HEAD_DIM
    for rows in micro_rows():
        keys = head_pairs(S.qkv, rows, K_HALF)
        for t in range(TILES):
            S.e[rows, t * TILE : (t + 1) * TILE] = nt(keys[t], diagonal(S.qkv, rows, t))
    for rows in micro_rows():
        bias = S.bias[rows, :]
        for t in range(TILES):
            s = S.e[rows, t * TILE : (t + 1) * TILE] + bias
            e = jnp.exp(s - jnp.max(s, 0, keepdims=True))
            z = 1.0 / jnp.sum(e, 0, keepdims=True)
            S.p[rows, t * TILE : (t + 1) * TILE] = (e * z).astype(BF)
    for rows in micro_rows():
        values = head_pairs(S.qkv, rows, V_HALF)
        for t in range(TILES):
            o = tn(S.p[rows, t * TILE : (t + 1) * TILE], values[t])
            m = jnp.where(low, o[:LONG_LEN], o[LONG_LEN:]).astype(BF)
            width = min(TILE, Q_WIDTH - t * TILE)
            S.mix[rows, t * TILE : t * TILE + width] = m[:, :width]


def block_forward(W, S, arrived):
    h = S.h
    x = h[...]
    S.x[:, :D] = x.astype(BF)
    S.n1[...] = (x * inverse_rms(x) * W.ga[...]).astype(BF)
    arrived("qkv")
    n1 = S.n1[...]
    for c, w in chunks(QKV_WIDTH):
        o = nn(n1, W.qkv[:, c : c + w])
        for t, tw in chunks(w, TILE):
            column = c + t
            tile = o[:, t : t + tw]
            if column < Q_WIDTH + KV_HEADS * HEAD_DIM:
                tile = tile * S.cos[...] + turn(tile) * S.sin[...]
                if column < Q_WIDTH:
                    tile = tile * query_scale(column, ROWS)
            S.qkv[:, column : column + tw] = tile.astype(BF)
    attention_forward(S)
    arrived("out")
    mix = S.mix[...]
    for c, w in chunks(D):
        h[:, c : c + w] = h[:, c : c + w] + nn(mix, W.out[:, c : c + w])
    x = h[...]
    S.mid[:, :D] = x.astype(BF)
    S.n2[...] = (x * inverse_rms(x) * W.gf[...]).astype(BF)
    arrived("gu")
    n2 = S.n2[...]
    for c, w in chunks(FF):
        gate = nn(n2, W.gu[:, c : c + w])
        up = nn(n2, W.gu[:, FF + c : FF + c + w])
        sg = 1.0 / (1.0 + jnp.exp(-gate))
        act = gate * sg
        S.B[:, c : c + w] = act.astype(BF)
        S.A[:, c : c + w] = (up * sg * (1.0 + gate * (1.0 - sg))).astype(BF)
        S.hid[:, c : c + w] = (act * up).astype(BF)
    arrived("dn")
    hid = S.hid[...]
    for c, w in chunks(D):
        h[:, c : c + w] = h[:, c : c + w] + nn(hid, W.dn[:, c : c + w])


def attention_backward(S):
    low = lane(LONG_LEN) < HEAD_DIM
    for rows in micro_rows():
        values = head_pairs(S.qkv, rows, V_HALF)
        for t in range(TILES):
            S.e[rows, t * TILE : (t + 1) * TILE] = nt(values[t], diagonal(S.gm, rows, t))
    for rows in micro_rows():
        for t in range(TILES):
            gp = S.e[rows, t * TILE : (t + 1) * TILE]
            p = S.p[rows, t * TILE : (t + 1) * TILE].astype(F32)
            total = jnp.sum(gp * p, 0, keepdims=True)
            S.gs[rows, t * TILE : (t + 1) * TILE] = (p * (gp - total)).astype(BF)

    def store(rows, column, value, turned):
        if turned:
            value = value * S.cos[rows, :] - turn(value) * S.sin[rows, :]
        width = min(TILE, QKV_WIDTH - column)
        S.gqkv[rows, column : column + width] = value[:, :width].astype(BF)

    def fold(parts):
        sums = []
        for head in range(KV_HEADS):
            lower, upper = None, None
            for q in (3 * head, 3 * head + 1, 3 * head + 2):
                part = parts[q // 2]
                if q % 2 == 0:
                    lower = part if lower is None else lower + part
                else:
                    upper = part if upper is None else upper + part
            sums.append((jnp.where(low, lower, 0.0), jnp.where(low, 0.0, upper)))
        return sums

    def placed(sums, head, half):
        lower, upper = sums[head]
        if half == 0:
            return lower + pltpu.roll(upper, HEAD_DIM, 1)
        return upper + pltpu.roll(lower, HEAD_DIM, 1)

    for rows in micro_rows():
        keys = head_pairs(S.qkv, rows, K_HALF)
        grad_k, grad_v = [], []
        last = None
        for t in range(TILES):
            gs = S.gs[rows, t * TILE : (t + 1) * TILE]
            grad_k.append(nn(gs, diagonal(S.qkv, rows, t)))
            grad_v.append(
                nn(S.p[rows, t * TILE : (t + 1) * TILE], diagonal(S.gm, rows, t))
            )
            o = tn(gs, keys[t])
            grad_q = jnp.where(low, o[:LONG_LEN], o[LONG_LEN:]) * HEAD_DIM**-0.5
            if t < TILES - 1:
                store(rows, t * TILE, grad_q, True)
            else:
                last = grad_q
        k, v = fold(grad_k), fold(grad_v)
        store(rows, 896, jnp.where(low, last, placed(k, 0, 1)), True)
        store(rows, 1024, placed(k, 1, 0) + placed(k, 2, 1), True)
        store(rows, 1152, placed(k, 3, 0) + placed(k, 4, 1), True)
        store(rows, 1280, placed(v, 0, 0) + placed(v, 1, 1), False)
        store(rows, 1408, placed(v, 2, 0) + placed(v, 3, 1), False)
        store(rows, 1536, placed(v, 4, 0), False)


def rms_backward(x, gain, e, base):
    r = inverse_rms(x)
    scaled = e * gain
    mean = jnp.mean(x * scaled, -1, keepdims=True)
    return base + r * scaled - x * (r * r * r * mean), jnp.sum(e * x * r, 0, keepdims=True)


def block_backward(W, S, gain_attn_grad, gain_ffn_grad):
    g = S.h
    S.gff[...] = g[...].astype(BF)
    gff = S.gff[...]
    for c, w in chunks(FF):
        gh = nn(gff, W.dnT[:, c : c + w])
        S.ggu[:, c : c + w] = (gh * S.A[:, c : c + w].astype(F32)).astype(BF)
        S.ggu[:, FF + c : FF + c + w] = (gh * S.B[:, c : c + w].astype(F32)).astype(BF)
    ggu = S.ggu[...]
    for c, w in chunks(D):
        S.e[:, c : c + w] = nn(ggu, W.guT[:, c : c + w])
    new, gain = rms_backward(S.mid[:, :D].astype(F32), W.gf[...], S.e[:, :D], g[...])
    gain_ffn_grad[...] += gain
    g[...] = new
    S.gat[...] = new.astype(BF)
    gat = S.gat[...]
    for c, w in chunks(Q_WIDTH):
        S.gm[:, c : c + w] = nn(gat, W.outT[:, c : c + w]).astype(BF)
    attention_backward(S)
    gqkv = S.gqkv[...]
    for c, w in chunks(D):
        S.e[:, c : c + w] = nn(gqkv, W.qkvT[:, c : c + w])
    new, gain = rms_backward(S.x[:, :D].astype(F32), W.ga[...], S.e[:, :D], g[...])
    gain_attn_grad[...] += gain
    g[...] = new


def flip(source, target, size=CHUNK):
    depth, width = source.shape
    whole = width // size

    def strip(start, w):
        for k, kw in chunks(depth):
            target[pl.ds(start, w), k : k + kw] = source[k : k + kw, pl.ds(start, w)].T

    def one(i, carry):
        strip(pl.multiple_of(i * size, size), size)
        return carry

    lax.fori_loop(0, whole, one, 0)
    if width % size:
        strip(whole * size, width % size)


def make_constants(S, meta, item, tables):
    cos_long, sin_long, cos_short, sin_short = tables
    shape = (LONG_LEN, TILE)
    slot = lax.broadcasted_iota(jnp.int32, shape, 0)
    other = lane(LONG_LEN) % LONG_LEN
    piece = (slot // SHORT_LEN).astype(F32)
    other_piece = (other // SHORT_LEN).astype(F32)
    for b, rows in enumerate(micro_rows()):
        is_long = jnp.broadcast_to(meta[item, b : b + 1, :], shape) > 0.5
        count = jnp.broadcast_to(meta[item, MICROS + b : MICROS + b + 1, :], shape)
        S.cos[rows, :] = jnp.where(is_long, cos_long[...], cos_short[...])
        S.sin[rows, :] = jnp.where(is_long, sin_long[...], sin_short[...])
        short = jnp.where(other_piece < count, 0.0, jnp.where(slot == other, 0.0, NEG))
        short = jnp.where(piece == other_piece, short, NEG)
        bias = jnp.where(is_long, 0.0, short)
        S.bias[rows, :] = jnp.where(slot <= other, bias, NEG)
        S.valid[rows, :] = jnp.where(is_long, 1.0, jnp.where(piece < count, 1.0, 0.0))


def named(names, refs):
    boxes = []
    for group in names:
        boxes.append(Box(zip(group, refs)))
        refs = refs[len(group) :]
    return boxes


def pipeline_kernel(sections, chips, own, names, *refs):
    I, O, R = named(names, refs)
    far = own * (chips - 1)
    section = lax.axis_index("section")
    data = lax.axis_index("dp")
    chip, core = data // 2, data % 2
    is_first, is_last = section == 0, section == sections - 1
    W = Box({name: R["w_" + name] for name in WEIGHTS})
    W.update({name + "T": R["t_" + name] for name in WEIGHTS})
    W.ga, W.gf = I.ga, I.gf

    def partner(d):
        return lax.rem(chip - d + chips, chips) * 2 + core

    barrier = pltpu.get_barrier_semaphore()

    @pl.when(section > 0)
    def _():
        pl.semaphore_signal(barrier, 1, device_id=dict(section=section - 1), device_id_type=MESH)

    @pl.when(section < sections - 1)
    def _():
        pl.semaphore_signal(barrier, 1, device_id=dict(section=section + 1), device_id_type=MESH)

    for d in range(1, chips):
        pl.semaphore_signal(barrier, 1, device_id=dict(dp=partner(d)), device_id_type=MESH)

    early_names = [name for name in WEIGHTS if name in I]
    weight_names = early_names + [DOWN]
    weight_copies = {
        name: pltpu.make_async_copy(I[name], W[name], R.w_sem.at[k])
        for k, name in enumerate(weight_names)
    }
    slab = W.dn.at[0:D, 0 : own * ROWS]
    token_copy = pltpu.make_async_copy(I.tok, slab, R.t_sem)
    cotangent_copy = pltpu.make_async_copy(I.cot, slab, R.t_sem)

    @pl.when(is_first)
    def _():
        token_copy.start()

    @pl.when(is_last)
    def _():
        cotangent_copy.start()

    for copy in weight_copies.values():
        copy.start()

    def columns_of(ref, j):
        return ref.at[:, pl.ds(pl.multiple_of(j * ROWS, ROWS), ROWS)]

    R.meta[0:own] = I.meta[...]
    O.gga[...] = jnp.zeros_like(O.gga)
    O.ggf[...] = jnp.zeros_like(O.ggf)
    R.gm[...] = jnp.zeros_like(R.gm)

    others = chips - 1
    near = jnp.where(is_first, 0, 1) + jnp.where(is_last, 0, 1)
    pl.semaphore_wait(barrier, near + others)

    def meta_copy(d):
        return pltpu.make_async_remote_copy(
            src_ref=I.meta,
            dst_ref=R.meta.at[pl.ds(own * d, own)],
            send_sem=R.ms_sem.at[d - 1],
            recv_sem=R.m_sem.at[d - 1],
            device_id=dict(dp=partner(d)),
            device_id_type=MESH,
        )

    def next_copy(j):
        return pltpu.make_async_remote_copy(
            src_ref=R.outs.at[j],
            dst_ref=R.fin.at[j],
            send_sem=R.fs_sem.at[j],
            recv_sem=R.f_sem.at[j],
            device_id=dict(section=section + 1),
            device_id_type=MESH,
        )

    def previous_copy(j):
        return pltpu.make_async_remote_copy(
            src_ref=R.outs.at[j],
            dst_ref=R.bin.at[j],
            send_sem=R.bs_sem.at[j],
            recv_sem=R.b_sem.at[j],
            device_id=dict(section=section - 1),
            device_id_type=MESH,
        )

    def far_copy(buffer, recv, send, d, j):
        return pltpu.make_async_remote_copy(
            src_ref=buffer.at[j],
            dst_ref=buffer.at[own * d + j],
            send_sem=send.at[own * (d - 1) + j],
            recv_sem=recv.at[own * d + j],
            device_id=dict(dp=partner(d)),
            device_id_type=MESH,
        )

    def far_forward(d, j):
        return far_copy(R.fin, R.f_sem, R.fx_sem, d, j)

    def far_backward(d, j):
        return far_copy(R.bin, R.b_sem, R.bx_sem, d, j)

    def out_copy(j):
        return pltpu.make_async_copy(R.flip, columns_of(O.out, j), R.o_sem.at[j])

    def grad_copy(j):
        return pltpu.make_async_copy(R.flip, columns_of(O.gin, j), R.g_sem.at[j])

    for d in range(1, chips):
        meta_copy(d).start()

    @pl.when(is_first)
    def _():
        token_copy.wait()
        for j in range(own):
            for c, w in chunks(D):
                R.fin[j, :, c : c + w] = slab[c : c + w, j * ROWS : (j + 1) * ROWS].T

    @pl.when(is_last)
    def _():
        cotangent_copy.wait()
        for j in range(own):
            for c, w in chunks(D):
                R.bin[j, :, c : c + w] = slab[c : c + w, j * ROWS : (j + 1) * ROWS].T

    early = section >= sections // 2

    def views(slot):
        S = Box(R)
        for name, (start, width) in KEEP.items():
            S[name] = R.keep.at[slot, :, start : start + width]
        for name in list(LEFT) + list(RIGHT):
            S[name] = R[name].at[slot]
        return S

    def left_copies(slot, index):
        pairs = [(R.keep.at[slot], O.keep.at[index])]
        pairs += [(R[name].at[slot], O[name].at[index]) for name in LEFT]
        return [
            pltpu.make_async_copy(a, b, R.l_sem.at[slot, k]) for k, (a, b) in enumerate(pairs)
        ]

    def right_copies(slot, index):
        return [
            pltpu.make_async_copy(R[name].at[slot], O[name].at[index], R.r_sem.at[slot, k])
            for k, name in enumerate(RIGHT)
        ]

    def keep_load(slot, index):
        return pltpu.make_async_copy(O.keep.at[index], R.keep.at[slot], R.k_sem.at[slot])

    def turn_out():
        value = R.h[...]

        for c, w in chunks(D):
            R.flip[c : c + w, :] = value[:, c : c + w].astype(BF).T

    def forward_phase(start, count, is_far):
        def step(k, carry):
            item = start + k

            @pl.when(is_far)
            def _():
                d = item // own
                far_forward(d, item - own * d).wait_recv()

            @pl.when(jnp.logical_not(is_far))
            def _():
                @pl.when(jnp.logical_not(is_first))
                def _():
                    next_copy(item).wait_recv()

                for d in range(1, chips):
                    far_forward(d, item).start()

            make_constants(
                R, R.meta, item, (I.cosl, I.sinl, I.coss, I.sins)
            )
            R.h[...] = R.fin[item].astype(F32)

            def one(f, carry):
                @pl.when(k > 0)
                def _():
                    for copy in left_copies(f, 2 * (item - 1) + f):
                        copy.wait()

                fresh = jnp.logical_not(early) & (item == 0) & (f == 0)

                def arrived(name):
                    if name not in early_names:

                        @pl.when(fresh & is_first)
                        def _():
                            weight_copies[DOWN].wait()
                            flip(W.dnT, W.dn)

                    else:

                        @pl.when(fresh)
                        def _():
                            weight_copies[name].wait()

                block_forward(W, views(f), arrived)

                @pl.when(f == 0)
                def _():
                    for copy in left_copies(0, 2 * item):
                        copy.start()

                return carry

            lax.fori_loop(0, 2, one, 0)

            @pl.when(jnp.logical_not(is_far))
            def _():
                R.h[...] = R.h[...] * R.valid[:, 0:1]
                R.outs[item] = R.h[...].astype(BF)

                @pl.when(jnp.logical_not(is_last))
                def _():
                    next_copy(item).start()

                @pl.when(item > 0)
                def _():
                    out_copy(item - 1).wait()

                turn_out()
                out_copy(item).start()

            for copy in left_copies(1, 2 * item + 1):
                copy.start()
            return carry

        lax.fori_loop(0, count, step, 0)
        for f in range(2):
            for copy in left_copies(f, 2 * (start + count - 1) + f):
                copy.wait()

    def backward_phase(start, count, is_far):
        keep_load(1, 2 * start + 1).start()

        def step(k, carry):
            item = start + k

            @pl.when(is_far)
            def _():
                d = item // own
                far_backward(d, item - own * d).wait_recv()

            @pl.when(jnp.logical_not(is_far))
            def _():
                @pl.when(jnp.logical_not(is_last))
                def _():
                    previous_copy(item).wait_recv()

                for d in range(1, chips):
                    far_backward(d, item).start()

            make_constants(
                R, R.meta, item, (I.cosl, I.sinl, I.coss, I.sins)
            )
            R.h[...] = R.bin[item].astype(F32) * R.valid[:, 0:1]

            def one(i, carry):
                f = 1 - i
                keep_load(f, 2 * item + f).wait()

                @pl.when(f == 1)
                def _():
                    keep_load(0, 2 * item).start()

                @pl.when((f == 0) & (k < count - 1))
                def _():
                    keep_load(1, 2 * item + 3).start()

                @pl.when(k > 0)
                def _():
                    for copy in right_copies(f, 2 * (item - 1) + f):
                        copy.wait()

                block_backward(W, views(f), O.gga, O.ggf)

                @pl.when(f == 1)
                def _():
                    for copy in right_copies(1, 2 * item + 1):
                        copy.start()

                return carry

            lax.fori_loop(0, 2, one, 0)

            @pl.when(jnp.logical_not(is_far))
            def _():
                @pl.when(jnp.logical_not(is_last))
                def _():
                    next_copy(item).wait_send()

                R.outs[item] = R.h[...].astype(BF)

                @pl.when(jnp.logical_not(is_first))
                def _():
                    previous_copy(item).start()

                @pl.when(item > 0)
                def _():
                    grad_copy(item - 1).wait()

                @pl.when(item == 0)
                def _():
                    out_copy(own - 1).wait()

                turn_out()
                grad_copy(item).start()

            for copy in right_copies(0, 2 * item):
                copy.start()
            return carry

        lax.fori_loop(0, count, step, 0)
        for f in range(2):
            for copy in right_copies(f, 2 * (start + count - 1) + f):
                copy.wait()

    phases = 4 if far else 2

    def phase(p, carry):
        if far:
            is_far = jnp.where(is_last, p >= 2, lax.rem(p, 2) == 1)
            is_back = jnp.where(is_last, lax.rem(p, 2) == 1, p >= 2)
            start = jnp.where(is_far, own, 0)
            count = jnp.where(is_far, far, own)
        else:
            is_far, is_back, start, count = p < 0, p == 1, 0, own

        @pl.when((p == 0) & jnp.logical_not(is_first))
        def _():
            weight_copies[DOWN].wait()
            flip(W.dnT, W.dn)

        @pl.when((p == 0) & early)
        def _():
            for name in early_names:
                weight_copies[name].wait()

        @pl.when(jnp.where(early, p == 0, p == phases // 2))
        def _():
            for name in early_names:
                flip(W[name], W[name + "T"])

        if far:

            @pl.when(is_far & jnp.logical_not(is_back))
            def _():
                for d in range(1, chips):
                    meta_copy(d).wait_recv()

        @pl.when(jnp.logical_not(is_back))
        def _():
            forward_phase(start, count, is_far)

        @pl.when(is_back)
        def _():
            backward_phase(start, count, is_far)

        return carry

    lax.fori_loop(0, phases, phase, 0)

    for j in range(own):

        @pl.when(jnp.logical_not(is_first))
        def _():
            previous_copy(j).wait_send()

        for d in range(1, chips):
            far_forward(d, j).wait_send()
            far_backward(d, j).wait_send()
    grad_copy(own - 1).wait()
    for d in range(1, chips):
        meta_copy(d).wait_send()


def rotary_tables():
    half = HEAD_DIM // 2
    frequency = BASE ** (-2.0 * np.arange(half, dtype=np.float32) / HEAD_DIM)
    slots = np.arange(LONG_LEN)
    tables = []
    for position in (slots, slots % SHORT_LEN):
        angle = position.astype(np.float32)[:, None] * frequency[None, :].astype(np.float32)
        cos, sin = np.cos(angle), np.sin(angle)
        tables.append(np.tile(np.concatenate([cos, cos], 1), (1, 2)).astype(np.float32))
        tables.append(np.tile(np.concatenate([-sin, sin], 1), (1, 2)).astype(np.float32))
    return tables


def vmem(*shape, dtype=BF):
    return pltpu.VMEM(shape, dtype)


HBM = pl.BlockSpec(memory_space=pl.ANY)
LOCAL = pl.BlockSpec(memory_space=pltpu.VMEM)
VMEM_LIMIT = 127 * 2**19


def run_pipeline(sections, chips, own, hbm_inputs, inputs):
    items = own * chips
    scratch = Box(
        fin=vmem(items, ROWS, D),
        bin=vmem(items, ROWS, D),
        outs=vmem(own, ROWS, D),
        flip=vmem(D, ROWS),
        meta=vmem(items, 8, TILE, dtype=F32),
        keep=vmem(2, ROWS, KEEP_WIDTH),
        h=vmem(ROWS, D, dtype=F32),
        e=vmem(ROWS, 1024, dtype=F32),
        gm=vmem(ROWS, 1024),
        gs=vmem(ROWS, 1024),
        cos=vmem(ROWS, TILE, dtype=F32),
        sin=vmem(ROWS, TILE, dtype=F32),
        bias=vmem(ROWS, TILE, dtype=F32),
        valid=vmem(ROWS, TILE, dtype=F32),
    )
    for name, width in {**LEFT, **RIGHT}.items():
        scratch[name] = vmem(2, ROWS, width)
    for name, (depth, width) in WEIGHTS.items():
        scratch["w_" + name] = vmem(depth, width)
        scratch["t_" + name] = vmem(width, depth)
    far = max(1, own * (chips - 1))
    counts = dict(
        w_sem=(len(WEIGHTS),),
        f_sem=(items,),
        b_sem=(items,),
        fs_sem=(own,),
        bs_sem=(own,),
        fx_sem=(far,),
        bx_sem=(far,),
        m_sem=(max(1, chips - 1),),
        ms_sem=(max(1, chips - 1),),
        o_sem=(own,),
        g_sem=(own,),
        l_sem=(2, 1 + len(LEFT)),
        r_sem=(2, len(RIGHT)),
        k_sem=(2,),
    )
    for name, shape in counts.items():
        scratch[name] = pltpu.SemaphoreType.DMA(shape)
    scratch.t_sem = pltpu.SemaphoreType.DMA
    shapes = Box(out=(D, own * ROWS), gin=(D, own * ROWS))
    for name, width in {**LEFT, **RIGHT}.items():
        shapes[name] = (2 * items, ROWS, width)
    shapes.keep = (2 * items, ROWS, KEEP_WIDTH)
    out_shape = Box({name: jax.ShapeDtypeStruct(shape, BF) for name, shape in shapes.items()})
    out_shape.gga = out_shape.ggf = jax.ShapeDtypeStruct((1, D), F32)
    names = [[*hbm_inputs, *inputs], list(out_shape), list(scratch)]
    results = pl.pallas_call(
        functools.partial(pipeline_kernel, sections, chips, own, names),
        out_shape=list(out_shape.values()),
        in_specs=[HBM] * len(hbm_inputs) + [LOCAL] * len(inputs),
        out_specs=[HBM] * len(shapes) + [LOCAL] * 2,
        scratch_shapes=list(scratch.values()),
        compiler_params=pltpu.CompilerParams(
            collective_id=0, has_side_effects=True, vmem_limit_bytes=VMEM_LIMIT
        ),
    )(*hbm_inputs.values(), *inputs.values())
    return Box(zip(out_shape, results))


PRODUCTS = dict(out=(*"gat mix".split(), Q_WIDTH), qkv=(*"n1 gqkv".split(), QKV_WIDTH))
PRODUCTS.update(dn=(*"gff hid".split(), FF), gu=(*"n2 ggu".split(), 2 * FF))
SPAN = 10


def spans_of(base, width):
    return [(base + i, n) for i, n in chunks(len(chunks(width)), SPAN)]


def gradient_kernel(depth, share, names, *refs):
    I, O, R = named(names, refs)
    data = lax.axis_index("dp")
    chip, core = data // 2, data % 2
    sibling = dict(dp=chip * 2 + 1 - core)
    barrier = pltpu.get_barrier_semaphore()
    pl.semaphore_signal(barrier, 1, device_id=sibling, device_id_type=MESH)
    order = [n for pair in PRODUCTS.values() for n in pair[:2]]
    loads = {
        name: pltpu.make_async_copy(I[name], R[name], R.load.at[k]) for k, name in enumerate(order)
    }
    for name in order[:4]:
        loads[name].start()
    later = order[4:]
    R.gain[0:1] = I.gga[...]
    R.gain[1:2] = I.ggf[...]
    pl.semaphore_wait(barrier, 1)

    def to_sibling(source, target, send, recv):
        return pltpu.make_async_remote_copy(
            src_ref=source,
            dst_ref=target,
            send_sem=send,
            recv_sem=recv,
            device_id=sibling,
            device_id_type=MESH,
        )

    gain_copy = to_sibling(R.gain, R.got_gain, R.gs, R.gr)
    gain_copy.start()

    def span_copy(first, n):
        blocks = pl.ds(first, n)
        return to_sibling(R.sent.at[blocks], R.got.at[blocks], R.ss.at[first], R.rs.at[first])

    mine = pl.ds(pl.multiple_of((2 * chip + core) * share, 16), share)
    other = pl.ds(pl.multiple_of((2 * chip + 1 - core) * share, 16), share)
    base = 0
    bases = {}
    for name, (left, right, width) in PRODUCTS.items():
        turned = R["t_" + left]
        loads[left].wait()
        for r, rw in chunks(depth):
            for c, w in chunks(D):
                turned[c : c + w, r : r + rw] = R[left][r : r + rw, c : c + w].T
        loads[right].wait()
        for more in later[:2]:
            loads[more].start()
        later = later[2:]
        for first, n in spans_of(base, width):
            for i in range(first, first + n):
                c = (i - base) * CHUNK
                w = min(CHUNK, width - c)
                R.sent[i, :, 0:w] = nn(turned[other, :], R[right][:, c : c + w]).astype(BF)
            span_copy(first, n).start()
        bases[name] = base
        base += len(chunks(width))
    for name, (left, right, width) in PRODUCTS.items():
        base = bases[name]
        for first, n in spans_of(base, width):
            span_copy(first, n).wait_recv()
            for i in range(first, first + n):
                c = (i - base) * CHUNK
                w = min(CHUNK, width - c)
                total = nn(R["t_" + left][mine, :], R[right][:, c : c + w])
                O[name][:, c : c + w] = (total + R.got[i, :, 0:w].astype(F32)).astype(BF)
    gain_copy.wait()
    O.gain[...] = R.gain[...] + R.got_gain[...]
    for name, (_, _, width) in PRODUCTS.items():
        for first, n in spans_of(bases[name], width):
            span_copy(first, n).wait_send()


def run_gradients(share, operands, gga, ggf):
    depth = operands.n1.shape[0]
    order = [n for pair in PRODUCTS.values() for n in pair[:2]]
    blocks = sum(len(chunks(width)) for _, _, width in PRODUCTS.values())
    scratch = Box({n: vmem(*operands[n].shape) for n in order})
    for left, _, _ in PRODUCTS.values():
        scratch["t_" + left] = vmem(D, depth)
    scratch.update(
        sent=vmem(blocks, share, CHUNK),
        got=vmem(blocks, share, CHUNK),
        gain=vmem(2, D, dtype=F32),
        got_gain=vmem(2, D, dtype=F32),
        load=pltpu.SemaphoreType.DMA((len(order),)),
        ss=pltpu.SemaphoreType.DMA((blocks,)),
        rs=pltpu.SemaphoreType.DMA((blocks,)),
        gs=pltpu.SemaphoreType.DMA,
        gr=pltpu.SemaphoreType.DMA,
    )
    inputs = Box({n: operands[n] for n in order})
    inputs.update(gga=gga, ggf=ggf)
    shapes = {n: jax.ShapeDtypeStruct((share, w), BF) for n, (_, _, w) in PRODUCTS.items()}
    shapes.update(gain=jax.ShapeDtypeStruct((2, D), F32))
    names = [list(inputs), list(shapes), list(scratch)]
    results = pl.pallas_call(
        functools.partial(gradient_kernel, depth, share, names),
        out_shape=list(shapes.values()),
        in_specs=[HBM] * len(order) + [LOCAL] * 2,
        out_specs=[LOCAL] * len(shapes),
        scratch_shapes=list(scratch.values()),
        compiler_params=pltpu.CompilerParams(
            collective_id=1, has_side_effects=True, vmem_limit_bytes=VMEM_LIMIT
        ),
    )(*inputs.values())
    return Box(zip(shapes, results))


def finish_kernel(groups, share, names, *refs):
    I, O, R = named(names, refs)
    data = lax.axis_index("dp")
    passing = [name for name in I if name not in PRODUCTS and name in O]
    passed_in = [
        pltpu.make_async_copy(I[name], R["i_" + name], R.pass_sem.at[2 * k])
        for k, name in enumerate(passing)
    ]
    passed_out = [
        pltpu.make_async_copy(R["i_" + name], O[name], R.pass_sem.at[2 * k + 1])
        for k, name in enumerate(passing)
    ]
    loads, stores = [], []
    for name, (_, _, width) in PRODUCTS.items():
        for c, w in chunks(width, FF):
            k = len(loads)
            source, target = I[name].at[:, c : c + w], O[name].at[:, c : c + w]
            place = R["o_" + name].at[:, c : c + w]
            if name == TURNED:
                target, place = O[name], R["o_" + name]
            loads.append(
                (name, c, w, pltpu.make_async_copy(source, R["i_" + name].at[:, c : c + w], R.load.at[k]))
            )
            stores.append(pltpu.make_async_copy(place, target, R.store.at[k]))
    for load in loads:
        load[3].start()
    for copy in passed_in:
        copy.start()
    for (name, c, w, load), store in zip(loads, stores):
        load.wait()
        for b, bw in chunks(w, 2 * CHUNK):
            columns = slice(c + b, c + b + bw)
            value = R["i_" + name][:, columns].astype(F32)
            if name == TURNED:
                R["o_" + name][columns, :] = value.T
            else:
                R["o_" + name][:, columns] = value
        store.start()
    for row, gain in enumerate((O.ga, O.gf)):
        value = I.gain[row : row + 1, 0:share]
        for q in range(1, groups):
            value = jnp.where(data == q, I.gain[row : row + 1, q * share : (q + 1) * share], value)
        gain[...] = value
    for arrival, copy in zip(passed_in, passed_out):
        arrival.wait()
        copy.start()
    for copy in stores + passed_out:
        copy.wait()


TURNED = "out"


def run_finish(groups, share, sums, rows):
    inputs = Box({n: sums[n] for n in PRODUCTS})
    inputs.update(rows, gain=sums.gain)
    shapes = Box()
    scratch = Box()
    for name, (_, _, width) in PRODUCTS.items():
        shape = (width, share) if name == TURNED else (share, width)
        shapes[name] = jax.ShapeDtypeStruct(shape, F32)
        scratch["i_" + name] = vmem(share, width)
        scratch["o_" + name] = vmem(*shape, dtype=F32)
    for name, value in rows.items():
        shapes[name] = jax.ShapeDtypeStruct(value.shape, BF)
        scratch["i_" + name] = vmem(*value.shape)
    shapes.ga = shapes.gf = jax.ShapeDtypeStruct((1, share), F32)
    copies = sum(len(chunks(width, FF)) for _, _, width in PRODUCTS.values())
    scratch.update(
        load=pltpu.SemaphoreType.DMA((copies,)),
        store=pltpu.SemaphoreType.DMA((copies,)),
        pass_sem=pltpu.SemaphoreType.DMA((2 * len(rows),)),
    )
    names = [list(inputs), list(shapes), list(scratch)]
    results = pl.pallas_call(
        functools.partial(finish_kernel, groups, share, names),
        out_shape=list(shapes.values()),
        in_specs=[HBM] * (len(inputs) - 1) + [LOCAL],
        out_specs=[HBM] * (len(shapes) - 2) + [LOCAL] * 2,
        scratch_shapes=list(scratch.values()),
        compiler_params=pltpu.CompilerParams(vmem_limit_bytes=VMEM_LIMIT),
    )(*inputs.values())
    return Box(zip(shapes, results))


def gradients_by_xla(groups, share, operands, rows, gga, ggf):
    data = lax.axis_index("dp")
    begin = (data // 2) * 2 * share
    swap = [(i, i ^ 1) for i in range(groups)]

    def exchange(both, axis=0):
        mine = lax.dynamic_slice_in_dim(both, (data % 2) * share, share, axis)
        other = lax.dynamic_slice_in_dim(both, (1 - data % 2) * share, share, axis)
        return mine + lax.ppermute(other.astype(BF), "dp", swap).astype(F32)

    sums = Box(rows)
    for name, (left, right, _) in PRODUCTS.items():
        part = lax.dynamic_slice_in_dim(operands[left], begin, 2 * share, 1)
        sums[name] = exchange(tn(part, operands[right]))
    sums[TURNED] = sums[TURNED].T
    sums.ga = exchange(lax.dynamic_slice_in_dim(gga, begin, 2 * share, 1), 1)
    sums.gf = exchange(lax.dynamic_slice_in_dim(ggf, begin, 2 * share, 1), 1)
    return sums


def body(tokens, cotangent, seq_counts, attn_gain, w_qkv, w_out, ffn_gain, w_gate_up, w_down):
    sections = lax.axis_size("section")
    groups = lax.axis_size("dp")
    chips = groups // 2
    own = tokens.shape[0] // ROWS
    meta = seq_counts.astype(F32).reshape(own, MICROS, 2).transpose(0, 2, 1)
    meta = jnp.pad(meta.reshape(own, 2 * MICROS), ((0, 0), (0, 8 - 2 * MICROS)))
    meta = jnp.broadcast_to(meta[:, :, None], (own, 8, TILE))
    cosl, sinl, coss, sins = rotary_tables()
    hbm_inputs = Box(tok=tokens.T, cot=cotangent.T, dnT=w_down[0].T)
    hbm_inputs.update(qkv=w_qkv[0], out=w_out[0], gu=w_gate_up[0])
    inputs = Box(meta=meta, ga=attn_gain, gf=ffn_gain)
    inputs.update(cosl=cosl, sinl=sinl, coss=coss, sins=sins)
    O = run_pipeline(sections, chips, own, hbm_inputs, inputs)
    share = D // groups
    operands = Box({n: O[n].reshape(-1, O[n].shape[-1]) for n in (*LEFT, *RIGHT)})
    rows = Box(rows_out=O.out, rows_gin=O.gin)
    if share % 16:
        sums = gradients_by_xla(groups, share, operands, rows, O.gga, O.ggf)
    else:
        sums = run_finish(groups, share, run_gradients(share, operands, O.gga, O.ggf), rows)
    return (
        sums.rows_out.T[None],
        sums.rows_gin.T[None],
        sums.ga,
        sums.qkv[None],
        sums.out[None],
        sums.gf,
        sums.gu[None],
        sums.dn.T[None],
    )


def solution(mesh):
    in_specs = (
        P("dp", None),
        P("dp", None),
        P("dp", None),
        P("section", None),
        P("section", None, None),
        P("section", None, None),
        P("section", None),
        P("section", None, None),
        P("section", None, None),
    )
    out_specs = (
        P("section", "dp", None),
        P("section", "dp", None),
        P("section", "dp"),
        P("section", "dp", None),
        P("section", None, "dp"),
        P("section", "dp"),
        P("section", "dp", None),
        P("section", None, "dp"),
    )
    return jax.shard_map(body, mesh=mesh, in_specs=in_specs, out_specs=out_specs, check_vma=False)
```

```python
import functools

import jax
import jax.numpy as jnp
import numpy as np
from jax import lax
from jax.experimental import pallas as pl
from jax.experimental.pallas import tpu as pltpu
from jax.sharding import PartitionSpec as P

HEADS = 15
KV_HEADS = 5
HEAD_DIM = 64
FF = 2560
D = 960
Q_WIDTH = 960
QKV_WIDTH = 1600
SHORT_LEN = 16
LONG_LEN = 64
EPS = 1e-05
BASE = 10000.0
NEG = -1e30


class Box(dict):
    __getattr__ = dict.__getitem__
    __setattr__ = dict.__setitem__


BF = jnp.bfloat16
F32 = jnp.float32
MICROS = 2
ROWS = MICROS * LONG_LEN
CHUNK = 256
TILE = 128
TILES = 8
K_HALF = 15
V_HALF = 20
MESH = pl.DeviceIdType.MESH
DOWN = "dnT"
HELD = 6

KEEP = dict(x=(0, 1024), mid=(1024, 1024), p=(2048, 1024), qkv=(3072, 1664))
KEEP.update(A=(4736, FF), B=(7296, FF))
KEEP_WIDTH = 9856
LEFT = dict(n1=D, mix=D, n2=D, hid=FF)
RIGHT = dict(gqkv=QKV_WIDTH, gat=D, ggu=2 * FF, gff=D)
WEIGHTS = dict(qkv=(D, QKV_WIDTH), out=(Q_WIDTH, D), gu=(D, 2 * FF), dn=(FF, D))


def nn(a, b):
    return lax.dot_general(a, b, (((1,), (0,)), ((), ())), preferred_element_type=F32)


def nt(a, b):
    return lax.dot_general(a, b, (((1,), (1,)), ((), ())), preferred_element_type=F32)


def tn(a, b):
    return lax.dot_general(a, b, (((0,), (0,)), ((), ())), preferred_element_type=F32)


def chunks(total, width=CHUNK):
    return [(c, min(width, total - c)) for c in range(0, total, width)]


def lane(rows):
    return lax.broadcasted_iota(jnp.int32, (rows, TILE), 1)


def inverse_rms(x):
    return lax.rsqrt(jnp.mean(x * x, -1, keepdims=True) + EPS)


def turn(tile):
    first = (lane(tile.shape[0]) % HEAD_DIM) < HEAD_DIM // 2
    return jnp.where(first, pltpu.roll(tile, TILE - 32, 1), pltpu.roll(tile, 32, 1))


def query_scale(column, rows):
    scale = HEAD_DIM**-0.5
    if column + TILE <= Q_WIDTH:
        return scale
    return jnp.where(lane(rows) < HEAD_DIM, scale, 1.0)


def head_pairs(ref, rows, first):
    low = lane(LONG_LEN) < HEAD_DIM
    tiles = {}
    spread = []
    for head in range(KV_HEADS):
        place = first + head
        t = place // 2
        if t not in tiles:
            width = min(TILE, QKV_WIDTH - t * TILE)
            x = ref[rows, t * TILE : t * TILE + width].astype(F32)
            if width < TILE:
                x = jnp.concatenate([x, x], 1)
            tiles[t] = (x, pltpu.roll(x, HEAD_DIM, 1))
        x, swapped = tiles[t]
        spread.append(jnp.where(low, x, swapped) if place % 2 == 0 else jnp.where(low, swapped, x))
    pairs = []
    for t in range(TILES):
        a = 2 * t // 3
        b = min((2 * t + 1) // 3, KV_HEADS - 1)
        pairs.append((spread[a] if a == b else jnp.where(low, spread[a], spread[b])).astype(BF))
    return pairs


def diagonal(ref, rows, t):
    low = lane(LONG_LEN) < HEAD_DIM
    x = ref[rows, t * TILE : (t + 1) * TILE].astype(F32)
    above = jnp.where(low, x, 0.0).astype(BF)
    below = jnp.where(low, 0.0, x).astype(BF)
    if t == TILES - 1:
        below = jnp.zeros_like(below)
    return jnp.concatenate([above, below], 0)


def micro_rows():
    return [slice(b * LONG_LEN, (b + 1) * LONG_LEN) for b in range(MICROS)]


def attention_forward(S):
    low = lane(LONG_LEN) < HEAD_DIM
    for rows in micro_rows():
        keys = head_pairs(S.qkv, rows, K_HALF)
        for t in range(TILES):
            S.e[rows, t * TILE : (t + 1) * TILE] = nt(keys[t], diagonal(S.qkv, rows, t))
    for rows in micro_rows():
        bias = S.bias[rows, :]
        for t in range(TILES):
            s = S.e[rows, t * TILE : (t + 1) * TILE] + bias
            e = jnp.exp(s - jnp.max(s, 0, keepdims=True))
            z = 1.0 / jnp.sum(e, 0, keepdims=True)
            S.p[rows, t * TILE : (t + 1) * TILE] = (e * z).astype(BF)
    for rows in micro_rows():
        values = head_pairs(S.qkv, rows, V_HALF)
        for t in range(TILES):
            o = tn(S.p[rows, t * TILE : (t + 1) * TILE], values[t])
            m = jnp.where(low, o[:LONG_LEN], o[LONG_LEN:]).astype(BF)
            width = min(TILE, Q_WIDTH - t * TILE)
            S.mix[rows, t * TILE : t * TILE + width] = m[:, :width]


def block_forward(W, S, arrived):
    h = S.h
    x = h[...]
    S.x[:, :D] = x.astype(BF)
    S.n1[...] = (x * inverse_rms(x) * W.ga[...]).astype(BF)
    arrived("qkv")
    n1 = S.n1[...]
    for c, w in chunks(QKV_WIDTH):
        o = nn(n1, W.qkv[:, c : c + w])
        for t, tw in chunks(w, TILE):
            column = c + t
            tile = o[:, t : t + tw]
            if column < Q_WIDTH + KV_HEADS * HEAD_DIM:
                tile = tile * S.cos[...] + turn(tile) * S.sin[...]
                if column < Q_WIDTH:
                    tile = tile * query_scale(column, ROWS)
            S.qkv[:, column : column + tw] = tile.astype(BF)
    attention_forward(S)
    arrived("out")
    mix = S.mix[...]
    for c, w in chunks(D):
        h[:, c : c + w] = h[:, c : c + w] + nn(mix, W.out[:, c : c + w])
    x = h[...]
    S.mid[:, :D] = x.astype(BF)
    S.n2[...] = (x * inverse_rms(x) * W.gf[...]).astype(BF)
    arrived("gu")
    n2 = S.n2[...]
    for c, w in chunks(FF):
        gate = nn(n2, W.gu[:, c : c + w])
        up = nn(n2, W.gu[:, FF + c : FF + c + w])
        sg = 1.0 / (1.0 + jnp.exp(-gate))
        act = gate * sg
        S.B[:, c : c + w] = act.astype(BF)
        S.A[:, c : c + w] = (up * sg * (1.0 + gate * (1.0 - sg))).astype(BF)
        S.hid[:, c : c + w] = (act * up).astype(BF)
    arrived("dn")
    hid = S.hid[...]
    for c, w in chunks(D):
        h[:, c : c + w] = h[:, c : c + w] + nn(hid, W.dn[:, c : c + w])


def attention_backward(S):
    low = lane(LONG_LEN) < HEAD_DIM
    for rows in micro_rows():
        values = head_pairs(S.qkv, rows, V_HALF)
        for t in range(TILES):
            S.e[rows, t * TILE : (t + 1) * TILE] = nt(values[t], diagonal(S.gm, rows, t))
    for rows in micro_rows():
        for t in range(TILES):
            gp = S.e[rows, t * TILE : (t + 1) * TILE]
            p = S.p[rows, t * TILE : (t + 1) * TILE].astype(F32)
            total = jnp.sum(gp * p, 0, keepdims=True)
            S.gs[rows, t * TILE : (t + 1) * TILE] = (p * (gp - total)).astype(BF)

    def store(rows, column, value, turned):
        if turned:
            value = value * S.cos[rows, :] - turn(value) * S.sin[rows, :]
        width = min(TILE, QKV_WIDTH - column)
        S.gqkv[rows, column : column + width] = value[:, :width].astype(BF)

    def fold(parts):
        sums = []
        for head in range(KV_HEADS):
            lower, upper = None, None
            for q in (3 * head, 3 * head + 1, 3 * head + 2):
                part = parts[q // 2]
                if q % 2 == 0:
                    lower = part if lower is None else lower + part
                else:
                    upper = part if upper is None else upper + part
            sums.append((jnp.where(low, lower, 0.0), jnp.where(low, 0.0, upper)))
        return sums

    def placed(sums, head, half):
        lower, upper = sums[head]
        if half == 0:
            return lower + pltpu.roll(upper, HEAD_DIM, 1)
        return upper + pltpu.roll(lower, HEAD_DIM, 1)

    for rows in micro_rows():
        keys = head_pairs(S.qkv, rows, K_HALF)
        grad_k, grad_v = [], []
        last = None
        for t in range(TILES):
            gs = S.gs[rows, t * TILE : (t + 1) * TILE]
            grad_k.append(nn(gs, diagonal(S.qkv, rows, t)))
            grad_v.append(
                nn(S.p[rows, t * TILE : (t + 1) * TILE], diagonal(S.gm, rows, t))
            )
            o = tn(gs, keys[t])
            grad_q = jnp.where(low, o[:LONG_LEN], o[LONG_LEN:]) * HEAD_DIM**-0.5
            if t < TILES - 1:
                store(rows, t * TILE, grad_q, True)
            else:
                last = grad_q
        k, v = fold(grad_k), fold(grad_v)
        store(rows, 896, jnp.where(low, last, placed(k, 0, 1)), True)
        store(rows, 1024, placed(k, 1, 0) + placed(k, 2, 1), True)
        store(rows, 1152, placed(k, 3, 0) + placed(k, 4, 1), True)
        store(rows, 1280, placed(v, 0, 0) + placed(v, 1, 1), False)
        store(rows, 1408, placed(v, 2, 0) + placed(v, 3, 1), False)
        store(rows, 1536, placed(v, 4, 0), False)


def rms_backward(x, gain, e, base):
    r = inverse_rms(x)
    scaled = e * gain
    mean = jnp.mean(x * scaled, -1, keepdims=True)
    return base + r * scaled - x * (r * r * r * mean), jnp.sum(e * x * r, 0, keepdims=True)


def block_backward(W, S, gain_attn_grad, gain_ffn_grad):
    g = S.h
    S.gff[...] = g[...].astype(BF)
    gff = S.gff[...]
    for c, w in chunks(FF):
        gh = nn(gff, W.dnT[:, c : c + w])
        S.ggu[:, c : c + w] = (gh * S.A[:, c : c + w].astype(F32)).astype(BF)
        S.ggu[:, FF + c : FF + c + w] = (gh * S.B[:, c : c + w].astype(F32)).astype(BF)
    ggu = S.ggu[...]
    for c, w in chunks(D):
        S.e[:, c : c + w] = nn(ggu, W.guT[:, c : c + w])
    new, gain = rms_backward(S.mid[:, :D].astype(F32), W.gf[...], S.e[:, :D], g[...])
    gain_ffn_grad[...] += gain
    g[...] = new
    S.gat[...] = new.astype(BF)
    gat = S.gat[...]
    for c, w in chunks(Q_WIDTH):
        S.gm[:, c : c + w] = nn(gat, W.outT[:, c : c + w]).astype(BF)
    attention_backward(S)
    gqkv = S.gqkv[...]
    for c, w in chunks(D):
        S.e[:, c : c + w] = nn(gqkv, W.qkvT[:, c : c + w])
    new, gain = rms_backward(S.x[:, :D].astype(F32), W.ga[...], S.e[:, :D], g[...])
    gain_attn_grad[...] += gain
    g[...] = new


def flip(source, target, first=0, end=None):
    depth, width = source.shape
    size = CHUNK
    whole = width // size

    def strip(start, w):
        for k, kw in chunks(depth):
            target[pl.ds(start, w), k : k + kw] = source[k : k + kw, pl.ds(start, w)].T

    def one(i, carry):
        strip(pl.multiple_of(i * size, size), size)
        return carry

    lax.fori_loop(first, whole if end is None else end, one, 0)
    if width % size:
        strip(whole * size, width % size)


def make_constants(S, meta, item, tables):
    cos_long, sin_long, cos_short, sin_short = tables
    shape = (LONG_LEN, TILE)
    slot = lax.broadcasted_iota(jnp.int32, shape, 0)
    other = lane(LONG_LEN) % LONG_LEN
    piece = (slot // SHORT_LEN).astype(F32)
    other_piece = (other // SHORT_LEN).astype(F32)
    for b, rows in enumerate(micro_rows()):
        is_long = jnp.broadcast_to(meta[item, b : b + 1, :], shape) > 0.5
        count = jnp.broadcast_to(meta[item, MICROS + b : MICROS + b + 1, :], shape)
        S.cos[rows, :] = jnp.where(is_long, cos_long[...], cos_short[...])
        S.sin[rows, :] = jnp.where(is_long, sin_long[...], sin_short[...])
        short = jnp.where(other_piece < count, 0.0, jnp.where(slot == other, 0.0, NEG))
        short = jnp.where(piece == other_piece, short, NEG)
        bias = jnp.where(is_long, 0.0, short)
        S.bias[rows, :] = jnp.where(slot <= other, bias, NEG)
        S.valid[rows, :] = jnp.where(is_long, 1.0, jnp.where(piece < count, 1.0, 0.0))


def named(names, refs):
    boxes = []
    for group in names:
        boxes.append(Box(zip(group, refs)))
        refs = refs[len(group) :]
    return boxes


def pipeline_kernel(sections, chips, own, names, *refs):
    I, O, R = named(names, refs)
    far = own * (chips - 1)
    section = lax.axis_index("section")
    data = lax.axis_index("dp")
    chip, core = data // 2, data % 2
    is_first, is_last = section == 0, section == sections - 1
    W = Box({name: R["w_" + name] for name in WEIGHTS})
    W.update({name + "T": R["t_" + name] for name in WEIGHTS})
    W.ga, W.gf = I.ga, I.gf

    crossed = lax.rem(section, 2) == 1
    sibling = chip * 2 + 1 - core
    holder = jnp.where(crossed, 1 - core, core)
    before, after = dict(section=section - 1, dp=sibling), dict(section=section + 1, dp=sibling)

    def far_chip(d):
        return lax.rem(chip - d + chips, chips) * 2

    def partner(d):
        return far_chip(d) + core

    barrier = pltpu.get_barrier_semaphore()

    @pl.when(section > 0)
    def _():
        pl.semaphore_signal(barrier, 1, device_id=before, device_id_type=MESH)

    @pl.when(section < sections - 1)
    def _():
        pl.semaphore_signal(barrier, 1, device_id=after, device_id_type=MESH)

    for d in range(1, 2 * chips):
        other = lax.rem(data + d, 2 * chips)
        pl.semaphore_signal(barrier, 1, device_id=dict(dp=other), device_id_type=MESH)

    early_names = [name for name in WEIGHTS if name in I]
    weight_names = early_names + [DOWN]
    weight_copies = {
        name: pltpu.make_async_copy(I[name], W[name], R.w_sem.at[k])
        for k, name in enumerate(weight_names)
    }
    slab = W.dn.at[0:D, 0 : own * ROWS]
    token_copy = pltpu.make_async_copy(I.tok, slab, R.t_sem)
    cotangent_copy = pltpu.make_async_copy(I.cot, slab, R.t_sem)

    @pl.when(is_first)
    def _():
        token_copy.start()

    @pl.when(is_last)
    def _():
        cotangent_copy.start()

    for name in early_names[:2]:
        weight_copies[name].start()

    def columns_of(ref, j):
        return ref.at[:, pl.ds(pl.multiple_of(j * ROWS, ROWS), ROWS)]

    O.gga[...] = jnp.zeros_like(O.gga)
    O.ggf[...] = jnp.zeros_like(O.ggf)
    R.gm[...] = jnp.zeros_like(R.gm)

    others = 2 * chips - 1
    near = jnp.where(is_first, 0, 1) + jnp.where(is_last, 0, 1)
    pl.semaphore_wait(barrier, near + others)
    for name in weight_names[2:]:
        weight_copies[name].start()

    def meta_copy(d):
        return pltpu.make_async_remote_copy(
            src_ref=I.meta,
            dst_ref=R.meta.at[pl.ds(own * d, own)],
            send_sem=R.ms_sem.at[d],
            recv_sem=R.m_sem.at[d],
            device_id=dict(dp=far_chip(d) + holder),
            device_id_type=MESH,
        )

    def next_copy(j):
        return pltpu.make_async_remote_copy(
            src_ref=R.outs.at[j],
            dst_ref=R.fin.at[j],
            send_sem=R.fs_sem.at[j],
            recv_sem=R.f_sem.at[j],
            device_id=after,
            device_id_type=MESH,
        )

    def previous_copy(j):
        return pltpu.make_async_remote_copy(
            src_ref=R.outs.at[j],
            dst_ref=R.bin.at[j],
            send_sem=R.bs_sem.at[j],
            recv_sem=R.b_sem.at[j],
            device_id=before,
            device_id_type=MESH,
        )

    def far_copy(buffer, recv, send, d, j):
        return pltpu.make_async_remote_copy(
            src_ref=buffer.at[j],
            dst_ref=buffer.at[own * d + j],
            send_sem=send.at[own * (d - 1) + j],
            recv_sem=recv.at[own * d + j],
            device_id=dict(dp=partner(d)),
            device_id_type=MESH,
        )

    def far_forward(d, j):
        return far_copy(R.fin, R.f_sem, R.fx_sem, d, j)

    def far_backward(d, j):
        return far_copy(R.bin, R.b_sem, R.bx_sem, d, j)

    class RowCopy:
        def __init__(self, target, j, sent, arrived):
            place = columns_of(target, j)
            self.here = pltpu.make_async_copy(R.flip, place, sent.at[j])
            self.there = pltpu.make_async_remote_copy(
                src_ref=R.flip,
                dst_ref=place,
                send_sem=sent.at[j],
                recv_sem=arrived.at[j],
                device_id=dict(dp=sibling),
                device_id_type=MESH,
            )

        def start(self):
            pl.when(crossed)(self.there.start)
            pl.when(jnp.logical_not(crossed))(self.here.start)

        def wait(self):
            pl.when(crossed)(self.there.wait_send)
            pl.when(jnp.logical_not(crossed))(self.here.wait)

    def out_copy(j):
        return RowCopy(O.out, j, R.o_sem, R.oa_sem)

    def grad_copy(j):
        return RowCopy(O.gin, j, R.g_sem, R.ga_sem)

    for d in range(1, chips):
        meta_copy(d).start()

    @pl.when(crossed)
    def _():
        meta_copy(0).start()

    @pl.when(jnp.logical_not(crossed))
    def _():
        R.meta[0:own] = I.meta[...]

    @pl.when(is_first)
    def _():
        token_copy.wait()
        for j in range(own):
            for c, w in chunks(D):
                R.fin[j, :, c : c + w] = slab[c : c + w, j * ROWS : (j + 1) * ROWS].T

    def cotangent_cross(j):
        return pltpu.make_async_remote_copy(
            src_ref=R.outs.at[j],
            dst_ref=R.bin.at[j],
            send_sem=R.fs_sem.at[j],
            recv_sem=R.b_sem.at[j],
            device_id=dict(dp=sibling),
            device_id_type=MESH,
        )

    @pl.when(is_last)
    def _():
        cotangent_copy.wait()
        target = R.outs if sections % 2 == 0 else R.bin
        for j in range(own):
            for c, w in chunks(D):
                target[j, :, c : c + w] = slab[c : c + w, j * ROWS : (j + 1) * ROWS].T
        if sections % 2 == 0:
            for j in range(own):
                cotangent_cross(j).start()
            for j in range(own):
                cotangent_cross(j).wait()

    @pl.when(crossed)
    def _():
        meta_copy(0).wait()

    held = is_first & (core == 1)
    early = section >= sections // 2

    def views(slot):
        S = Box(R)
        for name, (start, width) in KEEP.items():
            S[name] = R.keep.at[slot, :, start : start + width]
        for name in list(LEFT) + list(RIGHT):
            S[name] = R[name].at[slot]
        return S

    def left_copies(slot, index):
        pairs = [(R.keep.at[slot], O.keep.at[index])]
        pairs += [(R[name].at[slot], O[name].at[index]) for name in LEFT]
        return [
            pltpu.make_async_copy(a, b, R.l_sem.at[slot, k]) for k, (a, b) in enumerate(pairs)
        ]

    def right_copies(slot, index):
        return [
            pltpu.make_async_copy(R[name].at[slot], O[name].at[index], R.r_sem.at[slot, k])
            for k, name in enumerate(RIGHT)
        ]

    def keep_load(slot, index):
        return pltpu.make_async_copy(O.keep.at[index], R.keep.at[slot], R.k_sem.at[slot])

    def turn_out():
        value = R.h[...]

        for c, w in chunks(D):
            R.flip[c : c + w, :] = value[:, c : c + w].astype(BF).T

    def forward_phase(start, count, is_far):
        def step(k, carry):
            item = start + k
            make_constants(R, R.meta, item, (I.cosl, I.sinl, I.coss, I.sins))

            @pl.when(is_far)
            def _():
                d = item // own
                far_forward(d, item - own * d).wait_recv()

            @pl.when(jnp.logical_not(is_far))
            def _():
                @pl.when(jnp.logical_not(is_first))
                def _():
                    next_copy(item).wait_recv()

                for d in range(1, chips):
                    far_forward(d, item).start()

            R.h[...] = R.fin[item].astype(F32)

            def one(f, carry):
                @pl.when(k > 0)
                def _():
                    for copy in left_copies(f, 2 * (item - 1) + f):
                        copy.wait()

                fresh = jnp.logical_not(early) & (item == 0) & (f == 0)

                def arrived(name):
                    if name not in early_names:

                        @pl.when(fresh & is_first)
                        def _():
                            weight_copies[DOWN].wait()
                            flip(W.dnT, W.dn)

                    else:

                        waits = fresh & jnp.logical_not(held) if name == early_names[-1] else fresh

                        @pl.when(waits)
                        def _():
                            weight_copies[name].wait()

                block_forward(W, views(f), arrived)

                @pl.when(f == 0)
                def _():
                    for copy in left_copies(0, 2 * item):
                        copy.start()

                return carry

            lax.fori_loop(0, 2, one, 0)

            @pl.when(jnp.logical_not(is_far))
            def _():
                R.h[...] = R.h[...] * R.valid[:, 0:1]
                R.outs[item] = R.h[...].astype(BF)

                @pl.when(jnp.logical_not(is_last))
                def _():
                    next_copy(item).start()

                @pl.when(item > 0)
                def _():
                    out_copy(item - 1).wait()

                turn_out()
                out_copy(item).start()

            for copy in left_copies(1, 2 * item + 1):
                copy.start()
            return carry

        lax.fori_loop(0, count, step, 0)
        for f in range(2):
            for copy in left_copies(f, 2 * (start + count - 1) + f):
                copy.wait()

    def backward_phase(start, count, is_far):
        keep_load(1, 2 * start + 1).start()

        def step(k, carry):
            item = start + k
            make_constants(R, R.meta, item, (I.cosl, I.sinl, I.coss, I.sins))

            @pl.when(is_far)
            def _():
                d = item // own
                far_backward(d, item - own * d).wait_recv()

            @pl.when(jnp.logical_not(is_far))
            def _():
                @pl.when(jnp.logical_not(is_last))
                def _():
                    previous_copy(item).wait_recv()

                for d in range(1, chips):
                    far_backward(d, item).start()

            R.h[...] = R.bin[item].astype(F32) * R.valid[:, 0:1]

            def one(i, carry):
                f = 1 - i
                keep_load(f, 2 * item + f).wait()

                @pl.when(f == 1)
                def _():
                    keep_load(0, 2 * item).start()

                @pl.when((f == 0) & (k < count - 1))
                def _():
                    keep_load(1, 2 * item + 3).start()

                @pl.when(k > 0)
                def _():
                    for copy in right_copies(f, 2 * (item - 1) + f):
                        copy.wait()

                block_backward(W, views(f), O.gga, O.ggf)

                @pl.when(f == 1)
                def _():
                    for copy in right_copies(1, 2 * item + 1):
                        copy.start()

                return carry

            lax.fori_loop(0, 2, one, 0)

            @pl.when(jnp.logical_not(is_far))
            def _():
                @pl.when(jnp.logical_not(is_last))
                def _():
                    next_copy(item).wait_send()

                R.outs[item] = R.h[...].astype(BF)

                @pl.when(jnp.logical_not(is_first))
                def _():
                    previous_copy(item).start()

                @pl.when(item > 0)
                def _():
                    grad_copy(item - 1).wait()

                @pl.when(item == 0)
                def _():
                    out_copy(own - 1).wait()

                turn_out()
                grad_copy(item).start()

            for copy in right_copies(0, 2 * item):
                copy.start()
            return carry

        lax.fori_loop(0, count, step, 0)
        for f in range(2):
            for copy in right_copies(f, 2 * (start + count - 1) + f):
                copy.wait()

    phases = 4 if far else 2

    def phase(p, carry):
        if far:
            is_far = jnp.where(is_last, p >= 2, lax.rem(p, 2) == 1)
            is_back = jnp.where(is_last, lax.rem(p, 2) == 1, p >= 2)
            start = jnp.where(is_far, own, 0)
            count = jnp.where(is_far, far, own)
        else:
            is_far, is_back, start, count = p < 0, p == 1, 0, own

        @pl.when((p == 0) & jnp.logical_not(is_first))
        def _():
            weight_copies[DOWN].wait()
            flip(W.dnT, W.dn)

        @pl.when((p == 0) & early)
        def _():
            for name in early_names:
                weight_copies[name].wait()

        largest = early_names[-1]

        @pl.when((p == 0) & held)
        def _():
            weight_copies[largest].wait()
            flip(W[largest], W[largest + "T"], 0, HELD)

        @pl.when(jnp.where(early, p == 0, p == phases // 2))
        def _():
            for name in early_names[:-1]:
                flip(W[name], W[name + "T"])

            flip(W[largest], W[largest + "T"], jnp.where(held, HELD, 0))

        if far:

            @pl.when(is_far & jnp.logical_not(is_back))
            def _():
                for d in range(1, chips):
                    meta_copy(d).wait_recv()

        @pl.when(jnp.logical_not(is_back))
        def _():
            forward_phase(start, count, is_far)

        @pl.when(is_back)
        def _():
            backward_phase(start, count, is_far)

        return carry

    lax.fori_loop(0, phases, phase, 0)

    for j in range(own):

        @pl.when(jnp.logical_not(is_first))
        def _():
            previous_copy(j).wait_send()

        for d in range(1, chips):
            far_forward(d, j).wait_send()
            far_backward(d, j).wait_send()
    grad_copy(own - 1).wait()
    for d in range(1, chips):
        meta_copy(d).wait_send()

    @pl.when(crossed)
    def _():
        for j in range(own):
            out_copy(j).there.wait_recv()
            grad_copy(j).there.wait_recv()


def rotary_tables():
    half = HEAD_DIM // 2
    frequency = BASE ** (-2.0 * np.arange(half, dtype=np.float32) / HEAD_DIM)
    slots = np.arange(LONG_LEN)
    tables = []
    for position in (slots, slots % SHORT_LEN):
        angle = position.astype(np.float32)[:, None] * frequency[None, :].astype(np.float32)
        cos, sin = np.cos(angle), np.sin(angle)
        tables.append(np.tile(np.concatenate([cos, cos], 1), (1, 2)).astype(np.float32))
        tables.append(np.tile(np.concatenate([-sin, sin], 1), (1, 2)).astype(np.float32))
    return tables


def vmem(*shape, dtype=BF):
    return pltpu.VMEM(shape, dtype)


HBM = pl.BlockSpec(memory_space=pl.ANY)
LOCAL = pl.BlockSpec(memory_space=pltpu.VMEM)
VMEM_LIMIT = 127 * 2**19


def run_pipeline(sections, chips, own, hbm_inputs, inputs):
    items = own * chips
    scratch = Box(
        fin=vmem(items, ROWS, D),
        bin=vmem(items, ROWS, D),
        outs=vmem(own, ROWS, D),
        flip=vmem(D, ROWS),
        meta=vmem(items, 8, TILE, dtype=F32),
        keep=vmem(2, ROWS, KEEP_WIDTH),
        h=vmem(ROWS, D, dtype=F32),
        e=vmem(ROWS, 1024, dtype=F32),
        gm=vmem(ROWS, 1024),
        gs=vmem(ROWS, 1024),
        cos=vmem(ROWS, TILE, dtype=F32),
        sin=vmem(ROWS, TILE, dtype=F32),
        bias=vmem(ROWS, TILE, dtype=F32),
        valid=vmem(ROWS, TILE, dtype=F32),
    )
    for name, width in {**LEFT, **RIGHT}.items():
        scratch[name] = vmem(2, ROWS, width)
    for name, (depth, width) in WEIGHTS.items():
        scratch["w_" + name] = vmem(depth, width)
        scratch["t_" + name] = vmem(width, depth)
    far = max(1, own * (chips - 1))
    counts = dict(
        w_sem=(len(WEIGHTS),),
        f_sem=(items,),
        b_sem=(items,),
        fs_sem=(own,),
        bs_sem=(own,),
        fx_sem=(far,),
        bx_sem=(far,),
        m_sem=(chips,),
        ms_sem=(chips,),
        o_sem=(own,),
        g_sem=(own,),
        oa_sem=(own,),
        ga_sem=(own,),
        l_sem=(2, 1 + len(LEFT)),
        r_sem=(2, len(RIGHT)),
        k_sem=(2,),
    )
    for name, shape in counts.items():
        scratch[name] = pltpu.SemaphoreType.DMA(shape)
    scratch.t_sem = pltpu.SemaphoreType.DMA
    shapes = Box(out=(D, own * ROWS), gin=(D, own * ROWS))
    for name, width in {**LEFT, **RIGHT}.items():
        shapes[name] = (2 * items, ROWS, width)
    shapes.keep = (2 * items, ROWS, KEEP_WIDTH)
    out_shape = Box({name: jax.ShapeDtypeStruct(shape, BF) for name, shape in shapes.items()})
    out_shape.gga = out_shape.ggf = jax.ShapeDtypeStruct((1, D), F32)
    names = [[*hbm_inputs, *inputs], list(out_shape), list(scratch)]
    results = pl.pallas_call(
        functools.partial(pipeline_kernel, sections, chips, own, names),
        out_shape=list(out_shape.values()),
        in_specs=[HBM] * len(hbm_inputs) + [LOCAL] * len(inputs),
        out_specs=[HBM] * len(shapes) + [LOCAL] * 2,
        scratch_shapes=list(scratch.values()),
        compiler_params=pltpu.CompilerParams(
            collective_id=0, has_side_effects=True, vmem_limit_bytes=VMEM_LIMIT
        ),
    )(*hbm_inputs.values(), *inputs.values())
    return Box(zip(out_shape, results))


PRODUCTS = dict(out=(*"gat mix".split(), Q_WIDTH), qkv=(*"n1 gqkv".split(), QKV_WIDTH))
PRODUCTS.update(dn=(*"gff hid".split(), FF), gu=(*"n2 ggu".split(), 2 * FF))
SPAN = 10


def spans_of(base, width):
    return [(base + i, n) for i, n in chunks(len(chunks(width)), SPAN)]


def gradient_kernel(depth, share, names, *refs):
    I, O, R = named(names, refs)
    data = lax.axis_index("dp")
    chip, core = data // 2, data % 2
    sibling = dict(dp=chip * 2 + 1 - core)
    barrier = pltpu.get_barrier_semaphore()
    pl.semaphore_signal(barrier, 1, device_id=sibling, device_id_type=MESH)
    order = [n for pair in PRODUCTS.values() for n in pair[:2]]
    loads = {
        name: pltpu.make_async_copy(I[name], R[name], R.load.at[k]) for k, name in enumerate(order)
    }
    for name in order[:4]:
        loads[name].start()
    later = order[4:]
    R.gain[0:1] = I.gga[...]
    R.gain[1:2] = I.ggf[...]
    pl.semaphore_wait(barrier, 1)

    def to_sibling(source, target, send, recv):
        return pltpu.make_async_remote_copy(
            src_ref=source,
            dst_ref=target,
            send_sem=send,
            recv_sem=recv,
            device_id=sibling,
            device_id_type=MESH,
        )

    gain_copy = to_sibling(R.gain, R.got_gain, R.gs, R.gr)
    gain_copy.start()

    def span_copy(first, n):
        blocks = pl.ds(first, n)
        return to_sibling(R.sent.at[blocks], R.got.at[blocks], R.ss.at[first], R.rs.at[first])

    mine = pl.ds(pl.multiple_of((2 * chip + core) * share, 16), share)
    other = pl.ds(pl.multiple_of((2 * chip + 1 - core) * share, 16), share)
    base = 0
    bases = {}
    for name, (left, right, width) in PRODUCTS.items():
        turned = R["t_" + left]
        loads[left].wait()
        for r, rw in chunks(depth):
            for c, w in chunks(D):
                turned[c : c + w, r : r + rw] = R[left][r : r + rw, c : c + w].T
        loads[right].wait()
        for more in later[:2]:
            loads[more].start()
        later = later[2:]
        for first, n in spans_of(base, width):
            for i in range(first, first + n):
                c = (i - base) * CHUNK
                w = min(CHUNK, width - c)
                R.sent[i, :, 0:w] = nn(turned[other, :], R[right][:, c : c + w]).astype(BF)
            span_copy(first, n).start()
        bases[name] = base
        base += len(chunks(width))
    for name, (left, right, width) in PRODUCTS.items():
        base = bases[name]
        for first, n in spans_of(base, width):
            span_copy(first, n).wait_recv()
            for i in range(first, first + n):
                c = (i - base) * CHUNK
                w = min(CHUNK, width - c)
                total = nn(R["t_" + left][mine, :], R[right][:, c : c + w])
                O[name][:, c : c + w] = (total + R.got[i, :, 0:w].astype(F32)).astype(BF)
    gain_copy.wait()
    O.gain[...] = R.gain[...] + R.got_gain[...]
    for name, (_, _, width) in PRODUCTS.items():
        for first, n in spans_of(bases[name], width):
            span_copy(first, n).wait_send()


def run_gradients(share, operands, gga, ggf):
    depth = operands.n1.shape[0]
    order = [n for pair in PRODUCTS.values() for n in pair[:2]]
    blocks = sum(len(chunks(width)) for _, _, width in PRODUCTS.values())
    scratch = Box({n: vmem(*operands[n].shape) for n in order})
    for left, _, _ in PRODUCTS.values():
        scratch["t_" + left] = vmem(D, depth)
    scratch.update(
        sent=vmem(blocks, share, CHUNK),
        got=vmem(blocks, share, CHUNK),
        gain=vmem(2, D, dtype=F32),
        got_gain=vmem(2, D, dtype=F32),
        load=pltpu.SemaphoreType.DMA((len(order),)),
        ss=pltpu.SemaphoreType.DMA((blocks,)),
        rs=pltpu.SemaphoreType.DMA((blocks,)),
        gs=pltpu.SemaphoreType.DMA,
        gr=pltpu.SemaphoreType.DMA,
    )
    inputs = Box({n: operands[n] for n in order})
    inputs.update(gga=gga, ggf=ggf)
    shapes = {n: jax.ShapeDtypeStruct((share, w), BF) for n, (_, _, w) in PRODUCTS.items()}
    shapes.update(gain=jax.ShapeDtypeStruct((2, D), F32))
    names = [list(inputs), list(shapes), list(scratch)]
    results = pl.pallas_call(
        functools.partial(gradient_kernel, depth, share, names),
        out_shape=list(shapes.values()),
        in_specs=[HBM] * len(order) + [LOCAL] * 2,
        out_specs=[LOCAL] * len(shapes),
        scratch_shapes=list(scratch.values()),
        compiler_params=pltpu.CompilerParams(
            collective_id=1, has_side_effects=True, vmem_limit_bytes=VMEM_LIMIT
        ),
    )(*inputs.values())
    return Box(zip(shapes, results))


def finish_kernel(groups, share, names, *refs):
    I, O, R = named(names, refs)
    data = lax.axis_index("dp")
    passing = [name for name in I if name not in PRODUCTS and name in O]
    passed_in = [
        pltpu.make_async_copy(I[name], R["i_" + name], R.pass_sem.at[2 * k])
        for k, name in enumerate(passing)
    ]
    passed_out = [
        pltpu.make_async_copy(R["i_" + name], O[name], R.pass_sem.at[2 * k + 1])
        for k, name in enumerate(passing)
    ]
    loads, stores = [], []
    for name, (_, _, width) in PRODUCTS.items():
        for c, w in chunks(width, FF):
            k = len(loads)
            source, target = I[name].at[:, c : c + w], O[name].at[:, c : c + w]
            place = R["o_" + name].at[:, c : c + w]
            if name == TURNED:
                target, place = O[name], R["o_" + name]
            loads.append(
                (name, c, w, pltpu.make_async_copy(source, R["i_" + name].at[:, c : c + w], R.load.at[k]))
            )
            stores.append(pltpu.make_async_copy(place, target, R.store.at[k]))
    for load in loads:
        load[3].start()
    for copy in passed_in:
        copy.start()
    for (name, c, w, load), store in zip(loads, stores):
        load.wait()
        for b, bw in chunks(w, 2 * CHUNK):
            columns = slice(c + b, c + b + bw)
            value = R["i_" + name][:, columns].astype(F32)
            if name == TURNED:
                R["o_" + name][columns, :] = value.T
            else:
                R["o_" + name][:, columns] = value
        store.start()
    for row, gain in enumerate((O.ga, O.gf)):
        value = I.gain[row : row + 1, 0:share]
        for q in range(1, groups):
            value = jnp.where(data == q, I.gain[row : row + 1, q * share : (q + 1) * share], value)
        gain[...] = value
    for arrival, copy in zip(passed_in, passed_out):
        arrival.wait()
        copy.start()
    for copy in stores + passed_out:
        copy.wait()


TURNED = "out"


def run_finish(groups, share, sums, rows):
    inputs = Box({n: sums[n] for n in PRODUCTS})
    inputs.update(rows, gain=sums.gain)
    shapes = Box()
    scratch = Box()
    for name, (_, _, width) in PRODUCTS.items():
        shape = (width, share) if name == TURNED else (share, width)
        shapes[name] = jax.ShapeDtypeStruct(shape, F32)
        scratch["i_" + name] = vmem(share, width)
        scratch["o_" + name] = vmem(*shape, dtype=F32)
    for name, value in rows.items():
        shapes[name] = jax.ShapeDtypeStruct(value.shape, BF)
        scratch["i_" + name] = vmem(*value.shape)
    shapes.ga = shapes.gf = jax.ShapeDtypeStruct((1, share), F32)
    copies = sum(len(chunks(width, FF)) for _, _, width in PRODUCTS.values())
    scratch.update(
        load=pltpu.SemaphoreType.DMA((copies,)),
        store=pltpu.SemaphoreType.DMA((copies,)),
        pass_sem=pltpu.SemaphoreType.DMA((2 * len(rows),)),
    )
    names = [list(inputs), list(shapes), list(scratch)]
    results = pl.pallas_call(
        functools.partial(finish_kernel, groups, share, names),
        out_shape=list(shapes.values()),
        in_specs=[HBM] * (len(inputs) - 1) + [LOCAL],
        out_specs=[HBM] * (len(shapes) - 2) + [LOCAL] * 2,
        scratch_shapes=list(scratch.values()),
        compiler_params=pltpu.CompilerParams(vmem_limit_bytes=VMEM_LIMIT),
    )(*inputs.values())
    return Box(zip(shapes, results))


def gradients_by_xla(groups, share, operands, rows, gga, ggf):
    data = lax.axis_index("dp")
    begin = (data // 2) * 2 * share
    swap = [(i, i ^ 1) for i in range(groups)]

    def exchange(both, axis=0):
        mine = lax.dynamic_slice_in_dim(both, (data % 2) * share, share, axis)
        other = lax.dynamic_slice_in_dim(both, (1 - data % 2) * share, share, axis)
        return mine + lax.ppermute(other.astype(BF), "dp", swap).astype(F32)

    sums = Box(rows)
    for name, (left, right, _) in PRODUCTS.items():
        part = lax.dynamic_slice_in_dim(operands[left], begin, 2 * share, 1)
        sums[name] = exchange(tn(part, operands[right]))
    sums[TURNED] = sums[TURNED].T
    sums.ga = exchange(lax.dynamic_slice_in_dim(gga, begin, 2 * share, 1), 1)
    sums.gf = exchange(lax.dynamic_slice_in_dim(ggf, begin, 2 * share, 1), 1)
    return sums


def body(tokens, cotangent, seq_counts, attn_gain, w_qkv, w_out, ffn_gain, w_gate_up, w_down):
    sections = lax.axis_size("section")
    groups = lax.axis_size("dp")
    chips = groups // 2
    own = tokens.shape[0] // ROWS
    meta = seq_counts.astype(F32).reshape(own, MICROS, 2).transpose(0, 2, 1)
    meta = jnp.pad(meta.reshape(own, 2 * MICROS), ((0, 0), (0, 8 - 2 * MICROS)))
    meta = jnp.broadcast_to(meta[:, :, None], (own, 8, TILE))
    cosl, sinl, coss, sins = rotary_tables()
    hbm_inputs = Box(tok=tokens.T, cot=cotangent.T, dnT=w_down[0].T)
    hbm_inputs.update(qkv=w_qkv[0], out=w_out[0], gu=w_gate_up[0])
    inputs = Box(meta=meta, ga=attn_gain, gf=ffn_gain)
    inputs.update(cosl=cosl, sinl=sinl, coss=coss, sins=sins)
    O = run_pipeline(sections, chips, own, hbm_inputs, inputs)
    share = D // groups
    operands = Box({n: O[n].reshape(-1, O[n].shape[-1]) for n in (*LEFT, *RIGHT)})
    rows = Box(rows_out=O.out, rows_gin=O.gin)
    if share % 16:
        sums = gradients_by_xla(groups, share, operands, rows, O.gga, O.ggf)
    else:
        sums = run_finish(groups, share, run_gradients(share, operands, O.gga, O.ggf), rows)
    return (
        sums.rows_out.T[None],
        sums.rows_gin.T[None],
        sums.ga,
        sums.qkv[None],
        sums.out[None],
        sums.gf,
        sums.gu[None],
        sums.dn.T[None],
    )


def solution(mesh):
    in_specs = (
        P("dp", None),
        P("dp", None),
        P("dp", None),
        P("section", None),
        P("section", None, None),
        P("section", None, None),
        P("section", None),
        P("section", None, None),
        P("section", None, None),
    )
    out_specs = (
        P("section", "dp", None),
        P("section", "dp", None),
        P("section", "dp"),
        P("section", "dp", None),
        P("section", None, "dp"),
        P("section", "dp"),
        P("section", "dp", None),
        P("section", None, "dp"),
    )
    return jax.shard_map(body, mesh=mesh, in_specs=in_specs, out_specs=out_specs, check_vma=False)
```

```python
import functools

import jax
import jax.numpy as jnp
import numpy as np
from jax import lax
from jax.experimental import pallas as pl
from jax.experimental.pallas import tpu as pltpu
from jax.sharding import PartitionSpec as P

HEADS = 15
KV_HEADS = 5
HEAD_DIM = 64
FF = 2560
D = 960
Q_WIDTH = 960
QKV_WIDTH = 1600
SHORT_LEN = 16
LONG_LEN = 64
EPS = 1e-05
BASE = 10000.0
NEG = -1e30


class Box(dict):
    __getattr__ = dict.__getitem__
    __setattr__ = dict.__setitem__


BF = jnp.bfloat16
F32 = jnp.float32
MICROS = 2
ROWS = MICROS * LONG_LEN
CHUNK = 256
TILE = 128
TILES = 8
K_HALF = 15
V_HALF = 20
MESH = pl.DeviceIdType.MESH
DOWN = "dnT"
HELD = 12

KEEP = dict(x=D, mid=D, p=1024, qkv=1664, A=FF, B=FF)
LEFT = dict(n1=D, mix=D, n2=D, hid=FF)
RIGHT = dict(gqkv=QKV_WIDTH, gat=D, ggu=2 * FF, gff=D)
WEIGHTS = dict(qkv=(D, QKV_WIDTH), out=(Q_WIDTH, D), gu=(D, 2 * FF), dn=(FF, D))


def nn(a, b):
    return lax.dot_general(a, b, (((1,), (0,)), ((), ())), preferred_element_type=F32)


def nt(a, b):
    return lax.dot_general(a, b, (((1,), (1,)), ((), ())), preferred_element_type=F32)


def tn(a, b):
    return lax.dot_general(a, b, (((0,), (0,)), ((), ())), preferred_element_type=F32)


def chunks(total, width=CHUNK):
    return [(c, min(width, total - c)) for c in range(0, total, width)]


def lane(rows):
    return lax.broadcasted_iota(jnp.int32, (rows, TILE), 1)


def inverse_rms(x):
    return lax.rsqrt(jnp.mean(x * x, -1, keepdims=True) + EPS)


def turn(tile):
    first = (lane(tile.shape[0]) % HEAD_DIM) < HEAD_DIM // 2
    return jnp.where(first, pltpu.roll(tile, TILE - 32, 1), pltpu.roll(tile, 32, 1))


def query_scale(column, rows):
    scale = HEAD_DIM**-0.5
    if column + TILE <= Q_WIDTH:
        return scale
    return jnp.where(lane(rows) < HEAD_DIM, scale, 1.0)


def head_pairs(ref, rows, first):
    low = lane(LONG_LEN) < HEAD_DIM
    tiles = {}
    spread = []
    for head in range(KV_HEADS):
        place = first + head
        t = place // 2
        if t not in tiles:
            width = min(TILE, QKV_WIDTH - t * TILE)
            x = ref[rows, t * TILE : t * TILE + width].astype(F32)
            if width < TILE:
                x = jnp.concatenate([x, x], 1)
            tiles[t] = (x, pltpu.roll(x, HEAD_DIM, 1))
        x, swapped = tiles[t]
        spread.append(jnp.where(low, x, swapped) if place % 2 == 0 else jnp.where(low, swapped, x))
    pairs = []
    for t in range(TILES):
        a = 2 * t // 3
        b = min((2 * t + 1) // 3, KV_HEADS - 1)
        pairs.append((spread[a] if a == b else jnp.where(low, spread[a], spread[b])).astype(BF))
    return pairs


def diagonal(ref, rows, t):
    low = lane(LONG_LEN) < HEAD_DIM
    x = ref[rows, t * TILE : (t + 1) * TILE].astype(F32)
    above = jnp.where(low, x, 0.0).astype(BF)
    below = jnp.where(low, 0.0, x).astype(BF)
    if t == TILES - 1:
        below = jnp.zeros_like(below)
    return jnp.concatenate([above, below], 0)


def micro_rows():
    return [slice(b * LONG_LEN, (b + 1) * LONG_LEN) for b in range(MICROS)]


def attention_forward(S):
    low = lane(LONG_LEN) < HEAD_DIM
    for rows in micro_rows():
        keys = head_pairs(S.qkv, rows, K_HALF)
        for t in range(TILES):
            S.e[rows, t * TILE : (t + 1) * TILE] = nt(keys[t], diagonal(S.qkv, rows, t))
    for rows in micro_rows():
        bias = S.bias[rows, :]
        for t in range(TILES):
            s = S.e[rows, t * TILE : (t + 1) * TILE] + bias
            e = jnp.exp(s - jnp.max(s, 0, keepdims=True))
            z = 1.0 / jnp.sum(e, 0, keepdims=True)
            S.p[rows, t * TILE : (t + 1) * TILE] = (e * z).astype(BF)
    for rows in micro_rows():
        values = head_pairs(S.qkv, rows, V_HALF)
        for t in range(TILES):
            o = tn(S.p[rows, t * TILE : (t + 1) * TILE], values[t])
            m = jnp.where(low, o[:LONG_LEN], o[LONG_LEN:]).astype(BF)
            width = min(TILE, Q_WIDTH - t * TILE)
            S.mix[rows, t * TILE : t * TILE + width] = m[:, :width]


def block_forward(W, S, arrived):
    h = S.h
    x = h[...]
    S.x[:, :D] = x.astype(BF)
    S.n1[...] = (x * inverse_rms(x) * W.ga[...]).astype(BF)
    arrived("qkv")
    n1 = S.n1[...]
    for c, w in chunks(QKV_WIDTH):
        o = nn(n1, W.qkv[:, c : c + w])
        for t, tw in chunks(w, TILE):
            column = c + t
            tile = o[:, t : t + tw]
            if column < Q_WIDTH + KV_HEADS * HEAD_DIM:
                tile = tile * S.cos[...] + turn(tile) * S.sin[...]
                if column < Q_WIDTH:
                    tile = tile * query_scale(column, ROWS)
            S.qkv[:, column : column + tw] = tile.astype(BF)
    attention_forward(S)
    arrived("out")
    mix = S.mix[...]
    for c, w in chunks(D):
        h[:, c : c + w] = h[:, c : c + w] + nn(mix, W.out[:, c : c + w])
    x = h[...]
    S.mid[:, :D] = x.astype(BF)
    S.n2[...] = (x * inverse_rms(x) * W.gf[...]).astype(BF)
    arrived("gu")
    n2 = S.n2[...]
    for c, w in chunks(FF):
        gate = nn(n2, W.gu[:, c : c + w])
        up = nn(n2, W.gu[:, FF + c : FF + c + w])
        sg = 1.0 / (1.0 + jnp.exp(-gate))
        act = gate * sg
        S.B[:, c : c + w] = act.astype(BF)
        S.A[:, c : c + w] = (up * sg * (1.0 + gate * (1.0 - sg))).astype(BF)
        S.hid[:, c : c + w] = (act * up).astype(BF)
    arrived("dn")
    hid = S.hid[...]
    for c, w in chunks(D):
        h[:, c : c + w] = h[:, c : c + w] + nn(hid, W.dn[:, c : c + w])


def attention_backward(S):
    low = lane(LONG_LEN) < HEAD_DIM
    for rows in micro_rows():
        values = head_pairs(S.qkv, rows, V_HALF)
        for t in range(TILES):
            S.e[rows, t * TILE : (t + 1) * TILE] = nt(values[t], diagonal(S.gm, rows, t))
    for rows in micro_rows():
        for t in range(TILES):
            gp = S.e[rows, t * TILE : (t + 1) * TILE]
            p = S.p[rows, t * TILE : (t + 1) * TILE].astype(F32)
            total = jnp.sum(gp * p, 0, keepdims=True)
            S.gs[rows, t * TILE : (t + 1) * TILE] = (p * (gp - total)).astype(BF)

    def store(rows, column, value, turned):
        if turned:
            value = value * S.cos[rows, :] - turn(value) * S.sin[rows, :]
        width = min(TILE, QKV_WIDTH - column)
        S.gqkv[rows, column : column + width] = value[:, :width].astype(BF)

    def fold(parts):
        sums = []
        for head in range(KV_HEADS):
            lower, upper = None, None
            for q in (3 * head, 3 * head + 1, 3 * head + 2):
                part = parts[q // 2]
                if q % 2 == 0:
                    lower = part if lower is None else lower + part
                else:
                    upper = part if upper is None else upper + part
            sums.append((jnp.where(low, lower, 0.0), jnp.where(low, 0.0, upper)))
        return sums

    def placed(sums, head, half):
        lower, upper = sums[head]
        if half == 0:
            return lower + pltpu.roll(upper, HEAD_DIM, 1)
        return upper + pltpu.roll(lower, HEAD_DIM, 1)

    for rows in micro_rows():
        keys = head_pairs(S.qkv, rows, K_HALF)
        grad_k, grad_v = [], []
        last = None
        for t in range(TILES):
            gs = S.gs[rows, t * TILE : (t + 1) * TILE]
            grad_k.append(nn(gs, diagonal(S.qkv, rows, t)))
            grad_v.append(
                nn(S.p[rows, t * TILE : (t + 1) * TILE], diagonal(S.gm, rows, t))
            )
            o = tn(gs, keys[t])
            grad_q = jnp.where(low, o[:LONG_LEN], o[LONG_LEN:]) * HEAD_DIM**-0.5
            if t < TILES - 1:
                store(rows, t * TILE, grad_q, True)
            else:
                last = grad_q
        k, v = fold(grad_k), fold(grad_v)
        store(rows, 896, jnp.where(low, last, placed(k, 0, 1)), True)
        store(rows, 1024, placed(k, 1, 0) + placed(k, 2, 1), True)
        store(rows, 1152, placed(k, 3, 0) + placed(k, 4, 1), True)
        store(rows, 1280, placed(v, 0, 0) + placed(v, 1, 1), False)
        store(rows, 1408, placed(v, 2, 0) + placed(v, 3, 1), False)
        store(rows, 1536, placed(v, 4, 0), False)


def rms_backward(x, gain, e, base):
    r = inverse_rms(x)
    scaled = e * gain
    mean = jnp.mean(x * scaled, -1, keepdims=True)
    return base + r * scaled - x * (r * r * r * mean), jnp.sum(e * x * r, 0, keepdims=True)


def block_backward(W, S, gain_attn_grad, gain_ffn_grad):
    g = S.h
    S.gff[...] = g[...].astype(BF)
    gff = S.gff[...]
    for c, w in chunks(FF):
        gh = nn(gff, W.dnT[:, c : c + w])
        S.ggu[:, c : c + w] = (gh * S.A[:, c : c + w].astype(F32)).astype(BF)
        S.ggu[:, FF + c : FF + c + w] = (gh * S.B[:, c : c + w].astype(F32)).astype(BF)
    ggu = S.ggu[...]
    for c, w in chunks(D):
        S.e[:, c : c + w] = nn(ggu, W.guT[:, c : c + w])
    new, gain = rms_backward(S.mid[:, :D].astype(F32), W.gf[...], S.e[:, :D], g[...])
    gain_ffn_grad[...] += gain
    g[...] = new
    S.gat[...] = new.astype(BF)
    gat = S.gat[...]
    for c, w in chunks(Q_WIDTH):
        S.gm[:, c : c + w] = nn(gat, W.outT[:, c : c + w]).astype(BF)
    attention_backward(S)
    gqkv = S.gqkv[...]
    for c, w in chunks(D):
        S.e[:, c : c + w] = nn(gqkv, W.qkvT[:, c : c + w])
    new, gain = rms_backward(S.x[:, :D].astype(F32), W.ga[...], S.e[:, :D], g[...])
    gain_attn_grad[...] += gain
    g[...] = new


def flip(source, target, first=0, end=None):
    depth, width = source.shape
    size = CHUNK
    whole = width // size

    def strip(start, w):
        for k, kw in chunks(depth):
            target[pl.ds(start, w), k : k + kw] = source[k : k + kw, pl.ds(start, w)].T

    def one(i, carry):
        strip(pl.multiple_of(i * size, size), size)
        return carry

    lax.fori_loop(first, whole if end is None else end, one, 0)
    if width % size:
        strip(whole * size, width % size)


def make_constants(S, meta, item, tables):
    cos_long, sin_long, cos_short, sin_short = tables
    shape = (LONG_LEN, TILE)
    slot = lax.broadcasted_iota(jnp.int32, shape, 0)
    other = lane(LONG_LEN) % LONG_LEN
    piece = (slot // SHORT_LEN).astype(F32)
    other_piece = (other // SHORT_LEN).astype(F32)
    for b, rows in enumerate(micro_rows()):
        is_long = jnp.broadcast_to(meta[item, b : b + 1, :], shape) > 0.5
        count = jnp.broadcast_to(meta[item, MICROS + b : MICROS + b + 1, :], shape)
        S.cos[rows, :] = jnp.where(is_long, cos_long[...], cos_short[...])
        S.sin[rows, :] = jnp.where(is_long, sin_long[...], sin_short[...])
        short = jnp.where(other_piece < count, 0.0, jnp.where(slot == other, 0.0, NEG))
        short = jnp.where(piece == other_piece, short, NEG)
        bias = jnp.where(is_long, 0.0, short)
        S.bias[rows, :] = jnp.where(slot <= other, bias, NEG)
        S.valid[rows, :] = jnp.where(is_long, 1.0, jnp.where(piece < count, 1.0, 0.0))


def named(names, refs):
    boxes = []
    for group in names:
        boxes.append(Box(zip(group, refs)))
        refs = refs[len(group) :]
    return boxes


def pipeline_kernel(sections, chips, own, names, *refs):
    I, O, R = named(names, refs)
    far = own * (chips - 1)
    section = lax.axis_index("section")
    data = lax.axis_index("dp")
    chip, core = data // 2, data % 2
    is_first, is_last = section == 0, section == sections - 1
    W = Box({name: R["w_" + name] for name in WEIGHTS})
    W.update({name + "T": R["t_" + name] for name in WEIGHTS})
    W.ga, W.gf = I.ga, I.gf

    crossed = lax.rem(section, 2) == 1
    sibling = chip * 2 + 1 - core
    holder = jnp.where(crossed, 1 - core, core)
    before, after = dict(section=section - 1, dp=sibling), dict(section=section + 1, dp=sibling)

    def far_chip(d):
        return lax.rem(chip - d + chips, chips) * 2

    def partner(d):
        return far_chip(d) + core

    barrier = pltpu.get_barrier_semaphore()

    @pl.when(section > 0)
    def _():
        pl.semaphore_signal(barrier, 1, device_id=before, device_id_type=MESH)

    @pl.when(section < sections - 1)
    def _():
        pl.semaphore_signal(barrier, 1, device_id=after, device_id_type=MESH)

    for d in range(1, 2 * chips):
        other = lax.rem(data + d, 2 * chips)
        pl.semaphore_signal(barrier, 1, device_id=dict(dp=other), device_id_type=MESH)

    early_names = [name for name in WEIGHTS if name in I]
    weight_names = early_names + [DOWN]
    weight_copies = {
        name: pltpu.make_async_copy(I[name], W[name], R.w_sem.at[k])
        for k, name in enumerate(weight_names)
    }
    slab = W.dn.at[0:D, 0 : own * ROWS]
    token_copy = pltpu.make_async_copy(I.tok, slab, R.t_sem)
    cotangent_copy = pltpu.make_async_copy(I.cot, slab, R.t_sem)

    @pl.when(is_first)
    def _():
        token_copy.start()

    @pl.when(is_last)
    def _():
        cotangent_copy.start()

    for name in early_names[:2]:
        weight_copies[name].start()

    def columns_of(ref, j):
        return ref.at[:, pl.ds(pl.multiple_of(j * ROWS, ROWS), ROWS)]

    O.gga[...] = jnp.zeros_like(O.gga)
    O.ggf[...] = jnp.zeros_like(O.ggf)
    R.gm[...] = jnp.zeros_like(R.gm)

    others = 2 * chips - 1
    near = jnp.where(is_first, 0, 1) + jnp.where(is_last, 0, 1)

    @pl.when(is_first)
    def _():
        token_copy.wait()
        for j in range(own):
            for c, w in chunks(D):
                R.fin[j, :, c : c + w] = slab[c : c + w, j * ROWS : (j + 1) * ROWS].T

    for name in weight_names[2:]:
        weight_copies[name].start()
    pl.semaphore_wait(barrier, near + others)

    for j in range(own):
        for b in range(MICROS):
            for column in range(2):
                count = I.counts[column : column + 1, MICROS * j + b : MICROS * j + b + 1]
                row = column * MICROS + b
                R.mine[j, row : row + 1, :] = jnp.broadcast_to(count.astype(F32), (1, TILE))

    def meta_copy(d):
        return pltpu.make_async_remote_copy(
            src_ref=R.mine,
            dst_ref=R.meta.at[pl.ds(own * d, own)],
            send_sem=R.ms_sem.at[d],
            recv_sem=R.m_sem.at[d],
            device_id=dict(dp=far_chip(d) + holder),
            device_id_type=MESH,
        )

    def next_copy(j):
        return pltpu.make_async_remote_copy(
            src_ref=R.outs.at[j],
            dst_ref=R.fin.at[j],
            send_sem=R.fs_sem.at[j],
            recv_sem=R.f_sem.at[j],
            device_id=after,
            device_id_type=MESH,
        )

    def previous_copy(j):
        return pltpu.make_async_remote_copy(
            src_ref=R.outs.at[j],
            dst_ref=R.bin.at[j],
            send_sem=R.bs_sem.at[j],
            recv_sem=R.b_sem.at[j],
            device_id=before,
            device_id_type=MESH,
        )

    def far_copy(buffer, recv, send, d, j):
        return pltpu.make_async_remote_copy(
            src_ref=buffer.at[j],
            dst_ref=buffer.at[own * d + j],
            send_sem=send.at[own * (d - 1) + j],
            recv_sem=recv.at[own * d + j],
            device_id=dict(dp=partner(d)),
            device_id_type=MESH,
        )

    def far_forward(d, j):
        return far_copy(R.fin, R.f_sem, R.fx_sem, d, j)

    def far_backward(d, j):
        return far_copy(R.bin, R.b_sem, R.bx_sem, d, j)

    class RowCopy:
        def __init__(self, target, j, sent, arrived):
            place = columns_of(target, j)
            self.here = pltpu.make_async_copy(R.flip, place, sent.at[j])
            self.there = pltpu.make_async_remote_copy(
                src_ref=R.flip,
                dst_ref=place,
                send_sem=sent.at[j],
                recv_sem=arrived.at[j],
                device_id=dict(dp=sibling),
                device_id_type=MESH,
            )

        def start(self):
            pl.when(crossed)(self.there.start)
            pl.when(jnp.logical_not(crossed))(self.here.start)

        def wait(self):
            pl.when(crossed)(self.there.wait_send)
            pl.when(jnp.logical_not(crossed))(self.here.wait)

    def out_copy(j):
        return RowCopy(O.out, j, R.o_sem, R.oa_sem)

    def grad_copy(j):
        return RowCopy(O.gin, j, R.g_sem, R.ga_sem)

    for d in range(1, chips):
        meta_copy(d).start()

    @pl.when(crossed)
    def _():
        meta_copy(0).start()

    @pl.when(jnp.logical_not(crossed))
    def _():
        R.meta[0:own] = R.mine[...]

    def cotangent_cross(j):
        return pltpu.make_async_remote_copy(
            src_ref=R.outs.at[j],
            dst_ref=R.bin.at[j],
            send_sem=R.fs_sem.at[j],
            recv_sem=R.b_sem.at[j],
            device_id=dict(dp=sibling),
            device_id_type=MESH,
        )

    @pl.when(is_last)
    def _():
        cotangent_copy.wait()
        target = R.outs if sections % 2 == 0 else R.bin
        for j in range(own):
            for c, w in chunks(D):
                target[j, :, c : c + w] = slab[c : c + w, j * ROWS : (j + 1) * ROWS].T
        if sections % 2 == 0:
            for j in range(own):
                cotangent_cross(j).start()
            for j in range(own):
                cotangent_cross(j).wait()

    @pl.when(crossed)
    def _():
        meta_copy(0).wait()

    held = is_first & (core == 1)
    early = section >= sections // 2

    def views(slot):
        S = Box(R)
        for name in (*KEEP, *LEFT, *RIGHT):
            S[name] = R[name].at[slot]
        return S

    def left_copies(slot, index):
        return [
            pltpu.make_async_copy(R[name].at[slot], O[name].at[index], R.l_sem.at[slot, k])
            for k, name in enumerate((*KEEP, *LEFT))
        ]

    def right_copies(slot, index):
        return [
            pltpu.make_async_copy(R[name].at[slot], O[name].at[index], R.r_sem.at[slot, k])
            for k, name in enumerate(RIGHT)
        ]

    def keep_loads(slot, index):
        return [
            pltpu.make_async_copy(O[name].at[index], R[name].at[slot], R.k_sem.at[slot, k])
            for k, name in enumerate(KEEP)
        ]

    def turn_out():
        value = R.h[...]

        for c, w in chunks(D):
            R.flip[c : c + w, :] = value[:, c : c + w].astype(BF).T

    def forward_phase(start, count, is_far):
        def step(k, carry):
            item = start + k
            make_constants(R, R.meta, item, (I.cosl, I.sinl, I.coss, I.sins))

            @pl.when(is_far)
            def _():
                d = item // own
                far_forward(d, item - own * d).wait_recv()

            @pl.when(jnp.logical_not(is_far))
            def _():
                @pl.when(jnp.logical_not(is_first))
                def _():
                    next_copy(item).wait_recv()

                for d in range(1, chips):
                    far_forward(d, item).start()

            @pl.when(k > 0)
            def _():
                for copy in left_copies(1, 2 * item - 1):
                    copy.start()

            R.h[...] = R.fin[item].astype(F32)

            def one(f, carry):
                @pl.when(k > 0)
                def _():
                    for copy in left_copies(f, 2 * (item - 1) + f):
                        copy.wait()

                fresh = is_first & (item == 0) & (f == 0)

                def arrived(name):
                    if name in early_names[:-1]:
                        weight_copies[name].wait()
                    elif name in early_names:
                        pl.when(jnp.logical_not(held))(weight_copies[name].wait)
                    else:
                        weight_copies[DOWN].wait()
                        flip(W.dnT, W.dn)

                @pl.when(fresh)
                def _():
                    block_forward(W, views(f), arrived)

                @pl.when(jnp.logical_not(fresh))
                def _():
                    block_forward(W, views(f), lambda name: None)

                @pl.when(f == 0)
                def _():
                    for copy in left_copies(0, 2 * item):
                        copy.start()

                return carry

            lax.fori_loop(0, 2, one, 0)

            @pl.when(jnp.logical_not(is_far))
            def _():
                R.h[...] = R.h[...] * R.valid[:, 0:1]
                R.outs[item] = R.h[...].astype(BF)

                @pl.when(jnp.logical_not(is_last))
                def _():
                    next_copy(item).start()

                @pl.when(item > 0)
                def _():
                    out_copy(item - 1).wait()

                turn_out()
                out_copy(item).start()

            return carry

        lax.fori_loop(0, count, step, 0)
        for copy in left_copies(1, 2 * (start + count) - 1):
            copy.start()
        for f in range(2):
            for copy in left_copies(f, 2 * (start + count - 1) + f):
                copy.wait()

    def backward_phase(start, count, is_far):
        for copy in keep_loads(1, 2 * start + 1):
            copy.start()

        def step(k, carry):
            item = start + k
            make_constants(R, R.meta, item, (I.cosl, I.sinl, I.coss, I.sins))

            @pl.when(is_far)
            def _():
                d = item // own
                far_backward(d, item - own * d).wait_recv()

            @pl.when(jnp.logical_not(is_far))
            def _():
                @pl.when(jnp.logical_not(is_last))
                def _():
                    previous_copy(item).wait_recv()

                for d in range(1, chips):
                    far_backward(d, item).start()

            @pl.when(k > 0)
            def _():
                for copy in right_copies(0, 2 * item - 2):
                    copy.start()

            R.h[...] = R.bin[item].astype(F32) * R.valid[:, 0:1]

            def one(i, carry):
                f = 1 - i
                for copy in keep_loads(f, 2 * item + f):
                    copy.wait()

                @pl.when(f == 1)
                def _():
                    for copy in keep_loads(0, 2 * item):
                        copy.start()

                @pl.when((f == 0) & (k < count - 1))
                def _():
                    for copy in keep_loads(1, 2 * item + 3):
                        copy.start()

                @pl.when(k > 0)
                def _():
                    for copy in right_copies(f, 2 * (item - 1) + f):
                        copy.wait()

                block_backward(W, views(f), O.gga, O.ggf)

                @pl.when(f == 1)
                def _():
                    for copy in right_copies(1, 2 * item + 1):
                        copy.start()

                return carry

            lax.fori_loop(0, 2, one, 0)

            @pl.when(jnp.logical_not(is_far))
            def _():
                @pl.when(jnp.logical_not(is_last))
                def _():
                    next_copy(item).wait_send()

                R.outs[item] = R.h[...].astype(BF)

                @pl.when(jnp.logical_not(is_first))
                def _():
                    previous_copy(item).start()

                @pl.when(item > 0)
                def _():
                    grad_copy(item - 1).wait()

                @pl.when(item == 0)
                def _():
                    out_copy(own - 1).wait()

                turn_out()
                grad_copy(item).start()

            return carry

        lax.fori_loop(0, count, step, 0)
        for copy in right_copies(0, 2 * (start + count - 1)):
            copy.start()
        for f in range(2):
            for copy in right_copies(f, 2 * (start + count - 1) + f):
                copy.wait()

    phases = 4 if far else 2

    def phase(p, carry):
        if far:
            is_far = jnp.where(is_last, p >= 2, lax.rem(p, 2) == 1)
            is_back = jnp.where(is_last, lax.rem(p, 2) == 1, p >= 2)
            start = jnp.where(is_far, own, 0)
            count = jnp.where(is_far, far, own)
        else:
            is_far, is_back, start, count = p < 0, p == 1, 0, own

        @pl.when((p == 0) & jnp.logical_not(is_first))
        def _():
            weight_copies[DOWN].wait()
            flip(W.dnT, W.dn)
            for name in early_names:
                weight_copies[name].wait()

        largest = early_names[-1]

        @pl.when((p == 0) & held)
        def _():
            weight_copies[largest].wait()
            flip(W[largest], W[largest + "T"], 0, HELD)

        @pl.when(jnp.where(early, p == 0, p == phases // 2))
        def _():
            for name in early_names[:-1]:
                flip(W[name], W[name + "T"])

            flip(W[largest], W[largest + "T"], jnp.where(held, HELD, 0))

        if far:

            @pl.when(is_far & jnp.logical_not(is_back))
            def _():
                for d in range(1, chips):
                    meta_copy(d).wait_recv()

        @pl.when(jnp.logical_not(is_back))
        def _():
            forward_phase(start, count, is_far)

        @pl.when(is_back)
        def _():
            backward_phase(start, count, is_far)

        return carry

    lax.fori_loop(0, phases, phase, 0)

    for j in range(own):

        @pl.when(jnp.logical_not(is_first))
        def _():
            previous_copy(j).wait_send()

        for d in range(1, chips):
            far_forward(d, j).wait_send()
            far_backward(d, j).wait_send()
    grad_copy(own - 1).wait()
    for d in range(1, chips):
        meta_copy(d).wait_send()

    @pl.when(crossed)
    def _():
        for j in range(own):
            out_copy(j).there.wait_recv()
            grad_copy(j).there.wait_recv()


def rotary_tables():
    half = HEAD_DIM // 2
    frequency = BASE ** (-2.0 * np.arange(half, dtype=np.float32) / HEAD_DIM)
    slots = np.arange(LONG_LEN)
    tables = []
    for position in (slots, slots % SHORT_LEN):
        angle = position.astype(np.float32)[:, None] * frequency[None, :].astype(np.float32)
        cos, sin = np.cos(angle), np.sin(angle)
        tables.append(np.tile(np.concatenate([cos, cos], 1), (1, 2)).astype(np.float32))
        tables.append(np.tile(np.concatenate([-sin, sin], 1), (1, 2)).astype(np.float32))
    return tables


def vmem(*shape, dtype=BF):
    return pltpu.VMEM(shape, dtype)


HBM = pl.BlockSpec(memory_space=pl.ANY)
LOCAL = pl.BlockSpec(memory_space=pltpu.VMEM)
VMEM_LIMIT = 127 * 2**19


def run_pipeline(sections, chips, own, hbm_inputs, inputs):
    items = own * chips
    scratch = Box(
        fin=vmem(items, ROWS, D),
        bin=vmem(items, ROWS, D),
        outs=vmem(own, ROWS, D),
        flip=vmem(D, ROWS),
        meta=vmem(items, 8, TILE, dtype=F32),
        mine=vmem(own, 8, TILE, dtype=F32),
        h=vmem(ROWS, D, dtype=F32),
        e=vmem(ROWS, 1024, dtype=F32),
        gm=vmem(ROWS, 1024),
        gs=vmem(ROWS, 1024),
        cos=vmem(ROWS, TILE, dtype=F32),
        sin=vmem(ROWS, TILE, dtype=F32),
        bias=vmem(ROWS, TILE, dtype=F32),
        valid=vmem(ROWS, TILE, dtype=F32),
    )
    for name, width in {**KEEP, **LEFT, **RIGHT}.items():
        scratch[name] = vmem(2, ROWS, width)
    for name, (depth, width) in WEIGHTS.items():
        scratch["w_" + name] = vmem(depth, width)
        scratch["t_" + name] = vmem(width, depth)
    far = max(1, own * (chips - 1))
    counts = dict(
        w_sem=(len(WEIGHTS),),
        f_sem=(items,),
        b_sem=(items,),
        fs_sem=(own,),
        bs_sem=(own,),
        fx_sem=(far,),
        bx_sem=(far,),
        m_sem=(chips,),
        ms_sem=(chips,),
        o_sem=(own,),
        g_sem=(own,),
        oa_sem=(own,),
        ga_sem=(own,),
        l_sem=(2, len(KEEP) + len(LEFT)),
        r_sem=(2, len(RIGHT)),
        k_sem=(2, len(KEEP)),
    )
    for name, shape in counts.items():
        scratch[name] = pltpu.SemaphoreType.DMA(shape)
    scratch.t_sem = pltpu.SemaphoreType.DMA
    shapes = Box(out=(D, own * ROWS), gin=(D, own * ROWS))
    for name, width in {**KEEP, **LEFT, **RIGHT}.items():
        shapes[name] = (2 * items, ROWS, width)
    out_shape = Box({name: jax.ShapeDtypeStruct(shape, BF) for name, shape in shapes.items()})
    out_shape.gga = out_shape.ggf = jax.ShapeDtypeStruct((1, D), F32)
    names = [[*hbm_inputs, *inputs], list(out_shape), list(scratch)]
    results = pl.pallas_call(
        functools.partial(pipeline_kernel, sections, chips, own, names),
        out_shape=list(out_shape.values()),
        in_specs=[HBM] * len(hbm_inputs) + [LOCAL] * len(inputs),
        out_specs=[HBM] * len(shapes) + [LOCAL] * 2,
        scratch_shapes=list(scratch.values()),
        compiler_params=pltpu.CompilerParams(
            collective_id=0, has_side_effects=True, vmem_limit_bytes=VMEM_LIMIT
        ),
    )(*hbm_inputs.values(), *inputs.values())
    return Box(zip(out_shape, results))


PRODUCTS = dict(out=(*"gat mix".split(), Q_WIDTH), qkv=(*"n1 gqkv".split(), QKV_WIDTH))
PRODUCTS.update(dn=(*"gff hid".split(), FF), gu=(*"n2 ggu".split(), 2 * FF))
SPAN = 10


def spans_of(base, width):
    return [(base + i, n) for i, n in chunks(len(chunks(width)), SPAN)]


def gradient_kernel(depth, share, names, *refs):
    I, O, R = named(names, refs)
    data = lax.axis_index("dp")
    chip, core = data // 2, data % 2
    sibling = dict(dp=chip * 2 + 1 - core)
    barrier = pltpu.get_barrier_semaphore()
    pl.semaphore_signal(barrier, 1, device_id=sibling, device_id_type=MESH)
    order = [n for pair in PRODUCTS.values() for n in pair[:2]]
    loads = {
        name: pltpu.make_async_copy(I[name], R[name], R.load.at[k]) for k, name in enumerate(order)
    }
    for name in order[:4]:
        loads[name].start()
    later = order[4:]
    R.gain[0:1] = I.gga[...]
    R.gain[1:2] = I.ggf[...]
    pl.semaphore_wait(barrier, 1)

    def to_sibling(source, target, send, recv):
        return pltpu.make_async_remote_copy(
            src_ref=source,
            dst_ref=target,
            send_sem=send,
            recv_sem=recv,
            device_id=sibling,
            device_id_type=MESH,
        )

    gain_copy = to_sibling(R.gain, R.got_gain, R.gs, R.gr)
    gain_copy.start()

    def span_copy(first, n):
        blocks = pl.ds(first, n)
        return to_sibling(R.sent.at[blocks], R.got.at[blocks], R.ss.at[first], R.rs.at[first])

    mine = pl.ds(pl.multiple_of((2 * chip + core) * share, 16), share)
    other = pl.ds(pl.multiple_of((2 * chip + 1 - core) * share, 16), share)
    base = 0
    bases = {}
    for name, (left, right, width) in PRODUCTS.items():
        turned = R["t_" + left]
        loads[left].wait()
        for r, rw in chunks(depth):
            for c, w in chunks(D):
                turned[c : c + w, r : r + rw] = R[left][r : r + rw, c : c + w].T
        loads[right].wait()
        for more in later[:2]:
            loads[more].start()
        later = later[2:]
        for first, n in spans_of(base, width):
            for i in range(first, first + n):
                c = (i - base) * CHUNK
                w = min(CHUNK, width - c)
                R.sent[i, :, 0:w] = nn(turned[other, :], R[right][:, c : c + w]).astype(BF)
            span_copy(first, n).start()
        bases[name] = base
        base += len(chunks(width))
    for name, (left, right, width) in PRODUCTS.items():
        base = bases[name]
        for first, n in spans_of(base, width):
            span_copy(first, n).wait_recv()
            for i in range(first, first + n):
                c = (i - base) * CHUNK
                w = min(CHUNK, width - c)
                total = nn(R["t_" + left][mine, :], R[right][:, c : c + w])
                O[name][:, c : c + w] = (total + R.got[i, :, 0:w].astype(F32)).astype(BF)
    gain_copy.wait()
    O.gain[...] = R.gain[...] + R.got_gain[...]
    for name, (_, _, width) in PRODUCTS.items():
        for first, n in spans_of(bases[name], width):
            span_copy(first, n).wait_send()


def run_gradients(share, operands, gga, ggf):
    depth = operands.n1.shape[0]
    order = [n for pair in PRODUCTS.values() for n in pair[:2]]
    blocks = sum(len(chunks(width)) for _, _, width in PRODUCTS.values())
    scratch = Box({n: vmem(*operands[n].shape) for n in order})
    for left, _, _ in PRODUCTS.values():
        scratch["t_" + left] = vmem(D, depth)
    scratch.update(
        sent=vmem(blocks, share, CHUNK),
        got=vmem(blocks, share, CHUNK),
        gain=vmem(2, D, dtype=F32),
        got_gain=vmem(2, D, dtype=F32),
        load=pltpu.SemaphoreType.DMA((len(order),)),
        ss=pltpu.SemaphoreType.DMA((blocks,)),
        rs=pltpu.SemaphoreType.DMA((blocks,)),
        gs=pltpu.SemaphoreType.DMA,
        gr=pltpu.SemaphoreType.DMA,
    )
    inputs = Box({n: operands[n] for n in order})
    inputs.update(gga=gga, ggf=ggf)
    shapes = {n: jax.ShapeDtypeStruct((share, w), BF) for n, (_, _, w) in PRODUCTS.items()}
    shapes.update(gain=jax.ShapeDtypeStruct((2, D), F32))
    names = [list(inputs), list(shapes), list(scratch)]
    results = pl.pallas_call(
        functools.partial(gradient_kernel, depth, share, names),
        out_shape=list(shapes.values()),
        in_specs=[HBM] * len(order) + [LOCAL] * 2,
        out_specs=[LOCAL] * len(shapes),
        scratch_shapes=list(scratch.values()),
        compiler_params=pltpu.CompilerParams(
            collective_id=1, has_side_effects=True, vmem_limit_bytes=VMEM_LIMIT
        ),
    )(*inputs.values())
    return Box(zip(shapes, results))


def finish_kernel(groups, share, names, *refs):
    I, O, R = named(names, refs)
    data = lax.axis_index("dp")
    passing = [name for name in I if name not in PRODUCTS and name in O]
    passed_in = [
        pltpu.make_async_copy(I[name], R["i_" + name], R.pass_sem.at[2 * k])
        for k, name in enumerate(passing)
    ]
    passed_out = [
        pltpu.make_async_copy(R["i_" + name], O[name], R.pass_sem.at[2 * k + 1])
        for k, name in enumerate(passing)
    ]
    loads, stores = [], []
    for name, (_, _, width) in PRODUCTS.items():
        for c, w in chunks(width, FF):
            k = len(loads)
            source, target = I[name].at[:, c : c + w], O[name].at[:, c : c + w]
            place = R["o_" + name].at[:, c : c + w]
            if name == TURNED:
                target, place = O[name], R["o_" + name]
            loads.append(
                (name, c, w, pltpu.make_async_copy(source, R["i_" + name].at[:, c : c + w], R.load.at[k]))
            )
            stores.append(pltpu.make_async_copy(place, target, R.store.at[k]))
    for load in loads:
        load[3].start()
    for copy in passed_in:
        copy.start()
    for (name, c, w, load), store in zip(loads, stores):
        load.wait()
        for b, bw in chunks(w, 2 * CHUNK):
            columns = slice(c + b, c + b + bw)
            value = R["i_" + name][:, columns].astype(F32)
            if name == TURNED:
                R["o_" + name][columns, :] = value.T
            else:
                R["o_" + name][:, columns] = value
        store.start()
    for row, gain in enumerate((O.ga, O.gf)):
        value = I.gain[row : row + 1, 0:share]
        for q in range(1, groups):
            value = jnp.where(data == q, I.gain[row : row + 1, q * share : (q + 1) * share], value)
        gain[...] = value
    for arrival, copy in zip(passed_in, passed_out):
        arrival.wait()
        copy.start()
    for copy in stores + passed_out:
        copy.wait()


TURNED = "out"


def run_finish(groups, share, sums, rows):
    inputs = Box({n: sums[n] for n in PRODUCTS})
    inputs.update(rows, gain=sums.gain)
    shapes = Box()
    scratch = Box()
    for name, (_, _, width) in PRODUCTS.items():
        shape = (width, share) if name == TURNED else (share, width)
        shapes[name] = jax.ShapeDtypeStruct(shape, F32)
        scratch["i_" + name] = vmem(share, width)
        scratch["o_" + name] = vmem(*shape, dtype=F32)
    for name, value in rows.items():
        shapes[name] = jax.ShapeDtypeStruct(value.shape, BF)
        scratch["i_" + name] = vmem(*value.shape)
    shapes.ga = shapes.gf = jax.ShapeDtypeStruct((1, share), F32)
    copies = sum(len(chunks(width, FF)) for _, _, width in PRODUCTS.values())
    scratch.update(
        load=pltpu.SemaphoreType.DMA((copies,)),
        store=pltpu.SemaphoreType.DMA((copies,)),
        pass_sem=pltpu.SemaphoreType.DMA((2 * len(rows),)),
    )
    names = [list(inputs), list(shapes), list(scratch)]
    results = pl.pallas_call(
        functools.partial(finish_kernel, groups, share, names),
        out_shape=list(shapes.values()),
        in_specs=[HBM] * (len(inputs) - 1) + [LOCAL],
        out_specs=[HBM] * (len(shapes) - 2) + [LOCAL] * 2,
        scratch_shapes=list(scratch.values()),
        compiler_params=pltpu.CompilerParams(vmem_limit_bytes=VMEM_LIMIT),
    )(*inputs.values())
    return Box(zip(shapes, results))


def gradients_by_xla(groups, share, operands, rows, gga, ggf):
    data = lax.axis_index("dp")
    begin = (data // 2) * 2 * share
    swap = [(i, i ^ 1) for i in range(groups)]

    def exchange(both, axis=0):
        mine = lax.dynamic_slice_in_dim(both, (data % 2) * share, share, axis)
        other = lax.dynamic_slice_in_dim(both, (1 - data % 2) * share, share, axis)
        return mine + lax.ppermute(other.astype(BF), "dp", swap).astype(F32)

    sums = Box(rows)
    for name, (left, right, _) in PRODUCTS.items():
        part = lax.dynamic_slice_in_dim(operands[left], begin, 2 * share, 1)
        sums[name] = exchange(tn(part, operands[right]))
    sums[TURNED] = sums[TURNED].T
    sums.ga = exchange(lax.dynamic_slice_in_dim(gga, begin, 2 * share, 1), 1)
    sums.gf = exchange(lax.dynamic_slice_in_dim(ggf, begin, 2 * share, 1), 1)
    return sums


def body(tokens, cotangent, seq_counts, attn_gain, w_qkv, w_out, ffn_gain, w_gate_up, w_down):
    sections = lax.axis_size("section")
    groups = lax.axis_size("dp")
    chips = groups // 2
    own = tokens.shape[0] // ROWS
    cosl, sinl, coss, sins = rotary_tables()
    hbm_inputs = Box(tok=tokens.T, cot=cotangent.T, dnT=w_down[0].T)
    hbm_inputs.update(qkv=w_qkv[0], out=w_out[0], gu=w_gate_up[0])
    inputs = Box(counts=seq_counts.T, ga=attn_gain, gf=ffn_gain)
    inputs.update(cosl=cosl, sinl=sinl, coss=coss, sins=sins)
    O = run_pipeline(sections, chips, own, hbm_inputs, inputs)
    share = D // groups
    operands = Box({n: O[n].reshape(-1, O[n].shape[-1]) for n in (*LEFT, *RIGHT)})
    rows = Box(rows_out=O.out, rows_gin=O.gin)
    if share % 16:
        sums = gradients_by_xla(groups, share, operands, rows, O.gga, O.ggf)
    else:
        sums = run_finish(groups, share, run_gradients(share, operands, O.gga, O.ggf), rows)
    return (
        sums.rows_out.T[None],
        sums.rows_gin.T[None],
        sums.ga,
        sums.qkv[None],
        sums.out[None],
        sums.gf,
        sums.gu[None],
        sums.dn.T[None],
    )


def solution(mesh):
    in_specs = (
        P("dp", None),
        P("dp", None),
        P("dp", None),
        P("section", None),
        P("section", None, None),
        P("section", None, None),
        P("section", None),
        P("section", None, None),
        P("section", None, None),
    )
    out_specs = (
        P("section", "dp", None),
        P("section", "dp", None),
        P("section", "dp"),
        P("section", "dp", None),
        P("section", None, "dp"),
        P("section", "dp"),
        P("section", "dp", None),
        P("section", None, "dp"),
    )
    return jax.shard_map(body, mesh=mesh, in_specs=in_specs, out_specs=out_specs, check_vma=False)
```

```python
import functools

import jax
import jax.numpy as jnp
import numpy as np
from jax import lax
from jax.experimental import pallas as pl
from jax.experimental.pallas import tpu as pltpu
from jax.sharding import PartitionSpec as P

HEADS = 15
KV_HEADS = 5
HEAD_DIM = 64
FF = 2560
D = 960
Q_WIDTH = 960
QKV_WIDTH = 1600
SHORT_LEN = 16
LONG_LEN = 64
EPS = 1e-05
BASE = 10000.0
NEG = -1e30


class Box(dict):
    __getattr__ = dict.__getitem__
    __setattr__ = dict.__setitem__


BF = jnp.bfloat16
F32 = jnp.float32
MICROS = 2
ROWS = MICROS * LONG_LEN
CHUNK = 256
TILE = 128
TILES = 8
K_HALF = 15
V_HALF = 20
MESH = pl.DeviceIdType.MESH
DOWN = "dnT"
HELD = 9

KEEP = dict(x=D, mid=D, p=1024, qkv=1664, A=FF, B=FF)
LEFT = dict(n1=D, mix=D, n2=D, hid=FF)
RIGHT = dict(gqkv=QKV_WIDTH, gat=D, ggu=2 * FF, gff=D)
WEIGHTS = dict(qkv=(D, QKV_WIDTH), out=(Q_WIDTH, D), gu=(D, 2 * FF), dn=(FF, D))


def nn(a, b):
    return lax.dot_general(a, b, (((1,), (0,)), ((), ())), preferred_element_type=F32)


def nt(a, b):
    return lax.dot_general(a, b, (((1,), (1,)), ((), ())), preferred_element_type=F32)


def tn(a, b):
    return lax.dot_general(a, b, (((0,), (0,)), ((), ())), preferred_element_type=F32)


def chunks(total, width=CHUNK):
    return [(c, min(width, total - c)) for c in range(0, total, width)]


def lane(rows):
    return lax.broadcasted_iota(jnp.int32, (rows, TILE), 1)


def inverse_rms(x):
    return lax.rsqrt(jnp.mean(x * x, -1, keepdims=True) + EPS)


def turn(tile):
    first = (lane(tile.shape[0]) % HEAD_DIM) < HEAD_DIM // 2
    return jnp.where(first, pltpu.roll(tile, TILE - 32, 1), pltpu.roll(tile, 32, 1))


def query_scale(column, rows):
    scale = HEAD_DIM**-0.5
    if column + TILE <= Q_WIDTH:
        return scale
    return jnp.where(lane(rows) < HEAD_DIM, scale, 1.0)


def head_pairs(ref, rows, first):
    low = lane(LONG_LEN) < HEAD_DIM
    tiles = {}
    spread = []
    for head in range(KV_HEADS):
        place = first + head
        t = place // 2
        if t not in tiles:
            width = min(TILE, QKV_WIDTH - t * TILE)
            x = ref[rows, t * TILE : t * TILE + width].astype(F32)
            if width < TILE:
                x = jnp.concatenate([x, x], 1)
            tiles[t] = (x, pltpu.roll(x, HEAD_DIM, 1))
        x, swapped = tiles[t]
        spread.append(jnp.where(low, x, swapped) if place % 2 == 0 else jnp.where(low, swapped, x))
    pairs = []
    for t in range(TILES):
        a = 2 * t // 3
        b = min((2 * t + 1) // 3, KV_HEADS - 1)
        pairs.append((spread[a] if a == b else jnp.where(low, spread[a], spread[b])).astype(BF))
    return pairs


def diagonal(ref, rows, t):
    low = lane(LONG_LEN) < HEAD_DIM
    x = ref[rows, t * TILE : (t + 1) * TILE].astype(F32)
    above = jnp.where(low, x, 0.0).astype(BF)
    below = jnp.where(low, 0.0, x).astype(BF)
    if t == TILES - 1:
        below = jnp.zeros_like(below)
    return jnp.concatenate([above, below], 0)


def micro_rows():
    return [slice(b * LONG_LEN, (b + 1) * LONG_LEN) for b in range(MICROS)]


def attention_forward(S):
    low = lane(LONG_LEN) < HEAD_DIM
    for rows in micro_rows():
        keys = head_pairs(S.qkv, rows, K_HALF)
        for t in range(TILES):
            S.e[rows, t * TILE : (t + 1) * TILE] = nt(keys[t], diagonal(S.qkv, rows, t))
    for rows in micro_rows():
        bias = S.bias[rows, :]
        for t in range(TILES):
            s = S.e[rows, t * TILE : (t + 1) * TILE] + bias
            e = jnp.exp(s - jnp.max(s, 0, keepdims=True))
            z = 1.0 / jnp.sum(e, 0, keepdims=True)
            S.p[rows, t * TILE : (t + 1) * TILE] = (e * z).astype(BF)
    for rows in micro_rows():
        values = head_pairs(S.qkv, rows, V_HALF)
        for t in range(TILES):
            o = tn(S.p[rows, t * TILE : (t + 1) * TILE], values[t])
            m = jnp.where(low, o[:LONG_LEN], o[LONG_LEN:]).astype(BF)
            width = min(TILE, Q_WIDTH - t * TILE)
            S.mix[rows, t * TILE : t * TILE + width] = m[:, :width]


def block_forward(W, S, arrived):
    h = S.h
    x = h[...]
    S.x[:, :D] = x.astype(BF)
    S.n1[...] = (x * inverse_rms(x) * W.ga[...]).astype(BF)
    arrived("qkv")
    n1 = S.n1[...]
    for c, w in chunks(QKV_WIDTH):
        o = nn(n1, W.qkv[:, c : c + w])
        for t, tw in chunks(w, TILE):
            column = c + t
            tile = o[:, t : t + tw]
            if column < Q_WIDTH + KV_HEADS * HEAD_DIM:
                tile = tile * S.cos[...] + turn(tile) * S.sin[...]
                if column < Q_WIDTH:
                    tile = tile * query_scale(column, ROWS)
            S.qkv[:, column : column + tw] = tile.astype(BF)
    attention_forward(S)
    arrived("out")
    mix = S.mix[...]
    for c, w in chunks(D):
        h[:, c : c + w] = h[:, c : c + w] + nn(mix, W.out[:, c : c + w])
    x = h[...]
    S.mid[:, :D] = x.astype(BF)
    S.n2[...] = (x * inverse_rms(x) * W.gf[...]).astype(BF)
    arrived("gu")
    n2 = S.n2[...]
    for c, w in chunks(FF):
        gate = nn(n2, W.gu[:, c : c + w])
        up = nn(n2, W.gu[:, FF + c : FF + c + w])
        sg = 1.0 / (1.0 + jnp.exp(-gate))
        act = gate * sg
        S.B[:, c : c + w] = act.astype(BF)
        S.A[:, c : c + w] = (up * sg * (1.0 + gate * (1.0 - sg))).astype(BF)
        S.hid[:, c : c + w] = (act * up).astype(BF)
    arrived("dn")
    hid = S.hid[...]
    for c, w in chunks(D):
        h[:, c : c + w] = h[:, c : c + w] + nn(hid, W.dn[:, c : c + w])


def attention_backward(S):
    low = lane(LONG_LEN) < HEAD_DIM
    for rows in micro_rows():
        values = head_pairs(S.qkv, rows, V_HALF)
        for t in range(TILES):
            S.e[rows, t * TILE : (t + 1) * TILE] = nt(values[t], diagonal(S.gm, rows, t))
    for rows in micro_rows():
        for t in range(TILES):
            gp = S.e[rows, t * TILE : (t + 1) * TILE]
            p = S.p[rows, t * TILE : (t + 1) * TILE].astype(F32)
            total = jnp.sum(gp * p, 0, keepdims=True)
            S.gs[rows, t * TILE : (t + 1) * TILE] = (p * (gp - total)).astype(BF)

    def store(rows, column, value, turned):
        if turned:
            value = value * S.cos[rows, :] - turn(value) * S.sin[rows, :]
        width = min(TILE, QKV_WIDTH - column)
        S.gqkv[rows, column : column + width] = value[:, :width].astype(BF)

    def fold(parts):
        sums = []
        for head in range(KV_HEADS):
            lower, upper = None, None
            for q in (3 * head, 3 * head + 1, 3 * head + 2):
                part = parts[q // 2]
                if q % 2 == 0:
                    lower = part if lower is None else lower + part
                else:
                    upper = part if upper is None else upper + part
            sums.append((jnp.where(low, lower, 0.0), jnp.where(low, 0.0, upper)))
        return sums

    def placed(sums, head, half):
        lower, upper = sums[head]
        if half == 0:
            return lower + pltpu.roll(upper, HEAD_DIM, 1)
        return upper + pltpu.roll(lower, HEAD_DIM, 1)

    for rows in micro_rows():
        keys = head_pairs(S.qkv, rows, K_HALF)
        grad_k, grad_v = [], []
        last = None
        for t in range(TILES):
            gs = S.gs[rows, t * TILE : (t + 1) * TILE]
            grad_k.append(nn(gs, diagonal(S.qkv, rows, t)))
            grad_v.append(
                nn(S.p[rows, t * TILE : (t + 1) * TILE], diagonal(S.gm, rows, t))
            )
            o = tn(gs, keys[t])
            grad_q = jnp.where(low, o[:LONG_LEN], o[LONG_LEN:]) * HEAD_DIM**-0.5
            if t < TILES - 1:
                store(rows, t * TILE, grad_q, True)
            else:
                last = grad_q
        k, v = fold(grad_k), fold(grad_v)
        store(rows, 896, jnp.where(low, last, placed(k, 0, 1)), True)
        store(rows, 1024, placed(k, 1, 0) + placed(k, 2, 1), True)
        store(rows, 1152, placed(k, 3, 0) + placed(k, 4, 1), True)
        store(rows, 1280, placed(v, 0, 0) + placed(v, 1, 1), False)
        store(rows, 1408, placed(v, 2, 0) + placed(v, 3, 1), False)
        store(rows, 1536, placed(v, 4, 0), False)


def rms_backward(x, gain, e, base):
    r = inverse_rms(x)
    scaled = e * gain
    mean = jnp.mean(x * scaled, -1, keepdims=True)
    return base + r * scaled - x * (r * r * r * mean), jnp.sum(e * x * r, 0, keepdims=True)


def block_backward(W, S, gain_attn_grad, gain_ffn_grad):
    g = S.h
    S.gff[...] = g[...].astype(BF)
    gff = S.gff[...]
    for c, w in chunks(FF):
        gh = nn(gff, W.dnT[:, c : c + w])
        S.ggu[:, c : c + w] = (gh * S.A[:, c : c + w].astype(F32)).astype(BF)
        S.ggu[:, FF + c : FF + c + w] = (gh * S.B[:, c : c + w].astype(F32)).astype(BF)
    ggu = S.ggu[...]
    for c, w in chunks(D):
        S.e[:, c : c + w] = nn(ggu, W.guT[:, c : c + w])
    new, gain = rms_backward(S.mid[:, :D].astype(F32), W.gf[...], S.e[:, :D], g[...])
    gain_ffn_grad[...] += gain
    g[...] = new
    S.gat[...] = new.astype(BF)
    gat = S.gat[...]
    for c, w in chunks(Q_WIDTH):
        S.gm[:, c : c + w] = nn(gat, W.outT[:, c : c + w]).astype(BF)
    attention_backward(S)
    gqkv = S.gqkv[...]
    for c, w in chunks(D):
        S.e[:, c : c + w] = nn(gqkv, W.qkvT[:, c : c + w])
    new, gain = rms_backward(S.x[:, :D].astype(F32), W.ga[...], S.e[:, :D], g[...])
    gain_attn_grad[...] += gain
    g[...] = new


def flip(source, target, first=0, end=None):
    depth, width = source.shape
    size = CHUNK
    whole = width // size

    def strip(start, w):
        for k, kw in chunks(depth):
            target[pl.ds(start, w), k : k + kw] = source[k : k + kw, pl.ds(start, w)].T

    def one(i, carry):
        strip(pl.multiple_of(i * size, size), size)
        return carry

    lax.fori_loop(first, whole if end is None else end, one, 0)
    if width % size:
        strip(whole * size, width % size)


def make_constants(S, meta, item, tables):
    cos_long, sin_long, cos_short, sin_short = tables
    shape = (LONG_LEN, TILE)
    slot = lax.broadcasted_iota(jnp.int32, shape, 0)
    other = lane(LONG_LEN) % LONG_LEN
    piece = (slot // SHORT_LEN).astype(F32)
    other_piece = (other // SHORT_LEN).astype(F32)
    for b, rows in enumerate(micro_rows()):
        is_long = jnp.broadcast_to(meta[item, b : b + 1, :], shape) > 0.5
        count = jnp.broadcast_to(meta[item, MICROS + b : MICROS + b + 1, :], shape)
        S.cos[rows, :] = jnp.where(is_long, cos_long[...], cos_short[...])
        S.sin[rows, :] = jnp.where(is_long, sin_long[...], sin_short[...])
        short = jnp.where(other_piece < count, 0.0, jnp.where(slot == other, 0.0, NEG))
        short = jnp.where(piece == other_piece, short, NEG)
        bias = jnp.where(is_long, 0.0, short)
        S.bias[rows, :] = jnp.where(slot <= other, bias, NEG)
        S.valid[rows, :] = jnp.where(is_long, 1.0, jnp.where(piece < count, 1.0, 0.0))


def named(names, refs):
    boxes = []
    for group in names:
        boxes.append(Box(zip(group, refs)))
        refs = refs[len(group) :]
    return boxes


def pipeline_kernel(sections, chips, own, names, *refs):
    I, O, R = named(names, refs)
    far = own * (chips - 1)
    section = lax.axis_index("section")
    data = lax.axis_index("dp")
    chip, core = data // 2, data % 2
    is_first, is_last = section == 0, section == sections - 1
    W = Box({name: R["w_" + name] for name in WEIGHTS})
    W.update({name + "T": R["t_" + name] for name in WEIGHTS})
    W.ga, W.gf = I.ga, I.gf

    crossed = lax.rem(section, 2) == 1
    sibling = chip * 2 + 1 - core
    holder = jnp.where(crossed, 1 - core, core)
    before, after = dict(section=section - 1, dp=sibling), dict(section=section + 1, dp=sibling)

    def far_chip(d):
        return lax.rem(chip - d + chips, chips) * 2

    def partner(d):
        return far_chip(d) + core

    barrier = pltpu.get_barrier_semaphore()

    @pl.when(section > 0)
    def _():
        pl.semaphore_signal(barrier, 1, device_id=before, device_id_type=MESH)

    @pl.when(section < sections - 1)
    def _():
        pl.semaphore_signal(barrier, 1, device_id=after, device_id_type=MESH)

    for d in range(1, 2 * chips):
        other = lax.rem(data + d, 2 * chips)
        pl.semaphore_signal(barrier, 1, device_id=dict(dp=other), device_id_type=MESH)

    early_names = [name for name in WEIGHTS if name in I]
    weight_names = early_names + [DOWN]
    weight_copies = {
        name: pltpu.make_async_copy(I[name], W[name], R.w_sem.at[k])
        for k, name in enumerate(weight_names)
    }
    slab = W.dn.at[0:D, 0 : own * ROWS]
    token_copy = pltpu.make_async_copy(I.tok, slab, R.t_sem)
    cotangent_copy = pltpu.make_async_copy(I.cot, slab, R.t_sem)

    @pl.when(is_first)
    def _():
        token_copy.start()

    @pl.when(is_last)
    def _():
        cotangent_copy.start()

    for name in early_names[:2]:
        weight_copies[name].start()

    def columns_of(ref, j):
        return ref.at[:, pl.ds(pl.multiple_of(j * ROWS, ROWS), ROWS)]

    O.gga[...] = jnp.zeros_like(O.gga)
    O.ggf[...] = jnp.zeros_like(O.ggf)
    R.gm[...] = jnp.zeros_like(R.gm)

    others = 2 * chips - 1
    near = jnp.where(is_first, 0, 1) + jnp.where(is_last, 0, 1)

    @pl.when(is_first)
    def _():
        token_copy.wait()
        for j in range(own):
            for c, w in chunks(D):
                R.fin[j, :, c : c + w] = slab[c : c + w, j * ROWS : (j + 1) * ROWS].T

    for name in weight_names[2:]:
        weight_copies[name].start()
    pl.semaphore_wait(barrier, near + others)

    for j in range(own):
        for b in range(MICROS):
            for column in range(2):
                count = I.counts[column : column + 1, MICROS * j + b : MICROS * j + b + 1]
                row = column * MICROS + b
                R.mine[j, row : row + 1, :] = jnp.broadcast_to(count.astype(F32), (1, TILE))

    def meta_copy(d):
        return pltpu.make_async_remote_copy(
            src_ref=R.mine,
            dst_ref=R.meta.at[pl.ds(own * d, own)],
            send_sem=R.ms_sem.at[d],
            recv_sem=R.m_sem.at[d],
            device_id=dict(dp=far_chip(d) + holder),
            device_id_type=MESH,
        )

    def next_copy(j):
        return pltpu.make_async_remote_copy(
            src_ref=R.outs.at[j],
            dst_ref=R.fin.at[j],
            send_sem=R.fs_sem.at[j],
            recv_sem=R.f_sem.at[j],
            device_id=after,
            device_id_type=MESH,
        )

    def previous_copy(j):
        return pltpu.make_async_remote_copy(
            src_ref=R.outs.at[j],
            dst_ref=R.bin.at[j],
            send_sem=R.bs_sem.at[j],
            recv_sem=R.b_sem.at[j],
            device_id=before,
            device_id_type=MESH,
        )

    def far_copy(buffer, recv, send, d, j):
        return pltpu.make_async_remote_copy(
            src_ref=buffer.at[j],
            dst_ref=buffer.at[own * d + j],
            send_sem=send.at[own * (d - 1) + j],
            recv_sem=recv.at[own * d + j],
            device_id=dict(dp=partner(d)),
            device_id_type=MESH,
        )

    def far_forward(d, j):
        return far_copy(R.fin, R.f_sem, R.fx_sem, d, j)

    def far_backward(d, j):
        return far_copy(R.bin, R.b_sem, R.bx_sem, d, j)

    class RowCopy:
        def __init__(self, target, j, sent, arrived):
            place = columns_of(target, j)
            self.here = pltpu.make_async_copy(R.flip, place, sent.at[j])
            self.there = pltpu.make_async_remote_copy(
                src_ref=R.flip,
                dst_ref=place,
                send_sem=sent.at[j],
                recv_sem=arrived.at[j],
                device_id=dict(dp=sibling),
                device_id_type=MESH,
            )

        def start(self):
            pl.when(crossed)(self.there.start)
            pl.when(jnp.logical_not(crossed))(self.here.start)

        def wait(self):
            pl.when(crossed)(self.there.wait_send)
            pl.when(jnp.logical_not(crossed))(self.here.wait)

    def out_copy(j):
        return RowCopy(O.out, j, R.o_sem, R.oa_sem)

    def grad_copy(j):
        return RowCopy(O.gin, j, R.g_sem, R.ga_sem)

    for d in range(1, chips):
        meta_copy(d).start()

    @pl.when(crossed)
    def _():
        meta_copy(0).start()

    @pl.when(jnp.logical_not(crossed))
    def _():
        R.meta[0:own] = R.mine[...]

    def cotangent_cross(j):
        return pltpu.make_async_remote_copy(
            src_ref=R.outs.at[j],
            dst_ref=R.bin.at[j],
            send_sem=R.fs_sem.at[j],
            recv_sem=R.b_sem.at[j],
            device_id=dict(dp=sibling),
            device_id_type=MESH,
        )

    @pl.when(is_last)
    def _():
        cotangent_copy.wait()
        target = R.outs if sections % 2 == 0 else R.bin
        for j in range(own):
            for c, w in chunks(D):
                target[j, :, c : c + w] = slab[c : c + w, j * ROWS : (j + 1) * ROWS].T
        if sections % 2 == 0:
            for j in range(own):
                cotangent_cross(j).start()
            for j in range(own):
                cotangent_cross(j).wait()

    @pl.when(crossed)
    def _():
        meta_copy(0).wait()

    held = is_first & (core == 1)
    early = section >= sections // 2

    def views(slot):
        S = Box(R)
        for name in (*KEEP, *LEFT, *RIGHT):
            S[name] = R[name].at[slot]
        return S

    def left_copies(slot, index):
        return [
            pltpu.make_async_copy(R[name].at[slot], O[name].at[index], R.l_sem.at[slot, k])
            for k, name in enumerate((*KEEP, *LEFT))
        ]

    def right_copies(slot, index):
        return [
            pltpu.make_async_copy(R[name].at[slot], O[name].at[index], R.r_sem.at[slot, k])
            for k, name in enumerate(RIGHT)
        ]

    def keep_loads(slot, index):
        return [
            pltpu.make_async_copy(O[name].at[index], R[name].at[slot], R.k_sem.at[slot, k])
            for k, name in enumerate(KEEP)
        ]

    def turn_out():
        value = R.h[...]

        for c, w in chunks(D):
            R.flip[c : c + w, :] = value[:, c : c + w].astype(BF).T

    def forward_phase(start, count, is_far):
        def step(k, carry):
            item = start + k
            make_constants(R, R.meta, item, (I.cosl, I.sinl, I.coss, I.sins))

            @pl.when(is_far)
            def _():
                d = item // own
                far_forward(d, item - own * d).wait_recv()

            @pl.when(jnp.logical_not(is_far))
            def _():
                @pl.when(jnp.logical_not(is_first))
                def _():
                    next_copy(item).wait_recv()

                for d in range(1, chips):
                    far_forward(d, item).start()

            @pl.when(k > 0)
            def _():
                for copy in left_copies(1, 2 * item - 1):
                    copy.start()

            R.h[...] = R.fin[item].astype(F32)

            def one(f, carry):
                @pl.when(k > 0)
                def _():
                    for copy in left_copies(f, 2 * (item - 1) + f):
                        copy.wait()

                fresh = is_first & (item == 0) & (f == 0)

                def arrived(name):
                    if name in early_names[:-1]:
                        weight_copies[name].wait()
                    elif name in early_names:
                        pl.when(jnp.logical_not(held))(weight_copies[name].wait)
                    else:
                        weight_copies[DOWN].wait()
                        flip(W.dnT, W.dn)

                @pl.when(fresh)
                def _():
                    block_forward(W, views(f), arrived)

                @pl.when(jnp.logical_not(fresh))
                def _():
                    block_forward(W, views(f), lambda name: None)

                @pl.when(f == 0)
                def _():
                    for copy in left_copies(0, 2 * item):
                        copy.start()

                return carry

            lax.fori_loop(0, 2, one, 0)

            @pl.when(jnp.logical_not(is_far))
            def _():
                R.h[...] = R.h[...] * R.valid[:, 0:1]
                R.outs[item] = R.h[...].astype(BF)

                @pl.when(jnp.logical_not(is_last))
                def _():
                    next_copy(item).start()

                @pl.when(item > 0)
                def _():
                    out_copy(item - 1).wait()

                turn_out()
                out_copy(item).start()

            return carry

        lax.fori_loop(0, count, step, 0)
        for copy in left_copies(1, 2 * (start + count) - 1):
            copy.start()
        for f in range(2):
            for copy in left_copies(f, 2 * (start + count - 1) + f):
                copy.wait()

    def backward_phase(start, count, is_far):
        for copy in keep_loads(1, 2 * start + 1):
            copy.start()

        def step(k, carry):
            item = start + k
            make_constants(R, R.meta, item, (I.cosl, I.sinl, I.coss, I.sins))

            @pl.when(is_far)
            def _():
                d = item // own
                far_backward(d, item - own * d).wait_recv()

            @pl.when(jnp.logical_not(is_far))
            def _():
                @pl.when(jnp.logical_not(is_last))
                def _():
                    previous_copy(item).wait_recv()

                for d in range(1, chips):
                    far_backward(d, item).start()

            @pl.when(k > 0)
            def _():
                for copy in right_copies(0, 2 * item - 2):
                    copy.start()

            R.h[...] = R.bin[item].astype(F32) * R.valid[:, 0:1]

            def one(i, carry):
                f = 1 - i
                for copy in keep_loads(f, 2 * item + f):
                    copy.wait()

                @pl.when(f == 1)
                def _():
                    for copy in keep_loads(0, 2 * item):
                        copy.start()

                @pl.when((f == 0) & (k < count - 1))
                def _():
                    for copy in keep_loads(1, 2 * item + 3):
                        copy.start()

                @pl.when(k > 0)
                def _():
                    for copy in right_copies(f, 2 * (item - 1) + f):
                        copy.wait()

                block_backward(W, views(f), O.gga, O.ggf)

                @pl.when(f == 1)
                def _():
                    for copy in right_copies(1, 2 * item + 1):
                        copy.start()

                return carry

            lax.fori_loop(0, 2, one, 0)

            @pl.when(jnp.logical_not(is_far))
            def _():
                @pl.when(jnp.logical_not(is_last))
                def _():
                    next_copy(item).wait_send()

                R.outs[item] = R.h[...].astype(BF)

                @pl.when(jnp.logical_not(is_first))
                def _():
                    previous_copy(item).start()

                @pl.when(item > 0)
                def _():
                    grad_copy(item - 1).wait()

                @pl.when(item == 0)
                def _():
                    out_copy(own - 1).wait()

                turn_out()
                grad_copy(item).start()

            return carry

        lax.fori_loop(0, count, step, 0)
        for copy in right_copies(0, 2 * (start + count - 1)):
            copy.start()
        for f in range(2):
            for copy in right_copies(f, 2 * (start + count - 1) + f):
                copy.wait()

    phases = 4 if far else 2

    def phase(p, carry):
        if far:
            is_far = jnp.where(is_last, p >= 2, lax.rem(p, 2) == 1)
            is_back = jnp.where(is_last, lax.rem(p, 2) == 1, p >= 2)
            start = jnp.where(is_far, own, 0)
            count = jnp.where(is_far, far, own)
        else:
            is_far, is_back, start, count = p < 0, p == 1, 0, own

        @pl.when((p == 0) & jnp.logical_not(is_first))
        def _():
            weight_copies[DOWN].wait()
            flip(W.dnT, W.dn)
            for name in early_names:
                weight_copies[name].wait()

        largest = early_names[-1]

        @pl.when((p == 0) & held)
        def _():
            weight_copies[largest].wait()
            flip(W[largest], W[largest + "T"], 0, HELD)

        @pl.when(jnp.where(early, p == 0, p == phases // 2))
        def _():
            for name in early_names[:-1]:
                flip(W[name], W[name + "T"])

            flip(W[largest], W[largest + "T"], jnp.where(held, HELD, 0))

        if far:

            @pl.when(is_far & jnp.logical_not(is_back))
            def _():
                for d in range(1, chips):
                    meta_copy(d).wait_recv()

        @pl.when(jnp.logical_not(is_back))
        def _():
            forward_phase(start, count, is_far)

        @pl.when(is_back)
        def _():
            backward_phase(start, count, is_far)

        return carry

    lax.fori_loop(0, phases, phase, 0)

    for j in range(own):

        @pl.when(jnp.logical_not(is_first))
        def _():
            previous_copy(j).wait_send()

        for d in range(1, chips):
            far_forward(d, j).wait_send()
            far_backward(d, j).wait_send()
    grad_copy(own - 1).wait()
    for d in range(1, chips):
        meta_copy(d).wait_send()

    @pl.when(crossed)
    def _():
        for j in range(own):
            out_copy(j).there.wait_recv()
            grad_copy(j).there.wait_recv()


def rotary_tables():
    half = HEAD_DIM // 2
    frequency = BASE ** (-2.0 * np.arange(half, dtype=np.float32) / HEAD_DIM)
    slots = np.arange(LONG_LEN)
    tables = []
    for position in (slots, slots % SHORT_LEN):
        angle = position.astype(np.float32)[:, None] * frequency[None, :].astype(np.float32)
        cos, sin = np.cos(angle), np.sin(angle)
        tables.append(np.tile(np.concatenate([cos, cos], 1), (1, 2)).astype(np.float32))
        tables.append(np.tile(np.concatenate([-sin, sin], 1), (1, 2)).astype(np.float32))
    return tables


def vmem(*shape, dtype=BF):
    return pltpu.VMEM(shape, dtype)


HBM = pl.BlockSpec(memory_space=pl.ANY)
LOCAL = pl.BlockSpec(memory_space=pltpu.VMEM)
VMEM_LIMIT = 127 * 2**19


def run_pipeline(sections, chips, own, hbm_inputs, inputs):
    items = own * chips
    scratch = Box(
        fin=vmem(items, ROWS, D),
        bin=vmem(items, ROWS, D),
        outs=vmem(own, ROWS, D),
        flip=vmem(D, ROWS),
        meta=vmem(items, 8, TILE, dtype=F32),
        mine=vmem(own, 8, TILE, dtype=F32),
        h=vmem(ROWS, D, dtype=F32),
        e=vmem(ROWS, 1024, dtype=F32),
        gm=vmem(ROWS, 1024),
        gs=vmem(ROWS, 1024),
        cos=vmem(ROWS, TILE, dtype=F32),
        sin=vmem(ROWS, TILE, dtype=F32),
        bias=vmem(ROWS, TILE, dtype=F32),
        valid=vmem(ROWS, TILE, dtype=F32),
    )
    for name, width in {**KEEP, **LEFT, **RIGHT}.items():
        scratch[name] = vmem(2, ROWS, width)
    for name, (depth, width) in WEIGHTS.items():
        scratch["w_" + name] = vmem(depth, width)
        scratch["t_" + name] = vmem(width, depth)
    far = max(1, own * (chips - 1))
    counts = dict(
        w_sem=(len(WEIGHTS),),
        f_sem=(items,),
        b_sem=(items,),
        fs_sem=(own,),
        bs_sem=(own,),
        fx_sem=(far,),
        bx_sem=(far,),
        m_sem=(chips,),
        ms_sem=(chips,),
        o_sem=(own,),
        g_sem=(own,),
        oa_sem=(own,),
        ga_sem=(own,),
        l_sem=(2, len(KEEP) + len(LEFT)),
        r_sem=(2, len(RIGHT)),
        k_sem=(2, len(KEEP)),
    )
    for name, shape in counts.items():
        scratch[name] = pltpu.SemaphoreType.DMA(shape)
    scratch.t_sem = pltpu.SemaphoreType.DMA
    shapes = Box(out=(D, own * ROWS), gin=(D, own * ROWS))
    for name, width in {**KEEP, **LEFT, **RIGHT}.items():
        shapes[name] = (2 * items, ROWS, width)
    out_shape = Box({name: jax.ShapeDtypeStruct(shape, BF) for name, shape in shapes.items()})
    out_shape.gga = out_shape.ggf = jax.ShapeDtypeStruct((1, D), F32)
    names = [[*hbm_inputs, *inputs], list(out_shape), list(scratch)]
    results = pl.pallas_call(
        functools.partial(pipeline_kernel, sections, chips, own, names),
        out_shape=list(out_shape.values()),
        in_specs=[HBM] * len(hbm_inputs) + [LOCAL] * len(inputs),
        out_specs=[HBM] * len(shapes) + [LOCAL] * 2,
        scratch_shapes=list(scratch.values()),
        compiler_params=pltpu.CompilerParams(
            collective_id=0, has_side_effects=True, vmem_limit_bytes=VMEM_LIMIT
        ),
    )(*hbm_inputs.values(), *inputs.values())
    return Box(zip(out_shape, results))


PRODUCTS = dict(out=(*"gat mix".split(), Q_WIDTH), qkv=(*"n1 gqkv".split(), QKV_WIDTH))
PRODUCTS.update(dn=(*"gff hid".split(), FF), gu=(*"n2 ggu".split(), 2 * FF))
SPAN = 10


def spans_of(base, width):
    return [(base + i, n) for i, n in chunks(len(chunks(width)), SPAN)]


def gradient_kernel(depth, share, names, *refs):
    I, O, R = named(names, refs)
    data = lax.axis_index("dp")
    chip, core = data // 2, data % 2
    sibling = dict(dp=chip * 2 + 1 - core)
    barrier = pltpu.get_barrier_semaphore()
    pl.semaphore_signal(barrier, 1, device_id=sibling, device_id_type=MESH)
    order = [n for pair in PRODUCTS.values() for n in pair[:2]]
    loads = {
        name: pltpu.make_async_copy(I[name], R[name], R.load.at[k]) for k, name in enumerate(order)
    }
    for name in order[:2]:
        loads[name].start()
    later = order[4:]
    R.gain[0:1] = I.gga[...]
    R.gain[1:2] = I.ggf[...]
    pl.semaphore_wait(barrier, 1)
    for name in order[2:4]:
        loads[name].start()

    def to_sibling(source, target, send, recv):
        return pltpu.make_async_remote_copy(
            src_ref=source,
            dst_ref=target,
            send_sem=send,
            recv_sem=recv,
            device_id=sibling,
            device_id_type=MESH,
        )

    gain_copy = to_sibling(R.gain, R.got_gain, R.gs, R.gr)
    gain_copy.start()

    def span_copy(first, n):
        blocks = pl.ds(first, n)
        return to_sibling(R.sent.at[blocks], R.got.at[blocks], R.ss.at[first], R.rs.at[first])

    mine = pl.ds(pl.multiple_of((2 * chip + core) * share, 16), share)
    other = pl.ds(pl.multiple_of((2 * chip + 1 - core) * share, 16), share)
    def turn_left(left):
        for r, rw in chunks(depth):
            for c, w in chunks(D):
                R["t_" + left][c : c + w, r : r + rw] = R[left][r : r + rw, c : c + w].T

    bases, writes = {}, []
    products = list(PRODUCTS.items())
    lefts = [left for left, _, _ in PRODUCTS.values()]

    def span_columns(name, first, n, width):
        c = (first - bases[name]) * CHUNK
        return slice(c, min(c + n * CHUNK, width))

    def give(name, left, right, width):
        for first, n in spans_of(bases[name], width):
            columns = span_columns(name, first, n, width)
            for i, (c, w) in enumerate(chunks(columns.stop - columns.start)):
                c += columns.start
                value = nn(R["t_" + left][other, :], R[right][:, c : c + w])
                R.sent[first + i, :, 0:w] = value.astype(BF)
            span_copy(first, n).start()

    def take(name, left, right, width):
        for first, n in spans_of(bases[name], width):
            span_copy(first, n).wait_recv()
            columns = span_columns(name, first, n, width)
            for i, (c, w) in enumerate(chunks(columns.stop - columns.start)):
                c += columns.start
                total = nn(R["t_" + left][mine, :], R[right][:, c : c + w])
                total = total + R.got[first + i, :, 0:w].astype(F32)
                R["sum_" + name][:, c : c + w] = total.astype(BF)
            place = R["sum_" + name].at[:, columns], O[name].at[:, columns]
            writes.append(pltpu.make_async_copy(*place, R.write.at[len(writes)]))
            writes[-1].start()

    base = 0
    for k, (name, (left, right, width)) in enumerate(products):
        bases[name] = base
        base += len(chunks(width))
        loads[left].wait()
        turn_left(left)
        loads[right].wait()
        for more in later[:2]:
            loads[more].start()
        later = later[2:]
        give(name, left, right, width)
        if k > 0:
            before, spec = products[k - 1]
            take(before, *spec)
    take(products[-1][0], *products[-1][1])
    gain_copy.wait()
    O.gain[...] = R.gain[...] + R.got_gain[...]
    for name, (_, _, width) in PRODUCTS.items():
        for first, n in spans_of(bases[name], width):
            span_copy(first, n).wait_send()
    for write in writes:
        write.wait()


def run_gradients(share, operands, gga, ggf):
    depth = operands.n1.shape[0]
    order = [n for pair in PRODUCTS.values() for n in pair[:2]]
    blocks = sum(len(chunks(width)) for _, _, width in PRODUCTS.values())
    scratch = Box({n: vmem(*operands[n].shape) for n in order})
    for name, (left, _, width) in PRODUCTS.items():
        scratch["t_" + left] = vmem(D, depth)
        scratch["sum_" + name] = vmem(share, width)
    scratch.update(
        sent=vmem(blocks, share, CHUNK),
        got=vmem(blocks, share, CHUNK),
        gain=vmem(2, D, dtype=F32),
        got_gain=vmem(2, D, dtype=F32),
        load=pltpu.SemaphoreType.DMA((len(order),)),
        write=pltpu.SemaphoreType.DMA((blocks,)),
        ss=pltpu.SemaphoreType.DMA((blocks,)),
        rs=pltpu.SemaphoreType.DMA((blocks,)),
        gs=pltpu.SemaphoreType.DMA,
        gr=pltpu.SemaphoreType.DMA,
    )
    inputs = Box({n: operands[n] for n in order})
    inputs.update(gga=gga, ggf=ggf)
    shapes = {n: jax.ShapeDtypeStruct((share, w), BF) for n, (_, _, w) in PRODUCTS.items()}
    shapes.update(gain=jax.ShapeDtypeStruct((2, D), F32))
    names = [list(inputs), list(shapes), list(scratch)]
    results = pl.pallas_call(
        functools.partial(gradient_kernel, depth, share, names),
        out_shape=list(shapes.values()),
        in_specs=[HBM] * len(order) + [LOCAL] * 2,
        out_specs=[HBM] * len(PRODUCTS) + [LOCAL],
        scratch_shapes=list(scratch.values()),
        compiler_params=pltpu.CompilerParams(
            collective_id=1, has_side_effects=True, vmem_limit_bytes=VMEM_LIMIT
        ),
    )(*inputs.values())
    return Box(zip(shapes, results))


def finish_kernel(groups, share, names, *refs):
    I, O, R = named(names, refs)
    data = lax.axis_index("dp")
    passing = [name for name in I if name not in PRODUCTS and name in O]
    passed_in = [
        pltpu.make_async_copy(I[name], R["i_" + name], R.pass_sem.at[2 * k])
        for k, name in enumerate(passing)
    ]
    passed_out = [
        pltpu.make_async_copy(R["i_" + name], O[name], R.pass_sem.at[2 * k + 1])
        for k, name in enumerate(passing)
    ]
    loads, stores = [], []
    for name, (_, _, width) in PRODUCTS.items():
        for c, w in chunks(width, FF):
            k = len(loads)
            source, target = I[name].at[:, c : c + w], O[name].at[:, c : c + w]
            place = R["o_" + name].at[:, c : c + w]
            if name == TURNED:
                target, place = O[name], R["o_" + name]
            loads.append(
                (name, c, w, pltpu.make_async_copy(source, R["i_" + name].at[:, c : c + w], R.load.at[k]))
            )
            stores.append(pltpu.make_async_copy(place, target, R.store.at[k]))
    for load in loads:
        load[3].start()
    for copy in passed_in:
        copy.start()
    for (name, c, w, load), store in zip(loads, stores):
        load.wait()
        for b, bw in chunks(w, 2 * CHUNK):
            columns = slice(c + b, c + b + bw)
            value = R["i_" + name][:, columns].astype(F32)
            if name == TURNED:
                R["o_" + name][columns, :] = value.T
            else:
                R["o_" + name][:, columns] = value
        store.start()
    for row, gain in enumerate((O.ga, O.gf)):
        value = I.gain[row : row + 1, 0:share]
        for q in range(1, groups):
            value = jnp.where(data == q, I.gain[row : row + 1, q * share : (q + 1) * share], value)
        gain[...] = value
    for arrival, copy in zip(passed_in, passed_out):
        arrival.wait()
        copy.start()
    for copy in stores + passed_out:
        copy.wait()


TURNED = "out"


def run_finish(groups, share, sums, rows):
    inputs = Box({n: sums[n] for n in PRODUCTS})
    inputs.update(rows, gain=sums.gain)
    shapes = Box()
    scratch = Box()
    for name, (_, _, width) in PRODUCTS.items():
        shape = (width, share) if name == TURNED else (share, width)
        shapes[name] = jax.ShapeDtypeStruct(shape, F32)
        scratch["i_" + name] = vmem(share, width)
        scratch["o_" + name] = vmem(*shape, dtype=F32)
    for name, value in rows.items():
        shapes[name] = jax.ShapeDtypeStruct(value.shape, BF)
        scratch["i_" + name] = vmem(*value.shape)
    shapes.ga = shapes.gf = jax.ShapeDtypeStruct((1, share), F32)
    copies = sum(len(chunks(width, FF)) for _, _, width in PRODUCTS.values())
    scratch.update(
        load=pltpu.SemaphoreType.DMA((copies,)),
        store=pltpu.SemaphoreType.DMA((copies,)),
        pass_sem=pltpu.SemaphoreType.DMA((2 * len(rows),)),
    )
    names = [list(inputs), list(shapes), list(scratch)]
    results = pl.pallas_call(
        functools.partial(finish_kernel, groups, share, names),
        out_shape=list(shapes.values()),
        in_specs=[HBM] * (len(inputs) - 1) + [LOCAL],
        out_specs=[HBM] * (len(shapes) - 2) + [LOCAL] * 2,
        scratch_shapes=list(scratch.values()),
        compiler_params=pltpu.CompilerParams(vmem_limit_bytes=VMEM_LIMIT),
    )(*inputs.values())
    return Box(zip(shapes, results))


def gradients_by_xla(groups, share, operands, rows, gga, ggf):
    data = lax.axis_index("dp")
    begin = (data // 2) * 2 * share
    swap = [(i, i ^ 1) for i in range(groups)]

    def exchange(both, axis=0):
        mine = lax.dynamic_slice_in_dim(both, (data % 2) * share, share, axis)
        other = lax.dynamic_slice_in_dim(both, (1 - data % 2) * share, share, axis)
        return mine + lax.ppermute(other.astype(BF), "dp", swap).astype(F32)

    sums = Box(rows)
    for name, (left, right, _) in PRODUCTS.items():
        part = lax.dynamic_slice_in_dim(operands[left], begin, 2 * share, 1)
        sums[name] = exchange(tn(part, operands[right]))
    sums[TURNED] = sums[TURNED].T
    sums.ga = exchange(lax.dynamic_slice_in_dim(gga, begin, 2 * share, 1), 1)
    sums.gf = exchange(lax.dynamic_slice_in_dim(ggf, begin, 2 * share, 1), 1)
    return sums


def body(tokens, cotangent, seq_counts, attn_gain, w_qkv, w_out, ffn_gain, w_gate_up, w_down):
    sections = lax.axis_size("section")
    groups = lax.axis_size("dp")
    chips = groups // 2
    own = tokens.shape[0] // ROWS
    cosl, sinl, coss, sins = rotary_tables()
    hbm_inputs = Box(tok=tokens.T, cot=cotangent.T, dnT=w_down[0].T)
    hbm_inputs.update(qkv=w_qkv[0], out=w_out[0], gu=w_gate_up[0])
    inputs = Box(counts=seq_counts.T, ga=attn_gain, gf=ffn_gain)
    inputs.update(cosl=cosl, sinl=sinl, coss=coss, sins=sins)
    O = run_pipeline(sections, chips, own, hbm_inputs, inputs)
    share = D // groups
    operands = Box({n: O[n].reshape(-1, O[n].shape[-1]) for n in (*LEFT, *RIGHT)})
    rows = Box(rows_out=O.out, rows_gin=O.gin)
    if share % 16:
        sums = gradients_by_xla(groups, share, operands, rows, O.gga, O.ggf)
    else:
        sums = run_finish(groups, share, run_gradients(share, operands, O.gga, O.ggf), rows)
    return (
        sums.rows_out.T[None],
        sums.rows_gin.T[None],
        sums.ga,
        sums.qkv[None],
        sums.out[None],
        sums.gf,
        sums.gu[None],
        sums.dn.T[None],
    )


def solution(mesh):
    in_specs = (
        P("dp", None),
        P("dp", None),
        P("dp", None),
        P("section", None),
        P("section", None, None),
        P("section", None, None),
        P("section", None),
        P("section", None, None),
        P("section", None, None),
    )
    out_specs = (
        P("section", "dp", None),
        P("section", "dp", None),
        P("section", "dp"),
        P("section", "dp", None),
        P("section", None, "dp"),
        P("section", "dp"),
        P("section", "dp", None),
        P("section", None, "dp"),
    )
    return jax.shard_map(body, mesh=mesh, in_specs=in_specs, out_specs=out_specs, check_vma=False)
```

```python
import functools

import jax
import jax.numpy as jnp
import numpy as np
from jax import lax
from jax.experimental import pallas as pl
from jax.experimental.pallas import tpu as pltpu
from jax.sharding import PartitionSpec as P

HEADS = 15
KV_HEADS = 5
HEAD_DIM = 64
FF = 2560
D = 960
Q_WIDTH = 960
QKV_WIDTH = 1600
SHORT_LEN = 16
LONG_LEN = 64
EPS = 1e-05
BASE = 10000.0
NEG = -1e30


class Box(dict):
    __getattr__ = dict.__getitem__
    __setattr__ = dict.__setitem__


BF = jnp.bfloat16
F32 = jnp.float32
MICROS = 2
ROWS = MICROS * LONG_LEN
CHUNK = 256
TILE = 128
TILES = 8
K_HALF = 15
V_HALF = 20
MESH = pl.DeviceIdType.MESH
DOWN = "dnT"
HELD = 9

KEEP = dict(x=D, mid=D, p=1024, qkv=1664, A=FF, B=FF)
LEFT = dict(n1=D, mix=D, n2=D, hid=FF)
RIGHT = dict(gqkv=QKV_WIDTH, gat=D, ggu=2 * FF, gff=D)
WEIGHTS = dict(qkv=(D, QKV_WIDTH), out=(Q_WIDTH, D), gu=(D, 2 * FF), dn=(FF, D))


def nn(a, b):
    return lax.dot_general(a, b, (((1,), (0,)), ((), ())), preferred_element_type=F32)


def nt(a, b):
    return lax.dot_general(a, b, (((1,), (1,)), ((), ())), preferred_element_type=F32)


def tn(a, b):
    return lax.dot_general(a, b, (((0,), (0,)), ((), ())), preferred_element_type=F32)


def chunks(total, width=CHUNK):
    return [(c, min(width, total - c)) for c in range(0, total, width)]


def lane(rows):
    return lax.broadcasted_iota(jnp.int32, (rows, TILE), 1)


def inverse_rms(x):
    return lax.rsqrt(jnp.mean(x * x, -1, keepdims=True) + EPS)


def turn(tile):
    first = (lane(tile.shape[0]) % HEAD_DIM) < HEAD_DIM // 2
    return jnp.where(first, pltpu.roll(tile, TILE - 32, 1), pltpu.roll(tile, 32, 1))


def query_scale(column, rows):
    scale = HEAD_DIM**-0.5
    if column + TILE <= Q_WIDTH:
        return scale
    return jnp.where(lane(rows) < HEAD_DIM, scale, 1.0)


def head_pairs(ref, rows, first):
    low = lane(LONG_LEN) < HEAD_DIM
    tiles = {}
    spread = []
    for head in range(KV_HEADS):
        place = first + head
        t = place // 2
        if t not in tiles:
            width = min(TILE, QKV_WIDTH - t * TILE)
            x = ref[rows, t * TILE : t * TILE + width].astype(F32)
            if width < TILE:
                x = jnp.concatenate([x, x], 1)
            tiles[t] = (x, pltpu.roll(x, HEAD_DIM, 1))
        x, swapped = tiles[t]
        spread.append(jnp.where(low, x, swapped) if place % 2 == 0 else jnp.where(low, swapped, x))
    pairs = []
    for t in range(TILES):
        a = 2 * t // 3
        b = min((2 * t + 1) // 3, KV_HEADS - 1)
        pairs.append((spread[a] if a == b else jnp.where(low, spread[a], spread[b])).astype(BF))
    return pairs


def diagonal(ref, rows, t):
    low = lane(LONG_LEN) < HEAD_DIM
    x = ref[rows, t * TILE : (t + 1) * TILE].astype(F32)
    above = jnp.where(low, x, 0.0).astype(BF)
    below = jnp.where(low, 0.0, x).astype(BF)
    if t == TILES - 1:
        below = jnp.zeros_like(below)
    return jnp.concatenate([above, below], 0)


def micro_rows():
    return [slice(b * LONG_LEN, (b + 1) * LONG_LEN) for b in range(MICROS)]


def attention_forward(S):
    low = lane(LONG_LEN) < HEAD_DIM
    for rows in micro_rows():
        keys = head_pairs(S.qkv, rows, K_HALF)
        for t in range(TILES):
            S.e[rows, t * TILE : (t + 1) * TILE] = nt(keys[t], diagonal(S.qkv, rows, t))
    for rows in micro_rows():
        bias = S.bias[rows, :]
        for t in range(TILES):
            s = S.e[rows, t * TILE : (t + 1) * TILE] + bias
            e = jnp.exp(s - jnp.max(s, 0, keepdims=True))
            z = 1.0 / jnp.sum(e, 0, keepdims=True)
            S.p[rows, t * TILE : (t + 1) * TILE] = (e * z).astype(BF)
    for rows in micro_rows():
        values = head_pairs(S.qkv, rows, V_HALF)
        for t in range(TILES):
            o = tn(S.p[rows, t * TILE : (t + 1) * TILE], values[t])
            m = jnp.where(low, o[:LONG_LEN], o[LONG_LEN:]).astype(BF)
            width = min(TILE, Q_WIDTH - t * TILE)
            S.mix[rows, t * TILE : t * TILE + width] = m[:, :width]


def block_forward(W, S, arrived):
    h = S.h
    x = h[...]
    S.x[:, :D] = x.astype(BF)
    S.n1[...] = (x * inverse_rms(x) * W.ga[...]).astype(BF)
    arrived("qkv")
    n1 = S.n1[...]
    for c, w in chunks(QKV_WIDTH):
        o = nn(n1, W.qkv[:, c : c + w])
        for t, tw in chunks(w, TILE):
            column = c + t
            tile = o[:, t : t + tw]
            if column < Q_WIDTH + KV_HEADS * HEAD_DIM:
                tile = tile * S.cos[...] + turn(tile) * S.sin[...]
                if column < Q_WIDTH:
                    tile = tile * query_scale(column, ROWS)
            S.qkv[:, column : column + tw] = tile.astype(BF)
    attention_forward(S)
    arrived("out")
    mix = S.mix[...]
    for c, w in chunks(D):
        h[:, c : c + w] = h[:, c : c + w] + nn(mix, W.out[:, c : c + w])
    x = h[...]
    S.mid[:, :D] = x.astype(BF)
    S.n2[...] = (x * inverse_rms(x) * W.gf[...]).astype(BF)
    arrived("gu")
    n2 = S.n2[...]
    for c, w in chunks(FF):
        gate = nn(n2, W.gu[:, c : c + w])
        up = nn(n2, W.gu[:, FF + c : FF + c + w])
        sg = 1.0 / (1.0 + jnp.exp(-gate))
        act = gate * sg
        S.B[:, c : c + w] = act.astype(BF)
        S.A[:, c : c + w] = (up * sg * (1.0 + gate * (1.0 - sg))).astype(BF)
        S.hid[:, c : c + w] = (act * up).astype(BF)
    arrived("dn")
    hid = S.hid[...]
    for c, w in chunks(D):
        h[:, c : c + w] = h[:, c : c + w] + nn(hid, W.dn[:, c : c + w])


def attention_backward(S):
    low = lane(LONG_LEN) < HEAD_DIM
    for rows in micro_rows():
        values = head_pairs(S.qkv, rows, V_HALF)
        for t in range(TILES):
            S.e[rows, t * TILE : (t + 1) * TILE] = nt(values[t], diagonal(S.gm, rows, t))
    for rows in micro_rows():
        for t in range(TILES):
            gp = S.e[rows, t * TILE : (t + 1) * TILE]
            p = S.p[rows, t * TILE : (t + 1) * TILE].astype(F32)
            total = jnp.sum(gp * p, 0, keepdims=True)
            S.gs[rows, t * TILE : (t + 1) * TILE] = (p * (gp - total)).astype(BF)

    def store(rows, column, value, turned):
        if turned:
            value = value * S.cos[rows, :] - turn(value) * S.sin[rows, :]
        width = min(TILE, QKV_WIDTH - column)
        S.gqkv[rows, column : column + width] = value[:, :width].astype(BF)

    def fold(parts):
        sums = []
        for head in range(KV_HEADS):
            lower, upper = None, None
            for q in (3 * head, 3 * head + 1, 3 * head + 2):
                part = parts[q // 2]
                if q % 2 == 0:
                    lower = part if lower is None else lower + part
                else:
                    upper = part if upper is None else upper + part
            sums.append((jnp.where(low, lower, 0.0), jnp.where(low, 0.0, upper)))
        return sums

    def placed(sums, head, half):
        lower, upper = sums[head]
        if half == 0:
            return lower + pltpu.roll(upper, HEAD_DIM, 1)
        return upper + pltpu.roll(lower, HEAD_DIM, 1)

    for rows in micro_rows():
        keys = head_pairs(S.qkv, rows, K_HALF)
        grad_k, grad_v = [], []
        last = None
        for t in range(TILES):
            gs = S.gs[rows, t * TILE : (t + 1) * TILE]
            grad_k.append(nn(gs, diagonal(S.qkv, rows, t)))
            grad_v.append(
                nn(S.p[rows, t * TILE : (t + 1) * TILE], diagonal(S.gm, rows, t))
            )
            o = tn(gs, keys[t])
            grad_q = jnp.where(low, o[:LONG_LEN], o[LONG_LEN:]) * HEAD_DIM**-0.5
            if t < TILES - 1:
                store(rows, t * TILE, grad_q, True)
            else:
                last = grad_q
        k, v = fold(grad_k), fold(grad_v)
        store(rows, 896, jnp.where(low, last, placed(k, 0, 1)), True)
        store(rows, 1024, placed(k, 1, 0) + placed(k, 2, 1), True)
        store(rows, 1152, placed(k, 3, 0) + placed(k, 4, 1), True)
        store(rows, 1280, placed(v, 0, 0) + placed(v, 1, 1), False)
        store(rows, 1408, placed(v, 2, 0) + placed(v, 3, 1), False)
        store(rows, 1536, placed(v, 4, 0), False)


def rms_backward(x, gain, e, base):
    r = inverse_rms(x)
    scaled = e * gain
    mean = jnp.mean(x * scaled, -1, keepdims=True)
    return base + r * scaled - x * (r * r * r * mean), jnp.sum(e * x * r, 0, keepdims=True)


def block_backward(W, S, gain_attn_grad, gain_ffn_grad):
    g = S.h
    S.gff[...] = g[...].astype(BF)
    gff = S.gff[...]
    for c, w in chunks(FF):
        gh = nn(gff, W.dnT[:, c : c + w])
        S.ggu[:, c : c + w] = (gh * S.A[:, c : c + w].astype(F32)).astype(BF)
        S.ggu[:, FF + c : FF + c + w] = (gh * S.B[:, c : c + w].astype(F32)).astype(BF)
    ggu = S.ggu[...]
    for c, w in chunks(D):
        S.e[:, c : c + w] = nn(ggu, W.guT[:, c : c + w])
    new, gain = rms_backward(S.mid[:, :D].astype(F32), W.gf[...], S.e[:, :D], g[...])
    gain_ffn_grad[...] += gain
    g[...] = new
    S.gat[...] = new.astype(BF)
    gat = S.gat[...]
    for c, w in chunks(Q_WIDTH):
        S.gm[:, c : c + w] = nn(gat, W.outT[:, c : c + w]).astype(BF)
    attention_backward(S)
    gqkv = S.gqkv[...]
    for c, w in chunks(D):
        S.e[:, c : c + w] = nn(gqkv, W.qkvT[:, c : c + w])
    new, gain = rms_backward(S.x[:, :D].astype(F32), W.ga[...], S.e[:, :D], g[...])
    gain_attn_grad[...] += gain
    g[...] = new


def flip(source, target, first=0, end=None):
    depth, width = source.shape
    size = CHUNK
    whole = width // size

    def strip(start, w):
        for k, kw in chunks(depth):
            target[pl.ds(start, w), k : k + kw] = source[k : k + kw, pl.ds(start, w)].T

    def one(i, carry):
        strip(pl.multiple_of(i * size, size), size)
        return carry

    lax.fori_loop(first, whole if end is None else end, one, 0)
    if width % size:
        strip(whole * size, width % size)


def make_constants(S, meta, item, tables):
    cos_long, sin_long, cos_short, sin_short = tables
    shape = (LONG_LEN, TILE)
    slot = lax.broadcasted_iota(jnp.int32, shape, 0)
    other = lane(LONG_LEN) % LONG_LEN
    piece = (slot // SHORT_LEN).astype(F32)
    other_piece = (other // SHORT_LEN).astype(F32)
    for b, rows in enumerate(micro_rows()):
        is_long = jnp.broadcast_to(meta[item, b : b + 1, :], shape) > 0.5
        count = jnp.broadcast_to(meta[item, MICROS + b : MICROS + b + 1, :], shape)
        S.cos[rows, :] = jnp.where(is_long, cos_long[...], cos_short[...])
        S.sin[rows, :] = jnp.where(is_long, sin_long[...], sin_short[...])
        short = jnp.where(other_piece < count, 0.0, jnp.where(slot == other, 0.0, NEG))
        short = jnp.where(piece == other_piece, short, NEG)
        bias = jnp.where(is_long, 0.0, short)
        S.bias[rows, :] = jnp.where(slot <= other, bias, NEG)
        S.valid[rows, :] = jnp.where(is_long, 1.0, jnp.where(piece < count, 1.0, 0.0))


def named(names, refs):
    boxes = []
    for group in names:
        boxes.append(Box(zip(group, refs)))
        refs = refs[len(group) :]
    return boxes


def pipeline_kernel(sections, chips, own, names, *refs):
    I, O, R = named(names, refs)
    far = own * (chips - 1)
    section = lax.axis_index("section")
    data = lax.axis_index("dp")
    chip, core = data // 2, data % 2
    is_first, is_last = section == 0, section == sections - 1
    W = Box({name: R["w_" + name] for name in WEIGHTS})
    W.update({name + "T": R["t_" + name] for name in WEIGHTS})
    W.ga, W.gf = I.ga, I.gf

    crossed = lax.rem(section, 2) == 1
    sibling = chip * 2 + 1 - core
    holder = jnp.where(crossed, 1 - core, core)
    before, after = dict(section=section - 1, dp=sibling), dict(section=section + 1, dp=sibling)

    def far_chip(d):
        return lax.rem(chip - d + chips, chips) * 2

    def partner(d):
        return far_chip(d) + core

    barrier = pltpu.get_barrier_semaphore()

    @pl.when(section > 0)
    def _():
        pl.semaphore_signal(barrier, 1, device_id=before, device_id_type=MESH)

    @pl.when(section < sections - 1)
    def _():
        pl.semaphore_signal(barrier, 1, device_id=after, device_id_type=MESH)

    for d in range(1, 2 * chips):
        other = lax.rem(data + d, 2 * chips)
        pl.semaphore_signal(barrier, 1, device_id=dict(dp=other), device_id_type=MESH)

    early_names = [name for name in WEIGHTS if name in I]
    weight_names = early_names + [DOWN]
    weight_copies = {
        name: pltpu.make_async_copy(I[name], W[name], R.w_sem.at[k])
        for k, name in enumerate(weight_names)
    }
    slab = W.dn.at[0:D, 0 : own * ROWS]
    token_copy = pltpu.make_async_copy(I.tok, slab, R.t_sem)
    cotangent_copy = pltpu.make_async_copy(I.cot, slab, R.t_sem)

    @pl.when(is_first)
    def _():
        token_copy.start()

    @pl.when(is_last)
    def _():
        cotangent_copy.start()

    for name in early_names[:2]:
        weight_copies[name].start()

    def columns_of(ref, j):
        return ref.at[:, pl.ds(pl.multiple_of(j * ROWS, ROWS), ROWS)]

    O.gga[...] = jnp.zeros_like(O.gga)
    O.ggf[...] = jnp.zeros_like(O.ggf)
    R.gm[...] = jnp.zeros_like(R.gm)

    others = 2 * chips - 1
    near = jnp.where(is_first, 0, 1) + jnp.where(is_last, 0, 1)

    @pl.when(is_first)
    def _():
        token_copy.wait()
        for j in range(own):
            for c, w in chunks(D):
                R.fin[j, :, c : c + w] = slab[c : c + w, j * ROWS : (j + 1) * ROWS].T

    for name in weight_names[2:]:
        weight_copies[name].start()
    pl.semaphore_wait(barrier, near + others)

    for j in range(own):
        for b in range(MICROS):
            for column in range(2):
                count = I.counts[column : column + 1, MICROS * j + b : MICROS * j + b + 1]
                row = column * MICROS + b
                R.mine[j, row : row + 1, :] = jnp.broadcast_to(count.astype(F32), (1, TILE))

    def meta_copy(d):
        return pltpu.make_async_remote_copy(
            src_ref=R.mine,
            dst_ref=R.meta.at[pl.ds(own * d, own)],
            send_sem=R.ms_sem.at[d],
            recv_sem=R.m_sem.at[d],
            device_id=dict(dp=far_chip(d) + holder),
            device_id_type=MESH,
        )

    def next_copy(j):
        return pltpu.make_async_remote_copy(
            src_ref=R.outs.at[j],
            dst_ref=R.fin.at[j],
            send_sem=R.fs_sem.at[j],
            recv_sem=R.f_sem.at[j],
            device_id=after,
            device_id_type=MESH,
        )

    def previous_copy(j):
        return pltpu.make_async_remote_copy(
            src_ref=R.outs.at[j],
            dst_ref=R.bin.at[j],
            send_sem=R.bs_sem.at[j],
            recv_sem=R.b_sem.at[j],
            device_id=before,
            device_id_type=MESH,
        )

    def far_copy(buffer, recv, send, d, j):
        return pltpu.make_async_remote_copy(
            src_ref=buffer.at[j],
            dst_ref=buffer.at[own * d + j],
            send_sem=send.at[own * (d - 1) + j],
            recv_sem=recv.at[own * d + j],
            device_id=dict(dp=partner(d)),
            device_id_type=MESH,
        )

    def far_forward(d, j):
        return far_copy(R.fin, R.f_sem, R.fx_sem, d, j)

    def far_backward(d, j):
        return far_copy(R.bin, R.b_sem, R.bx_sem, d, j)

    class RowCopy:
        def __init__(self, target, j, sent, arrived):
            place = columns_of(target, j)
            self.here = pltpu.make_async_copy(R.flip, place, sent.at[j])
            self.there = pltpu.make_async_remote_copy(
                src_ref=R.flip,
                dst_ref=place,
                send_sem=sent.at[j],
                recv_sem=arrived.at[j],
                device_id=dict(dp=sibling),
                device_id_type=MESH,
            )

        def start(self):
            pl.when(crossed)(self.there.start)
            pl.when(jnp.logical_not(crossed))(self.here.start)

        def wait(self):
            pl.when(crossed)(self.there.wait_send)
            pl.when(jnp.logical_not(crossed))(self.here.wait)

    def out_copy(j):
        return RowCopy(O.out, j, R.o_sem, R.oa_sem)

    def grad_copy(j):
        return RowCopy(O.gin, j, R.g_sem, R.ga_sem)

    for d in range(1, chips):
        meta_copy(d).start()

    @pl.when(crossed)
    def _():
        meta_copy(0).start()

    @pl.when(jnp.logical_not(crossed))
    def _():
        R.meta[0:own] = R.mine[...]

    def cotangent_cross(j):
        return pltpu.make_async_remote_copy(
            src_ref=R.outs.at[j],
            dst_ref=R.bin.at[j],
            send_sem=R.fs_sem.at[j],
            recv_sem=R.b_sem.at[j],
            device_id=dict(dp=sibling),
            device_id_type=MESH,
        )

    @pl.when(is_last)
    def _():
        cotangent_copy.wait()
        target = R.outs if sections % 2 == 0 else R.bin
        for j in range(own):
            for c, w in chunks(D):
                target[j, :, c : c + w] = slab[c : c + w, j * ROWS : (j + 1) * ROWS].T
        if sections % 2 == 0:
            for j in range(own):
                cotangent_cross(j).start()
            for j in range(own):
                cotangent_cross(j).wait()

    @pl.when(crossed)
    def _():
        meta_copy(0).wait()

    held = is_first & (core == 1)
    early = section >= sections // 2

    def views(slot):
        S = Box(R)
        for name in (*KEEP, *LEFT, *RIGHT):
            S[name] = R[name].at[slot]
        return S

    def left_copies(slot, index):
        return [
            pltpu.make_async_copy(R[name].at[slot], O[name].at[index], R.l_sem.at[slot, k])
            for k, name in enumerate((*KEEP, *LEFT))
        ]

    def right_copies(slot, index):
        return [
            pltpu.make_async_copy(R[name].at[slot], O[name].at[index], R.r_sem.at[slot, k])
            for k, name in enumerate(RIGHT)
        ]

    def keep_loads(slot, index):
        return [
            pltpu.make_async_copy(O[name].at[index], R[name].at[slot], R.k_sem.at[slot, k])
            for k, name in enumerate(KEEP)
        ]

    def turn_out():
        value = R.h[...]

        for c, w in chunks(D):
            R.flip[c : c + w, :] = value[:, c : c + w].astype(BF).T

    def forward_phase(start, count, is_far):
        def step(k, carry):
            item = start + k
            make_constants(R, R.meta, item, (I.cosl, I.sinl, I.coss, I.sins))

            @pl.when(is_far)
            def _():
                d = item // own
                far_forward(d, item - own * d).wait_recv()

            @pl.when(jnp.logical_not(is_far))
            def _():
                @pl.when(jnp.logical_not(is_first))
                def _():
                    next_copy(item).wait_recv()

                for d in range(1, chips):
                    far_forward(d, item).start()

            @pl.when(k > 0)
            def _():
                for copy in left_copies(1, 2 * item - 1):
                    copy.start()

            R.h[...] = R.fin[item].astype(F32)

            def one(f, carry):
                @pl.when(k > 0)
                def _():
                    for copy in left_copies(f, 2 * (item - 1) + f):
                        copy.wait()

                fresh = is_first & (item == 0)

                def arrived(name):
                    if name in early_names[:-1]:
                        weight_copies[name].wait()
                    elif name in early_names:
                        pl.when(jnp.logical_not(held))(weight_copies[name].wait)
                    else:
                        weight_copies[DOWN].wait()
                        flip(W.dnT, W.dn)

                def forward():
                    block_forward(W, views(f), lambda name: None)

                if f == 0:

                    @pl.when(fresh)
                    def _():
                        block_forward(W, views(f), arrived)

                    pl.when(jnp.logical_not(fresh))(forward)
                else:
                    forward()

                @pl.when(f == 0)
                def _():
                    for copy in left_copies(0, 2 * item):
                        copy.start()

                return carry

            for f in range(2):
                one(f, 0)

            @pl.when(jnp.logical_not(is_far))
            def _():
                R.h[...] = R.h[...] * R.valid[:, 0:1]
                R.outs[item] = R.h[...].astype(BF)

                @pl.when(jnp.logical_not(is_last))
                def _():
                    next_copy(item).start()

                @pl.when(item > 0)
                def _():
                    out_copy(item - 1).wait()

                turn_out()
                out_copy(item).start()

            return carry

        lax.fori_loop(0, count, step, 0)
        for copy in left_copies(1, 2 * (start + count) - 1):
            copy.start()
        for f in range(2):
            for copy in left_copies(f, 2 * (start + count - 1) + f):
                copy.wait()

    def backward_phase(start, count, is_far):
        for copy in keep_loads(1, 2 * start + 1):
            copy.start()

        def step(k, carry):
            item = start + k
            make_constants(R, R.meta, item, (I.cosl, I.sinl, I.coss, I.sins))

            @pl.when(is_far)
            def _():
                d = item // own
                far_backward(d, item - own * d).wait_recv()

            @pl.when(jnp.logical_not(is_far))
            def _():
                @pl.when(jnp.logical_not(is_last))
                def _():
                    previous_copy(item).wait_recv()

                for d in range(1, chips):
                    far_backward(d, item).start()

            @pl.when(k > 0)
            def _():
                for copy in right_copies(0, 2 * item - 2):
                    copy.start()

            R.h[...] = R.bin[item].astype(F32) * R.valid[:, 0:1]

            def one(i, carry):
                f = 1 - i
                for copy in keep_loads(f, 2 * item + f):
                    copy.wait()

                @pl.when(f == 1)
                def _():
                    for copy in keep_loads(0, 2 * item):
                        copy.start()

                @pl.when((f == 0) & (k < count - 1))
                def _():
                    for copy in keep_loads(1, 2 * item + 3):
                        copy.start()

                @pl.when(k > 0)
                def _():
                    for copy in right_copies(f, 2 * (item - 1) + f):
                        copy.wait()

                block_backward(W, views(f), O.gga, O.ggf)

                @pl.when(f == 1)
                def _():
                    for copy in right_copies(1, 2 * item + 1):
                        copy.start()

                return carry

            for i in range(2):
                one(i, 0)

            @pl.when(jnp.logical_not(is_far))
            def _():
                @pl.when(jnp.logical_not(is_last))
                def _():
                    next_copy(item).wait_send()

                R.outs[item] = R.h[...].astype(BF)

                @pl.when(jnp.logical_not(is_first))
                def _():
                    previous_copy(item).start()

                @pl.when(item > 0)
                def _():
                    grad_copy(item - 1).wait()

                @pl.when(item == 0)
                def _():
                    out_copy(own - 1).wait()

                turn_out()
                grad_copy(item).start()

            return carry

        lax.fori_loop(0, count, step, 0)
        for copy in right_copies(0, 2 * (start + count - 1)):
            copy.start()
        for f in range(2):
            for copy in right_copies(f, 2 * (start + count - 1) + f):
                copy.wait()

    phases = 4 if far else 2

    def phase(p, carry):
        if far:
            is_far = jnp.where(is_last, p >= 2, lax.rem(p, 2) == 1)
            is_back = jnp.where(is_last, lax.rem(p, 2) == 1, p >= 2)
            start = jnp.where(is_far, own, 0)
            count = jnp.where(is_far, far, own)
        else:
            is_far, is_back, start, count = p < 0, p == 1, 0, own

        @pl.when((p == 0) & jnp.logical_not(is_first))
        def _():
            weight_copies[DOWN].wait()
            flip(W.dnT, W.dn)
            for name in early_names:
                weight_copies[name].wait()

        largest = early_names[-1]

        @pl.when((p == 0) & held)
        def _():
            weight_copies[largest].wait()
            flip(W[largest], W[largest + "T"], 0, HELD)

        @pl.when(jnp.where(early, p == 0, p == phases // 2))
        def _():
            for name in early_names[:-1]:
                flip(W[name], W[name + "T"])

            flip(W[largest], W[largest + "T"], jnp.where(held, HELD, 0))

        if far:

            @pl.when(is_far & jnp.logical_not(is_back))
            def _():
                for d in range(1, chips):
                    meta_copy(d).wait_recv()

        @pl.when(jnp.logical_not(is_back))
        def _():
            forward_phase(start, count, is_far)

        @pl.when(is_back)
        def _():
            backward_phase(start, count, is_far)

        return carry

    lax.fori_loop(0, phases, phase, 0)

    for j in range(own):

        @pl.when(jnp.logical_not(is_first))
        def _():
            previous_copy(j).wait_send()

        for d in range(1, chips):
            far_forward(d, j).wait_send()
            far_backward(d, j).wait_send()
    grad_copy(own - 1).wait()
    for d in range(1, chips):
        meta_copy(d).wait_send()

    @pl.when(crossed)
    def _():
        for j in range(own):
            out_copy(j).there.wait_recv()
            grad_copy(j).there.wait_recv()


def rotary_tables():
    half = HEAD_DIM // 2
    frequency = BASE ** (-2.0 * np.arange(half, dtype=np.float32) / HEAD_DIM)
    slots = np.arange(LONG_LEN)
    tables = []
    for position in (slots, slots % SHORT_LEN):
        angle = position.astype(np.float32)[:, None] * frequency[None, :].astype(np.float32)
        cos, sin = np.cos(angle), np.sin(angle)
        tables.append(np.tile(np.concatenate([cos, cos], 1), (1, 2)).astype(np.float32))
        tables.append(np.tile(np.concatenate([-sin, sin], 1), (1, 2)).astype(np.float32))
    return tables


def vmem(*shape, dtype=BF):
    return pltpu.VMEM(shape, dtype)


HBM = pl.BlockSpec(memory_space=pl.ANY)
LOCAL = pl.BlockSpec(memory_space=pltpu.VMEM)
VMEM_LIMIT = 127 * 2**19


def run_pipeline(sections, chips, own, hbm_inputs, inputs):
    items = own * chips
    scratch = Box(
        fin=vmem(items, ROWS, D),
        bin=vmem(items, ROWS, D),
        outs=vmem(own, ROWS, D),
        flip=vmem(D, ROWS),
        meta=vmem(items, 8, TILE, dtype=F32),
        mine=vmem(own, 8, TILE, dtype=F32),
        h=vmem(ROWS, D, dtype=F32),
        e=vmem(ROWS, 1024, dtype=F32),
        gm=vmem(ROWS, 1024),
        gs=vmem(ROWS, 1024),
        cos=vmem(ROWS, TILE, dtype=F32),
        sin=vmem(ROWS, TILE, dtype=F32),
        bias=vmem(ROWS, TILE, dtype=F32),
        valid=vmem(ROWS, TILE, dtype=F32),
    )
    for name, width in {**KEEP, **LEFT, **RIGHT}.items():
        scratch[name] = vmem(2, ROWS, width)
    for name, (depth, width) in WEIGHTS.items():
        scratch["w_" + name] = vmem(depth, width)
        scratch["t_" + name] = vmem(width, depth)
    far = max(1, own * (chips - 1))
    counts = dict(
        w_sem=(len(WEIGHTS),),
        f_sem=(items,),
        b_sem=(items,),
        fs_sem=(own,),
        bs_sem=(own,),
        fx_sem=(far,),
        bx_sem=(far,),
        m_sem=(chips,),
        ms_sem=(chips,),
        o_sem=(own,),
        g_sem=(own,),
        oa_sem=(own,),
        ga_sem=(own,),
        l_sem=(2, len(KEEP) + len(LEFT)),
        r_sem=(2, len(RIGHT)),
        k_sem=(2, len(KEEP)),
    )
    for name, shape in counts.items():
        scratch[name] = pltpu.SemaphoreType.DMA(shape)
    scratch.t_sem = pltpu.SemaphoreType.DMA
    shapes = Box(out=(D, own * ROWS), gin=(D, own * ROWS))
    for name, width in {**KEEP, **LEFT, **RIGHT}.items():
        shapes[name] = (2 * items, ROWS, width)
    out_shape = Box({name: jax.ShapeDtypeStruct(shape, BF) for name, shape in shapes.items()})
    out_shape.gga = out_shape.ggf = jax.ShapeDtypeStruct((1, D), F32)
    names = [[*hbm_inputs, *inputs], list(out_shape), list(scratch)]
    results = pl.pallas_call(
        functools.partial(pipeline_kernel, sections, chips, own, names),
        out_shape=list(out_shape.values()),
        in_specs=[HBM] * len(hbm_inputs) + [LOCAL] * len(inputs),
        out_specs=[HBM] * len(shapes) + [LOCAL] * 2,
        scratch_shapes=list(scratch.values()),
        compiler_params=pltpu.CompilerParams(
            collective_id=0, has_side_effects=True, vmem_limit_bytes=VMEM_LIMIT
        ),
    )(*hbm_inputs.values(), *inputs.values())
    return Box(zip(out_shape, results))


PRODUCTS = dict(out=(*"gat mix".split(), Q_WIDTH), qkv=(*"n1 gqkv".split(), QKV_WIDTH))
PRODUCTS.update(dn=(*"gff hid".split(), FF), gu=(*"n2 ggu".split(), 2 * FF))
SPAN = 10


def spans_of(base, width):
    return [(base + i, n) for i, n in chunks(len(chunks(width)), SPAN)]


def gradient_kernel(depth, share, names, *refs):
    I, O, R = named(names, refs)
    data = lax.axis_index("dp")
    chip, core = data // 2, data % 2
    sibling = dict(dp=chip * 2 + 1 - core)
    barrier = pltpu.get_barrier_semaphore()
    pl.semaphore_signal(barrier, 1, device_id=sibling, device_id_type=MESH)
    order = [n for pair in PRODUCTS.values() for n in pair[:2]]
    loads = {
        name: pltpu.make_async_copy(I[name], R[name], R.load.at[k]) for k, name in enumerate(order)
    }
    for name in order[:2]:
        loads[name].start()
    later = order[4:]
    R.gain[0:1] = I.gga[...]
    R.gain[1:2] = I.ggf[...]
    pl.semaphore_wait(barrier, 1)
    for name in order[2:4]:
        loads[name].start()

    def to_sibling(source, target, send, recv):
        return pltpu.make_async_remote_copy(
            src_ref=source,
            dst_ref=target,
            send_sem=send,
            recv_sem=recv,
            device_id=sibling,
            device_id_type=MESH,
        )

    gain_copy = to_sibling(R.gain, R.got_gain, R.gs, R.gr)
    gain_copy.start()

    def span_copy(first, n):
        blocks = pl.ds(first, n)
        return to_sibling(R.sent.at[blocks], R.got.at[blocks], R.ss.at[first], R.rs.at[first])

    mine = pl.ds(pl.multiple_of((2 * chip + core) * share, 16), share)
    other = pl.ds(pl.multiple_of((2 * chip + 1 - core) * share, 16), share)
    def turn_left(left):
        for r, rw in chunks(depth):
            for c, w in chunks(D):
                R["t_" + left][c : c + w, r : r + rw] = R[left][r : r + rw, c : c + w].T

    bases, writes = {}, []
    products = list(PRODUCTS.items())
    lefts = [left for left, _, _ in PRODUCTS.values()]

    def span_columns(name, first, n, width):
        c = (first - bases[name]) * CHUNK
        return slice(c, min(c + n * CHUNK, width))

    def give(name, left, right, width):
        for first, n in spans_of(bases[name], width):
            columns = span_columns(name, first, n, width)
            for i, (c, w) in enumerate(chunks(columns.stop - columns.start)):
                c += columns.start
                value = nn(R["t_" + left][other, :], R[right][:, c : c + w])
                R.sent[first + i, :, 0:w] = value.astype(BF)
            span_copy(first, n).start()

    def take(name, left, right, width):
        for first, n in spans_of(bases[name], width):
            span_copy(first, n).wait_recv()
            columns = span_columns(name, first, n, width)
            for i, (c, w) in enumerate(chunks(columns.stop - columns.start)):
                c += columns.start
                total = nn(R["t_" + left][mine, :], R[right][:, c : c + w])
                total = total + R.got[first + i, :, 0:w].astype(F32)
                R["sum_" + name][:, c : c + w] = total.astype(BF)
            place = R["sum_" + name].at[:, columns], O[name].at[:, columns]
            writes.append(pltpu.make_async_copy(*place, R.write.at[len(writes)]))
            writes[-1].start()

    base = 0
    for k, (name, (left, right, width)) in enumerate(products):
        bases[name] = base
        base += len(chunks(width))
        loads[left].wait()
        turn_left(left)
        loads[right].wait()
        for more in later[:2]:
            loads[more].start()
        later = later[2:]
        give(name, left, right, width)
        if k > 0:
            before, spec = products[k - 1]
            take(before, *spec)
    take(products[-1][0], *products[-1][1])
    gain_copy.wait()
    O.gain[...] = R.gain[...] + R.got_gain[...]
    for name, (_, _, width) in PRODUCTS.items():
        for first, n in spans_of(bases[name], width):
            span_copy(first, n).wait_send()
    for write in writes:
        write.wait()


def run_gradients(share, operands, gga, ggf):
    depth = operands.n1.shape[0]
    order = [n for pair in PRODUCTS.values() for n in pair[:2]]
    blocks = sum(len(chunks(width)) for _, _, width in PRODUCTS.values())
    scratch = Box({n: vmem(*operands[n].shape) for n in order})
    for name, (left, _, width) in PRODUCTS.items():
        scratch["t_" + left] = vmem(D, depth)
        scratch["sum_" + name] = vmem(share, width)
    scratch.update(
        sent=vmem(blocks, share, CHUNK),
        got=vmem(blocks, share, CHUNK),
        gain=vmem(2, D, dtype=F32),
        got_gain=vmem(2, D, dtype=F32),
        load=pltpu.SemaphoreType.DMA((len(order),)),
        write=pltpu.SemaphoreType.DMA((blocks,)),
        ss=pltpu.SemaphoreType.DMA((blocks,)),
        rs=pltpu.SemaphoreType.DMA((blocks,)),
        gs=pltpu.SemaphoreType.DMA,
        gr=pltpu.SemaphoreType.DMA,
    )
    inputs = Box({n: operands[n] for n in order})
    inputs.update(gga=gga, ggf=ggf)
    shapes = {n: jax.ShapeDtypeStruct((share, w), BF) for n, (_, _, w) in PRODUCTS.items()}
    shapes.update(gain=jax.ShapeDtypeStruct((2, D), F32))
    names = [list(inputs), list(shapes), list(scratch)]
    results = pl.pallas_call(
        functools.partial(gradient_kernel, depth, share, names),
        out_shape=list(shapes.values()),
        in_specs=[HBM] * len(order) + [LOCAL] * 2,
        out_specs=[HBM] * len(PRODUCTS) + [LOCAL],
        scratch_shapes=list(scratch.values()),
        compiler_params=pltpu.CompilerParams(
            collective_id=1, has_side_effects=True, vmem_limit_bytes=VMEM_LIMIT
        ),
    )(*inputs.values())
    return Box(zip(shapes, results))


def finish_kernel(groups, share, names, *refs):
    I, O, R = named(names, refs)
    data = lax.axis_index("dp")
    passing = [name for name in I if name not in PRODUCTS and name in O]
    passed_in = [
        pltpu.make_async_copy(I[name], R["i_" + name], R.pass_sem.at[2 * k])
        for k, name in enumerate(passing)
    ]
    passed_out = [
        pltpu.make_async_copy(R["i_" + name], O[name], R.pass_sem.at[2 * k + 1])
        for k, name in enumerate(passing)
    ]
    loads, stores = [], []
    for name, (_, _, width) in PRODUCTS.items():
        for c, w in chunks(width, FF):
            k = len(loads)
            source, target = I[name].at[:, c : c + w], O[name].at[:, c : c + w]
            place = R["o_" + name].at[:, c : c + w]
            if name == TURNED:
                target, place = O[name], R["o_" + name]
            loads.append(
                (name, c, w, pltpu.make_async_copy(source, R["i_" + name].at[:, c : c + w], R.load.at[k]))
            )
            stores.append(pltpu.make_async_copy(place, target, R.store.at[k]))
    for load in loads:
        load[3].start()
    for copy in passed_in:
        copy.start()
    for (name, c, w, load), store in zip(loads, stores):
        load.wait()
        for b, bw in chunks(w, 2 * CHUNK):
            columns = slice(c + b, c + b + bw)
            value = R["i_" + name][:, columns].astype(F32)
            if name == TURNED:
                R["o_" + name][columns, :] = value.T
            else:
                R["o_" + name][:, columns] = value
        store.start()
    for row, gain in enumerate((O.ga, O.gf)):
        value = I.gain[row : row + 1, 0:share]
        for q in range(1, groups):
            value = jnp.where(data == q, I.gain[row : row + 1, q * share : (q + 1) * share], value)
        gain[...] = value
    for arrival, copy in zip(passed_in, passed_out):
        arrival.wait()
        copy.start()
    for copy in stores + passed_out:
        copy.wait()


TURNED = "out"


def run_finish(groups, share, sums, rows):
    inputs = Box({n: sums[n] for n in PRODUCTS})
    inputs.update(rows, gain=sums.gain)
    shapes = Box()
    scratch = Box()
    for name, (_, _, width) in PRODUCTS.items():
        shape = (width, share) if name == TURNED else (share, width)
        shapes[name] = jax.ShapeDtypeStruct(shape, F32)
        scratch["i_" + name] = vmem(share, width)
        scratch["o_" + name] = vmem(*shape, dtype=F32)
    for name, value in rows.items():
        shapes[name] = jax.ShapeDtypeStruct(value.shape, BF)
        scratch["i_" + name] = vmem(*value.shape)
    shapes.ga = shapes.gf = jax.ShapeDtypeStruct((1, share), F32)
    copies = sum(len(chunks(width, FF)) for _, _, width in PRODUCTS.values())
    scratch.update(
        load=pltpu.SemaphoreType.DMA((copies,)),
        store=pltpu.SemaphoreType.DMA((copies,)),
        pass_sem=pltpu.SemaphoreType.DMA((2 * len(rows),)),
    )
    names = [list(inputs), list(shapes), list(scratch)]
    results = pl.pallas_call(
        functools.partial(finish_kernel, groups, share, names),
        out_shape=list(shapes.values()),
        in_specs=[HBM] * (len(inputs) - 1) + [LOCAL],
        out_specs=[HBM] * (len(shapes) - 2) + [LOCAL] * 2,
        scratch_shapes=list(scratch.values()),
        compiler_params=pltpu.CompilerParams(vmem_limit_bytes=VMEM_LIMIT),
    )(*inputs.values())
    return Box(zip(shapes, results))


def gradients_by_xla(groups, share, operands, rows, gga, ggf):
    data = lax.axis_index("dp")
    begin = (data // 2) * 2 * share
    swap = [(i, i ^ 1) for i in range(groups)]

    def exchange(both, axis=0):
        mine = lax.dynamic_slice_in_dim(both, (data % 2) * share, share, axis)
        other = lax.dynamic_slice_in_dim(both, (1 - data % 2) * share, share, axis)
        return mine + lax.ppermute(other.astype(BF), "dp", swap).astype(F32)

    sums = Box(rows)
    for name, (left, right, _) in PRODUCTS.items():
        part = lax.dynamic_slice_in_dim(operands[left], begin, 2 * share, 1)
        sums[name] = exchange(tn(part, operands[right]))
    sums[TURNED] = sums[TURNED].T
    sums.ga = exchange(lax.dynamic_slice_in_dim(gga, begin, 2 * share, 1), 1)
    sums.gf = exchange(lax.dynamic_slice_in_dim(ggf, begin, 2 * share, 1), 1)
    return sums


def body(tokens, cotangent, seq_counts, attn_gain, w_qkv, w_out, ffn_gain, w_gate_up, w_down):
    sections = lax.axis_size("section")
    groups = lax.axis_size("dp")
    chips = groups // 2
    own = tokens.shape[0] // ROWS
    cosl, sinl, coss, sins = rotary_tables()
    hbm_inputs = Box(tok=tokens.T, cot=cotangent.T, dnT=w_down[0].T)
    hbm_inputs.update(qkv=w_qkv[0], out=w_out[0], gu=w_gate_up[0])
    inputs = Box(counts=seq_counts.T, ga=attn_gain, gf=ffn_gain)
    inputs.update(cosl=cosl, sinl=sinl, coss=coss, sins=sins)
    O = run_pipeline(sections, chips, own, hbm_inputs, inputs)
    share = D // groups
    operands = Box({n: O[n].reshape(-1, O[n].shape[-1]) for n in (*LEFT, *RIGHT)})
    rows = Box(rows_out=O.out, rows_gin=O.gin)
    if share % 16:
        sums = gradients_by_xla(groups, share, operands, rows, O.gga, O.ggf)
    else:
        sums = run_finish(groups, share, run_gradients(share, operands, O.gga, O.ggf), rows)
    return (
        sums.rows_out.T[None],
        sums.rows_gin.T[None],
        sums.ga,
        sums.qkv[None],
        sums.out[None],
        sums.gf,
        sums.gu[None],
        sums.dn.T[None],
    )


def solution(mesh):
    in_specs = (
        P("dp", None),
        P("dp", None),
        P("dp", None),
        P("section", None),
        P("section", None, None),
        P("section", None, None),
        P("section", None),
        P("section", None, None),
        P("section", None, None),
    )
    out_specs = (
        P("section", "dp", None),
        P("section", "dp", None),
        P("section", "dp"),
        P("section", "dp", None),
        P("section", None, "dp"),
        P("section", "dp"),
        P("section", "dp", None),
        P("section", None, "dp"),
    )
    return jax.shard_map(body, mesh=mesh, in_specs=in_specs, out_specs=out_specs, check_vma=False)
```
